32 devices in a mesh: parts: 2 (over y), term: 4 (over z), env: 2 (over x), blk: 2 (over core).
Axes of the slice: x: 2, y: 2, z: 4, core: 2. Of those that a mesh axis runs over, the one named last changes fastest.
Arguments:
- psi: bfloat16 [16, 256, 256], P(('parts', 'blk')), parts along dimension 0, may hold values from -6 to 6
- left_env: bfloat16 [64, 8, 256, 256], P(('parts', 'term'), 'blk', 'env'), parts along dimension 0, may hold values from -0.0625 to 0.0625
- right_env: bfloat16 [64, 8, 256, 256], P(('parts', 'term'), 'blk', 'env'), parts along dimension 0, may hold values from -0.375 to 0.375
- pairing: int32 [64, 8], P(('parts', 'term'), 'blk'), parts along dimension 0, may hold values from 0 to 7
- sector_dims: int32 [16], P('parts'), parts along dimension 0, may hold values from 1 to 256, 1536 in all
- precond: float32 [16, 256, 256], P(('parts', 'blk')), parts along dimension 0, may hold values from 0.3 to 3
Outputs:
- sigmas: float32 [3, 16, 256, 256], P(None, ('parts', 'blk'), 'term'), parts along dimension 1
- subspace: float32 [6, 3], P('parts'), parts along dimension 0
The draws below stay inside these ranges and needn't reach their ends.
There are 2 independent parts, one for each index of `parts`. The reference program is written for one: setup_inputs(seed, part) draws one part's arguments, and reference() takes and returns one part's arrays. A program takes and returns all parts, laid end to end along the dimension named above; each array names one. Nothing has to cross between parts.
All inputs are finite; a program needn't handle non-finite values.
Results may differ from the reference program's by a relative error of at most 0.0057.
Values may be sent and summed in bfloat16 or wider, within the bound.
No kernel may reach another device: no remote copies, remote signals or barrier semaphores. Data moves between devices by JAX's collectives and lax.ppermute only.
A program may use at most 64 MiB of HBM per device.

```python
import math
import jax
import jax.numpy as jnp
import numpy as np
from jax import lax

BD = 256
NSEC = 8
ITERS = 3
TERMS = 32


def touch_ends(drawn, rng, least, top_value):
    shape = drawn.shape
    index_at = [jax.random.randint(jax.random.fold_in(rng, axis), (), 0, shape[axis]) for axis in range(len(shape))]
    drawn = drawn.at[tuple(index_at)].set(least)
    longest = shape.index(max(shape))
    index_at[longest] = (index_at[longest] + 1) % shape[longest]
    return drawn.at[tuple(index_at)].set(top_value)


def levels(rng, dims, cuts, low, high):
    gain = 1.0
    for dim, blocks in cuts:
        draws = jax.random.uniform(jax.random.fold_in(jax.random.fold_in(rng, 6), dim), (blocks,), jnp.float32, low / len(cuts), high / len(cuts))
        gain = gain * jnp.repeat(jnp.exp(draws), dims[dim] // blocks).reshape((-1,) + (1,) * (len(dims) - 1 - dim))
    return gain


def profile(number_of, total, limit, slope):
    portions = [(1 << 20) // math.isqrt(rank ** slope) + 1 for rank in range(2, number_of + 1)]
    surplus, given = total - limit - (number_of - 1), [1] * (number_of - 1)
    while surplus > 0:
        free = [i for i in range(number_of - 1) if given[i] < limit]
        mass, remaining = sum([portions[i] for i in free]), surplus
        for i in free:
            addition = min(limit - given[i], max(1, remaining * portions[i] // mass), surplus)
            given[i] = given[i] + addition
            surplus = surplus - addition
    return np.array([limit] + given)


def uneven_parts(key, number_of, total, most, slope):
    if number_of == 2:
        one = jax.random.randint(key, (), max(1, total - most), min(most, total - 1) + 1)
        return jnp.stack([one, total - one])
    lengths = jnp.asarray(profile(number_of, total, most, slope), jnp.int32)
    pairs = (number_of - 1) // 2
    giver, sink = lengths[1:1 + 2 * pairs:2], lengths[2:2 + 2 * pairs:2]
    room = jnp.minimum(giver - 1, most - sink)
    moved = jax.random.randint(jax.random.fold_in(key, 1), (pairs,), 0, 1 << 20) % (room + 1)
    lengths = lengths.at[1:1 + 2 * pairs:2].set(giver - moved).at[2:2 + 2 * pairs:2].set(sink + moved)
    return lengths[jax.random.permutation(jax.random.fold_in(key, 2), number_of)]


def noise(stream_key, dims, width, bound, shards=(), kind=jnp.bfloat16):
    factor_of = levels(stream_key, dims, shards, -0.22, 0.18) if shards else 1.0
    result = jax.random.normal(stream_key, dims, jnp.float32) * width * factor_of
    return jnp.minimum(jnp.maximum(result, -bound), bound).astype(kind)


def setup_inputs(seed: int = 0, part: int = 0) -> dict:
    seeds = jax.random.split(jax.random.key(seed), 7)
    part_splits = jax.random.split(jax.random.fold_in(seeds[6], part), 7)
    psi = noise(part_splits[0], (NSEC, BD, BD), 1.0, 6.0, ((0, 2),))
    left_env = noise(part_splits[1], (TERMS, NSEC, BD, BD), (BD * TERMS) ** -0.5, 0.0625, ((0, 4), (1, 2), (2, 2)))
    right_env = noise(part_splits[2], (TERMS, NSEC, BD, BD), BD ** -0.5, 0.375, ((0, 4), (1, 2), (2, 2)))
    pairing = touch_ends(jax.random.randint(part_splits[3], (TERMS, NSEC), 0, NSEC), jax.random.fold_in(part_splits[3], 1), 0, NSEC - 1).astype(jnp.int32)
    sector_dims = uneven_parts(part_splits[4], NSEC, 3 * NSEC * BD // 4, BD, 0).astype(jnp.int32)
    precond = jnp.clip(jnp.exp(math.log(3.0) - 2.3025851 * jax.random.uniform(part_splits[5], (NSEC, BD, BD), jnp.float32) ** levels(part_splits[5], (NSEC, BD, BD), ((0, 2),), -0.2, 0.2)), 0.3, 3.0)
    return dict(psi=psi, left_env=left_env, right_env=right_env, pairing=pairing, sector_dims=sector_dims, precond=precond)


eps = 1e-06

def apply_terms(vb, left_env, right_env, pairing):
    hi = lax.Precision.HIGHEST

    def one(total, pieces):
        left, right, pair = pieces
        chosen = vb[pair].astype(jnp.float32)
        inner = jnp.einsum('kcj,kbj->kcb', chosen, right.astype(jnp.float32), precision=hi).astype(jnp.bfloat16)
        term = jnp.einsum('kca,kcb->kab', left.astype(jnp.float32), inner.astype(jnp.float32), precision=hi)
        return (total + term, None)
    start = jnp.zeros(vb.shape, jnp.float32)
    total, unused = lax.scan(one, start, (left_env, right_env, pairing))
    return total

def reference(psi, left_env, right_env, pairing, sector_dims, precond):
    count = NSEC * BD * BD
    row_ids = jnp.arange(BD, dtype=jnp.int32)
    live = sector_dims.astype(jnp.int32)
    mask = ((row_ids[None, :, None] < live[:, None, None]) & (row_ids[None, None, :] < live[:, None, None])).astype(jnp.float32)
    start = psi.astype(jnp.float32) * mask
    vec = start * lax.rsqrt(jnp.sum(start * start) / count + eps)
    basis = [vec]
    sigma_list = []
    for step in range(ITERS):
        vb = vec.astype(jnp.bfloat16)
        sigma = apply_terms(vb, left_env, right_env, pairing) * mask
        sigma_list.append(sigma)
        if step + 1 < ITERS:
            resid = sigma
            for other in basis:
                resid = resid - jnp.sum(other * sigma) / count * other
            trial = resid * precond
            shifted = trial
            for other in basis:
                shifted = shifted - jnp.sum(other * trial) / count * other
            vec = shifted * lax.rsqrt(jnp.sum(shifted * shifted) / count + eps)
            basis.append(vec)
    rows = []
    for step in range(ITERS):
        rows.append(jnp.stack([jnp.sum(basis[j] * sigma_list[step]) / count for j in range(ITERS)]))
    return (jnp.stack(sigma_list), jnp.stack(rows))
```

```python
import functools

import jax
import jax.numpy as jnp
from jax import lax
from jax.experimental import pallas as pl
from jax.experimental.pallas import tpu as pltpu
from jax.sharding import PartitionSpec as P

ITERS = 3
EPS = 1e-06
F32, BF16 = jnp.float32, jnp.bfloat16
ROWS = 32
VMEM_LIMIT = 40 * 1024 * 1024


def _specs(*shapes):
    return [pl.BlockSpec(memory_space=s) for s in shapes]


ANY, VM, SM = pl.ANY, pltpu.VMEM, pltpu.SMEM


def _fold(x):
    return jnp.sum(x.reshape(x.shape[0] // 8, 8, x.shape[1]), axis=0)


def _over(n_sec, states, width, n_acc, body):
    blocks = states // ROWS

    def step(i, accs):
        sec, rows = i // blocks, pl.ds(pl.multiple_of((i % blocks) * ROWS, ROWS), ROWS)
        return tuple(a + b for a, b in zip(accs, body(sec, rows)))

    zero = tuple(jnp.zeros((8, width), F32) for _ in range(n_acc))
    return tuple(jnp.sum(a) for a in lax.fori_loop(0, n_sec * blocks, step, zero, unroll=2))


def _write_vb(vb, sec, rows, value, env_pos, swap):
    half = value.shape[1] // 2
    low = value.astype(BF16)
    if swap:
        turned = jnp.concatenate([value[:, half:], value[:, :half]], axis=1).astype(BF16)
        low = jnp.where(env_pos == 0, low, turned)
    vb[sec, rows, :] = low


def _put_scalars(ref, values):
    shape = ref.shape
    row = lax.broadcasted_iota(jnp.int32, shape, 0)
    out = jnp.zeros(shape, F32)
    for index, value in enumerate(values):
        out = jnp.where(row == index, value, out)
    ref[...] = out


def _emit(cfg, meta, acc, outs):
    if cfg["direct"]:
        n, part = cfg["n_term"], cfg["part"]
        z = meta[1]
        for s in range(n):
            rows = pl.ds(pl.multiple_of((z ^ s) * part, part), part)
            for k in range(cfg["sec"]):
                outs[s][k] = acc[k, rows, :].astype(outs[s].dtype)
    else:
        outs[0][...] = acc[...]


def _first_kernel(cfg, meta, psi, psi_o, pre, pre_o, right, v0, pret, inner, vb, work):
    sec, states, width = psi.shape
    n_sec = sec * cfg["n_blk"]
    blk, env_pos = meta[2], meta[0]
    base = blk * sec
    for part, (p_ref, c_ref) in enumerate(((psi, pre), (psi_o, pre_o))):
        for k in range(p_ref.shape[0]):
            at = lax.rem(base + part * sec + k, n_sec)
            live = meta[cfg["dims_at"] + at]
            row = lax.broadcasted_iota(jnp.int32, (states, width), 0)
            col = lax.broadcasted_iota(jnp.int32, (states, width), 1)
            value = jnp.where((row < live) & (col < live), p_ref[k].astype(F32).T, 0.0)
            work[at] = value
            pret[at] = c_ref[k].T
    (total,) = _over(n_sec, states, width, 1, lambda s, r: (_fold(work[s, r, :] * work[s, r, :]),))
    scale = lax.rsqrt(total / (n_sec * states * width) + EPS)

    def make(s, r):
        value = work[s, r, :] * scale
        v0[s, r, :] = value
        _write_vb(vb, s, r, value, env_pos, cfg["swap"])
        return ()

    _over(n_sec, states, width, 0, make)
    terms = right.shape[0]

    def one(i, carry):
        k, t = i % sec, i // sec
        chosen = vb[meta[cfg["pair_at"] + t * sec + k]]
        inner[t, k] = jnp.dot(right[t, k], chosen, preferred_element_type=F32).astype(BF16)
        return carry

    lax.fori_loop(0, terms * sec, one, 0, unroll=4)


def _second_kernel(cfg, n_left, meta, inner, *rest):
    lefts, outs, acc = rest[:n_left], rest[n_left:-1], rest[-1]
    terms, sec = inner.shape[:2]

    def one(k, carry):
        total = None
        for t in range(terms):
            left = jnp.concatenate([ref[t, k] for ref in lefts], axis=0)
            got = jnp.dot(inner[t, k], left, preferred_element_type=F32)
            total = got if total is None else total + got
        acc[k] = total
        return carry

    lax.fori_loop(0, sec, one, 0)
    _emit(cfg, meta, acc, outs)


def _step_kernel(cfg, step, n_left, n_shard, last, meta, *refs):
    it = iter(refs)
    take = lambda n: [next(it) for _ in range(n)]
    shards = take(n_shard)
    basis_h, (pre_h,), olds_h, (right_h,), left_h = take(step), take(1), take(step - 1), take(1), take(n_left)
    v_h, sig_h, dots = take(3)
    outs = take(cfg["n_out"])
    basis, (pre,), olds, (right,), lefts = take(step), take(1), take(step - 1), take(1), take(n_left)
    vnew, sig, vb, acc, sem = take(5)
    env_pos = meta[0]
    n_sec, states, width = vnew.shape
    sec = cfg["sec"]
    count = n_sec * states * width
    copies = []
    for i, (a, b) in enumerate(zip([*basis_h, pre_h, *olds_h, right_h, *left_h], [*basis, pre, *olds, right, *lefts])):
        copies.append(pltpu.make_async_copy(a, b, sem.at[i]))
        copies[-1].start()
    n_in = len(copies)
    v_out = pltpu.make_async_copy(vnew, v_h, sem.at[n_in])
    sig_out = pltpu.make_async_copy(sig, sig_h, sem.at[n_in + 1])
    for i, shard in enumerate(shards):
        s0, r0 = meta[cfg["shard_at"] + 2 * i], meta[cfg["shard_at"] + 2 * i + 1]
        rows = shard.shape[1]
        for k in range(shard.shape[0]):
            sig[s0 + k, pl.ds(pl.multiple_of(r0, rows), rows), :] = shard[k].astype(BF16)
    sig_out.start()
    for c in copies[:step]:
        c.wait()
    over = functools.partial(_over, n_sec, states, width)
    sums = over(step, lambda s, r: tuple(_fold(b[s, r, :] * sig[s, r, :].astype(F32)) for b in basis))
    proj = [x / count for x in sums]
    copies[step].wait()

    def trial_pass(s, r):
        resid = sig[s, r, :].astype(F32)
        held = [b[s, r, :] for b in basis]
        for h, b in zip(proj, held):
            resid = resid - h * b
        trial = resid * pre[s, r, :]
        vnew[s, r, :] = trial
        return tuple(_fold(b * trial) for b in held)

    back = [x / count for x in over(step, trial_pass)]

    def shift_pass(s, r):
        trial = vnew[s, r, :]
        for g, b in zip(back, basis):
            trial = trial - g * b[s, r, :]
        vnew[s, r, :] = trial
        return (_fold(trial * trial),)

    (square,) = over(1, shift_pass)
    scale = lax.rsqrt(square / count + EPS)
    for c in copies[step + 1 : 2 * step]:
        c.wait()

    def final_pass(s, r):
        value = vnew[s, r, :] * scale
        vnew[s, r, :] = value
        _write_vb(vb, s, r, value, env_pos, cfg["swap"])
        return tuple(_fold(value * o[s, r, :].astype(F32)) for o in [*olds, sig])

    cross = [x / count for x in over(step, final_pass)]
    v_out.start()
    scalars = proj + cross
    for c in copies[2 * step :]:
        c.wait()
    terms = right.shape[0]

    def one(k, carry):
        total = None
        for t in range(terms):
            chosen = vb[meta[cfg["pair_at"] + t * sec + k]]
            inner = jnp.dot(right[t, k], chosen, preferred_element_type=F32).astype(BF16)
            left = jnp.concatenate([ref[t, k] for ref in lefts], axis=0)
            got = jnp.dot(inner, left, preferred_element_type=F32)
            total = got if total is None else total + got
        acc[k] = total
        return carry

    lax.fori_loop(0, sec, one, 0)
    if last:
        rows_b = acc.shape[1]
        first = meta[2] * sec
        mine = []
        for b in [*basis, vnew]:
            def part(k, total, b=b):
                rows = pl.ds(pl.multiple_of(env_pos * rows_b, rows_b), rows_b)
                return total + _fold(b[first + k, rows, :] * acc[k])

            mine.append(jnp.sum(lax.fori_loop(0, sec, part, jnp.zeros((8, width), F32))) / count)
        scalars = scalars + mine
        for k in range(sec):
            acc[k, :, :] = acc[k, :, :]
        if cfg["direct"]:
            n, part = cfg["n_term"], width // cfg["n_term"]
            turned = cfg["turned"]
            for k in range(sec):
                outs[n][k] = acc[k].T
            z = meta[1]
            for s in range(n):
                rows = pl.ds(pl.multiple_of((z ^ s) * part, part), part)
                for k in range(sec):
                    outs[s][k] = outs[n][k, rows, :].astype(outs[s].dtype)
        else:
            for k in range(sec):
                outs[0][k] = acc[k].T
    else:
        _emit(cfg, meta, acc, outs)
    _put_scalars(dots, scalars)
    v_out.wait()
    sig_out.wait()


def solution(mesh):
    n_env, n_term, n_blk = (mesh.shape[a] for a in ("env", "term", "blk"))

    def on_device(psi, left_env, right_env, pairing, sector_dims, precond):
        return _on_device(n_env, n_term, n_blk, psi, left_env, right_env, pairing, sector_dims, precond)

    placed = (
        P(("parts", "blk"), None, None),
        P(("parts", "term"), "blk", "env", None),
        P(("parts", "term"), "blk", "env", None),
        P(("parts", "term"), "blk"),
        P("parts"),
        P(("parts", "blk"), None, None),
    )
    return jax.shard_map(
        on_device,
        mesh=mesh,
        in_specs=placed,
        out_specs=(P(None, ("parts", "blk"), "term", None), P("parts", None)),
        check_vma=False,
    )


def _xor(axis, n, s):
    return functools.partial(lax.ppermute, axis_name=axis, perm=[(i, i ^ s) for i in range(n)])


def _on_device(n_env, n_term, n_blk, psi, left_env, right_env, pairing, sector_dims, precond):
    sec, states, width = psi.shape
    terms = left_env.shape[0]
    n_sec = sec * n_blk
    half = right_env.shape[2]
    direct = n_env == 2 and n_blk == 2 and n_term in (2, 4)
    part = half // n_term
    cfg = dict(direct=direct, swap=direct, n_term=n_term, n_blk=n_blk, sec=sec, part=part, turned=None)
    env_pos, term_pos, blk_pos = (lax.axis_index(a) for a in ("env", "term", "blk"))
    other_env = _xor("env", 2, 1)
    other_blk = _xor("blk", 2, 1)

    places = []
    if direct:
        for b in range(2):
            for e in range(2):
                for s in range(n_term):
                    places += [(blk_pos ^ b) * sec, (env_pos ^ e) * half + (term_pos ^ s) * part]
    else:
        places = [0, 0]
    flat = jnp.stack([jnp.asarray(x, jnp.int32) for x in [env_pos, term_pos, blk_pos, *places]])
    meta = jnp.concatenate([flat, pairing.reshape(-1), sector_dims.reshape(-1)])
    cfg["shard_at"] = 3
    cfg["pair_at"] = 3 + len(places)
    cfg["dims_at"] = cfg["pair_at"] + terms * sec

    if direct:
        lefts = [left_env, other_env(left_env)]
        psi_o, pre_o = other_blk(psi), other_blk(precond)
    else:
        lefts = [lax.all_gather(left_env, "env", axis=2, tiled=True)]
        others = [lax.dynamic_slice_in_dim(
            lax.all_gather(x, "blk", axis=0, tiled=True), ((blk_pos + 1) % n_blk) * sec, sec * (n_blk - 1), 0
        ) for x in (psi, precond)] if n_blk == 2 else [psi, precond]
        psi_o, pre_o = others
    n_left = len(lefts)

    full = (n_sec, states, width)
    sds = jax.ShapeDtypeStruct
    params = pltpu.CompilerParams(vmem_limit_bytes=VMEM_LIMIT)
    v0, pret, inner = pl.pallas_call(
        functools.partial(_first_kernel, cfg),
        out_shape=(sds(full, F32), sds(full, F32), sds((terms, sec, half, states), BF16)),
        in_specs=_specs(SM, VM, VM, VM, VM, VM),
        out_specs=_specs(VM, VM, VM),
        scratch_shapes=[pltpu.VMEM(full, BF16), pltpu.VMEM(full, F32)],
        compiler_params=params,
        name="start_vector",
    )(meta, psi, psi_o, precond, pre_o, right_env)

    if direct:
        piece_shapes = [sds((sec, part, width), F32)] + [sds((sec, part, width), BF16)] * (n_term - 1)
    else:
        piece_shapes = [sds((sec, half, width), F32)]
    pieces = pl.pallas_call(
        functools.partial(_second_kernel, cfg, n_left),
        out_shape=tuple(piece_shapes),
        in_specs=_specs(SM, *[VM] * (1 + n_left)),
        out_specs=tuple(_specs(*[VM] * len(piece_shapes))),
        scratch_shapes=[pltpu.VMEM((sec, half, width), F32)],
        compiler_params=params,
        name="first_sigma",
    )(meta, inner, *lefts)

    live_own = lax.dynamic_slice_in_dim(sector_dims, blk_pos * sec, sec)[:, None, None]

    def reduce(pieces):
        if direct:
            got = [_xor("term", n_term, s)(pieces[s]) for s in range(1, n_term)]
            total = pieces[0]
            for g in got:
                total = total + g.astype(F32)
            row = env_pos * half + term_pos * part + lax.broadcasted_iota(jnp.int32, total.shape, 1)
            col = lax.broadcasted_iota(jnp.int32, total.shape, 2)
            return jnp.where((row < live_own) & (col < live_own), total, 0.0).astype(BF16)
        flat_sum = lax.psum_scatter(pieces[0].reshape(sec * half, width), "term", scatter_dimension=0, tiled=True)
        return flat_sum

    def gather(shard):
        if direct:
            along = [shard] + [_xor("term", n_term, s)(shard) for s in range(1, n_term)]
            along = along + [other_env(a) for a in along]
            return along + [other_blk(a) for a in along]
        whole = lax.all_gather(shard, "term", axis=0, tiled=True).reshape(sec, half, width)
        whole = lax.all_gather(whole, "env", axis=1, tiled=True)
        row = lax.broadcasted_iota(jnp.int32, whole.shape, 1)
        col = lax.broadcasted_iota(jnp.int32, whole.shape, 2)
        whole = jnp.where((row < live_own) & (col < live_own), whole, 0.0).astype(BF16)
        return [lax.all_gather(whole, "blk", axis=0, tiled=True)]

    basis, olds, rows_out = [v0], [], []
    chunk = states // n_term
    dots_all = []
    for step in range(1, ITERS):
        last = step + 1 == ITERS
        shards = gather(reduce(pieces))
        if last:
            if direct:
                outs = [sds((sec, chunk, half), F32)] + [sds((sec, chunk, half), BF16)] * (n_term - 1)
                outs.append(sds((sec, states, half), F32))
            else:
                outs = [sds((sec, states, half), F32)]
        else:
            outs = piece_shapes
        cfg_step = dict(cfg, n_out=len(outs))
        moved = [sds(full, F32)] * step + [sds(full, F32)] + [sds(full, BF16)] * (step - 1)
        moved += [sds(right_env.shape, BF16)] + [sds(x.shape, BF16) for x in lefts]
        results = pl.pallas_call(
            functools.partial(_step_kernel, cfg_step, step, n_left, len(shards), last),
            out_shape=(sds(full, F32), sds(full, BF16), sds((16, 128), F32), *outs),
            in_specs=_specs(SM, *[VM] * len(shards), *[ANY] * len(moved)),
            out_specs=tuple(_specs(ANY, ANY, VM, *[VM] * len(outs))),
            scratch_shapes=[pltpu.VMEM(m.shape, m.dtype) for m in moved]
            + [
                pltpu.VMEM(full, F32),
                pltpu.VMEM(full, BF16),
                pltpu.VMEM(full, BF16),
                pltpu.VMEM((sec, half, width), F32),
                pltpu.SemaphoreType.DMA((len(moved) + 2,)),
            ],
            compiler_params=params,
            name=f"vector_and_sigma_{step}",
        )(meta, *shards, *basis, pret, *olds, right_env, *lefts)
        vec, sig, dots = results[:3]
        pieces = results[3:]
        basis.append(vec)
        olds.append(sig)
        dots_all.append(dots)
        mine = lax.dynamic_slice(sig, (blk_pos * sec, 0, term_pos * chunk), (sec, states, chunk))
        rows_out.append(jnp.swapaxes(mine, 1, 2).astype(F32))

    tail = dots_all[-1]
    n_mid = 2 * (ITERS - 1)
    if direct:
        total, scal = pieces[0], tail
        for s in range(1, n_term):
            total = total + _xor("term", n_term, s)(pieces[s]).astype(F32)
            scal = scal + _xor("term", n_term, s)(tail)
        row = term_pos * chunk + lax.broadcasted_iota(jnp.int32, total.shape, 1)
        col = env_pos * half + lax.broadcasted_iota(jnp.int32, total.shape, 2)
        own = jnp.where((row < live_own) & (col < live_own), total, 0.0)
        theirs = other_env(own.astype(BF16)).astype(F32)
        scal = scal + other_env(scal)
        scal = scal + other_blk(scal)
        both = jnp.where(env_pos == 0, jnp.concatenate([own, theirs], 2), jnp.concatenate([theirs, own], 2))
    else:
        own = lax.psum_scatter(pieces[0], "term", scatter_dimension=1, tiled=True)
        both = lax.all_gather(own, "env", axis=2, tiled=True)
        row = term_pos * chunk + lax.broadcasted_iota(jnp.int32, both.shape, 1)
        col = lax.broadcasted_iota(jnp.int32, both.shape, 2)
        both = jnp.where((row < live_own) & (col < live_own), both, 0.0)
        scal = lax.psum(tail, ("term", "env", "blk"))
    rows_out.append(both)
    first, second = dots_all[0][:, 0], tail[:, 0]
    subspace = jnp.stack([
        jnp.stack([first[0], first[1], second[2]]),
        jnp.stack([second[0], second[1], second[3]]),
        scal[n_mid : n_mid + ITERS, 0],
    ])
    return jnp.stack(rows_out), subspace
```

```python
import functools

import jax
import jax.numpy as jnp
from jax import lax
from jax.experimental import pallas as pl
from jax.experimental.pallas import tpu as pltpu
from jax.sharding import PartitionSpec as P

ITERS = 3
EPS = 1e-06
F32, BF16 = jnp.float32, jnp.bfloat16
ROWS = 32
VMEM_LIMIT = 40 * 1024 * 1024


def _specs(*shapes):
    return [pl.BlockSpec(memory_space=s) for s in shapes]


HB, VM, SM = pltpu.HBM, pltpu.VMEM, pltpu.SMEM


def _hbm(*arrays):
    return [pltpu.with_memory_space_constraint(x, pltpu.HBM) for x in arrays]


def _vmem(*arrays):
    return [pltpu.with_memory_space_constraint(x, pltpu.VMEM) for x in arrays]


def _fold(x):
    return jnp.sum(x.reshape(x.shape[0] // 8, 8, x.shape[1]), axis=0)


def _over(n_sec, states, width, n_acc, body):
    blocks = states // ROWS

    def step(i, accs):
        sec, rows = i // blocks, pl.ds(pl.multiple_of((i % blocks) * ROWS, ROWS), ROWS)
        return tuple(a + b for a, b in zip(accs, body(sec, rows)))

    zero = tuple(jnp.zeros((8, width), F32) for _ in range(n_acc))
    return tuple(jnp.sum(a) for a in lax.fori_loop(0, n_sec * blocks, step, zero, unroll=2))


def _write_vb(vb, sec, rows, value, env_pos, swap):
    half = value.shape[1] // 2
    low = value.astype(BF16)
    if swap:
        turned = jnp.concatenate([value[:, half:], value[:, :half]], axis=1).astype(BF16)
        low = jnp.where(env_pos == 0, low, turned)
    vb[sec, rows, :] = low


def _put_scalars(ref, values):
    shape = ref.shape
    row = lax.broadcasted_iota(jnp.int32, shape, 0)
    out = jnp.zeros(shape, F32)
    for index, value in enumerate(values):
        out = jnp.where(row == index, value, out)
    ref[...] = out


def _emit(cfg, meta, acc, outs):
    if cfg["direct"]:
        n, part = cfg["n_term"], cfg["part"]
        z = meta[1]
        for s in range(n):
            rows = pl.ds(pl.multiple_of((z ^ s) * part, part), part)
            for k in range(cfg["sec"]):
                outs[s][k] = acc[k, rows, :].astype(outs[s].dtype)
    else:
        outs[0][...] = acc[...]


def _first_kernel(cfg, meta, psi, psi_o, pre, pre_o, right, *refs):
    held_h, held, (vb, work, sem) = refs[:3], refs[3:6], refs[6:]
    v0, pret, inner = held
    saves = [pltpu.make_async_copy(a, b, sem.at[i]) for i, (a, b) in enumerate(zip(held, held_h))]
    sec, states, width = psi.shape
    n_sec = sec * cfg["n_blk"]
    blk, env_pos = meta[2], meta[0]
    base = blk * sec
    for part, (p_ref, c_ref) in enumerate(((psi, pre), (psi_o, pre_o))):
        for k in range(p_ref.shape[0]):
            at = lax.rem(base + part * sec + k, n_sec)
            live = meta[cfg["dims_at"] + at]
            row = lax.broadcasted_iota(jnp.int32, (states, width), 0)
            col = lax.broadcasted_iota(jnp.int32, (states, width), 1)
            value = jnp.where((row < live) & (col < live), p_ref[k].astype(F32).T, 0.0)
            work[at] = value
            pret[at] = c_ref[k].T
    (total,) = _over(n_sec, states, width, 1, lambda s, r: (_fold(work[s, r, :] * work[s, r, :]),))
    scale = lax.rsqrt(total / (n_sec * states * width) + EPS)

    def make(s, r):
        value = work[s, r, :] * scale
        v0[s, r, :] = value
        _write_vb(vb, s, r, value, env_pos, cfg["swap"])
        return ()

    _over(n_sec, states, width, 0, make)
    saves[0].start()
    saves[1].start()
    terms = right.shape[0]

    def one(i, carry):
        k, t = i % sec, i // sec
        chosen = vb[meta[cfg["pair_at"] + t * sec + k]]
        inner[t, k] = jnp.dot(right[t, k], chosen, preferred_element_type=F32).astype(BF16)
        return carry

    lax.fori_loop(0, terms * sec, one, 0, unroll=4)
    saves[2].start()
    for c in saves:
        c.wait()


def _second_kernel(cfg, n_left, meta, *refs):
    ins_h, outs, acc = refs[: 1 + n_left], refs[1 + n_left : -3 - n_left], refs[-3 - n_left]
    ins, sem = refs[-2 - n_left : -1], refs[-1]
    terms, sec = ins[0].shape[:2]
    copies = [
        [pltpu.make_async_copy(a.at[:, k], b.at[:, k], sem.at[i, k]) for i, (a, b) in enumerate(zip(ins_h, ins))]
        for k in range(sec)
    ]
    for group in copies:
        for c in group:
            c.start()
    for k in range(sec):
        for c in copies[k]:
            c.wait()
        total = None
        for t in range(terms):
            left = jnp.concatenate([ref[t, k] for ref in ins[1:]], axis=0)
            got = jnp.dot(ins[0][t, k], left, preferred_element_type=F32)
            total = got if total is None else total + got
        acc[k] = total
    _emit(cfg, meta, acc, outs)


def _step_kernel(cfg, step, n_left, n_shard, last, meta, *refs):
    it = iter(refs)
    take = lambda n: [next(it) for _ in range(n)]
    shards = take(n_shard)
    basis_h, (pre_h,), olds_h, (right_h,), left_h = take(step), take(1), take(step - 1), take(1), take(n_left)
    v_h, sig_h, dots = take(3)
    outs = take(cfg["n_out"])
    basis, (pre,), olds, (right,), lefts = take(step), take(1), take(step - 1), take(1), take(n_left)
    vnew, sig, vb, acc, sem = take(5)
    env_pos = meta[0]
    n_sec, states, width = vnew.shape
    sec = cfg["sec"]
    count = n_sec * states * width
    copies = []
    for i, (a, b) in enumerate(zip([*basis_h, pre_h, *olds_h, right_h, *left_h], [*basis, pre, *olds, right, *lefts])):
        copies.append(pltpu.make_async_copy(a, b, sem.at[i]))
        copies[-1].start()
    n_in = len(copies)
    v_out = pltpu.make_async_copy(vnew, v_h, sem.at[n_in])
    sig_out = pltpu.make_async_copy(sig, sig_h, sem.at[n_in + 1])
    for i, shard in enumerate(shards):
        s0, r0 = meta[cfg["shard_at"] + 2 * i], meta[cfg["shard_at"] + 2 * i + 1]
        rows = shard.shape[1]
        for k in range(shard.shape[0]):
            sig[s0 + k, pl.ds(pl.multiple_of(r0, rows), rows), :] = shard[k].astype(BF16)
    sig_out.start()
    for c in copies[:step]:
        c.wait()
    over = functools.partial(_over, n_sec, states, width)
    sums = over(step, lambda s, r: tuple(_fold(b[s, r, :] * sig[s, r, :].astype(F32)) for b in basis))
    proj = [x / count for x in sums]
    copies[step].wait()

    def trial_pass(s, r):
        resid = sig[s, r, :].astype(F32)
        held = [b[s, r, :] for b in basis]
        for h, b in zip(proj, held):
            resid = resid - h * b
        trial = resid * pre[s, r, :]
        vnew[s, r, :] = trial
        return tuple(_fold(b * trial) for b in held)

    back = [x / count for x in over(step, trial_pass)]

    def shift_pass(s, r):
        trial = vnew[s, r, :]
        for g, b in zip(back, basis):
            trial = trial - g * b[s, r, :]
        vnew[s, r, :] = trial
        return (_fold(trial * trial),)

    (square,) = over(1, shift_pass)
    scale = lax.rsqrt(square / count + EPS)
    for c in copies[step + 1 : 2 * step]:
        c.wait()

    def final_pass(s, r):
        value = vnew[s, r, :] * scale
        vnew[s, r, :] = value
        _write_vb(vb, s, r, value, env_pos, cfg["swap"])
        return tuple(_fold(value * o[s, r, :].astype(F32)) for o in [*olds, sig])

    cross = [x / count for x in over(step, final_pass)]
    v_out.start()
    scalars = proj + cross
    for c in copies[2 * step :]:
        c.wait()
    terms = right.shape[0]

    def one(k, carry):
        total = None
        for t in range(terms):
            chosen = vb[meta[cfg["pair_at"] + t * sec + k]]
            inner = jnp.dot(right[t, k], chosen, preferred_element_type=F32).astype(BF16)
            left = jnp.concatenate([ref[t, k] for ref in lefts], axis=0)
            got = jnp.dot(inner, left, preferred_element_type=F32)
            total = got if total is None else total + got
        acc[k] = total
        return carry

    lax.fori_loop(0, sec, one, 0)
    if last:
        rows_b = acc.shape[1]
        first = meta[2] * sec
        mine = []
        for b in [*basis, vnew]:
            def part(k, total, b=b):
                rows = pl.ds(pl.multiple_of(env_pos * rows_b, rows_b), rows_b)
                return total + _fold(b[first + k, rows, :] * acc[k])

            mine.append(jnp.sum(lax.fori_loop(0, sec, part, jnp.zeros((8, width), F32))) / count)
        scalars = scalars + mine
        if cfg["direct"]:
            n, part = cfg["n_term"], width // cfg["n_term"]
            for k in range(sec):
                outs[n][k] = acc[k].T
            z = meta[1]
            for s in range(n):
                rows = pl.ds(pl.multiple_of((z ^ s) * part, part), part)
                for k in range(sec):
                    outs[s][k] = outs[n][k, rows, :].astype(outs[s].dtype)
        else:
            for k in range(sec):
                outs[0][k] = acc[k].T
    else:
        _emit(cfg, meta, acc, outs)
    _put_scalars(dots, scalars)
    v_out.wait()
    sig_out.wait()


def solution(mesh):
    n_env, n_term, n_blk = (mesh.shape[a] for a in ("env", "term", "blk"))

    def on_device(psi, left_env, right_env, pairing, sector_dims, precond):
        return _on_device(n_env, n_term, n_blk, psi, left_env, right_env, pairing, sector_dims, precond)

    placed = (
        P(("parts", "blk"), None, None),
        P(("parts", "term"), "blk", "env", None),
        P(("parts", "term"), "blk", "env", None),
        P(("parts", "term"), "blk"),
        P("parts"),
        P(("parts", "blk"), None, None),
    )
    return jax.shard_map(
        on_device,
        mesh=mesh,
        in_specs=placed,
        out_specs=(P(None, ("parts", "blk"), "term", None), P("parts", None)),
        check_vma=False,
    )


def _xor(axis, n, s):
    return functools.partial(lax.ppermute, axis_name=axis, perm=[(i, i ^ s) for i in range(n)])


def _on_device(n_env, n_term, n_blk, psi, left_env, right_env, pairing, sector_dims, precond):
    sec, states, width = psi.shape
    terms = left_env.shape[0]
    n_sec = sec * n_blk
    half = right_env.shape[2]
    direct = n_env == 2 and n_blk == 2 and n_term in (2, 4)
    part = half // n_term
    cfg = dict(direct=direct, swap=direct, n_term=n_term, n_blk=n_blk, sec=sec, part=part)
    env_pos, term_pos, blk_pos = (lax.axis_index(a) for a in ("env", "term", "blk"))
    other_env = _xor("env", 2, 1)
    other_blk = _xor("blk", 2, 1)

    places = []
    if direct:
        for b in range(2):
            for e in range(2):
                for s in range(n_term):
                    places += [(blk_pos ^ b) * sec, (env_pos ^ e) * half + (term_pos ^ s) * part]
    else:
        places = [0, 0]
    flat = jnp.stack([jnp.asarray(x, jnp.int32) for x in [env_pos, term_pos, blk_pos, *places]])
    meta = jnp.concatenate([flat, pairing.reshape(-1), sector_dims.reshape(-1)])
    cfg["shard_at"] = 3
    cfg["pair_at"] = 3 + len(places)
    cfg["dims_at"] = cfg["pair_at"] + terms * sec

    if direct:
        lefts = [left_env, other_env(left_env)]
        psi_o, pre_o = other_blk(psi), other_blk(precond)
    else:
        lefts = [lax.all_gather(left_env, "env", axis=2, tiled=True)]
        others = [lax.dynamic_slice_in_dim(
            lax.all_gather(x, "blk", axis=0, tiled=True), ((blk_pos + 1) % n_blk) * sec, sec * (n_blk - 1), 0
        ) for x in (psi, precond)] if n_blk == 2 else [psi, precond]
        psi_o, pre_o = others
    n_left = len(lefts)

    full = (n_sec, states, width)
    sds = jax.ShapeDtypeStruct
    params = pltpu.CompilerParams(vmem_limit_bytes=VMEM_LIMIT)
    v0, pret, inner = pl.pallas_call(
        functools.partial(_first_kernel, cfg),
        out_shape=(HB(full, F32), HB(full, F32), HB((terms, sec, half, states), BF16)),
        in_specs=_specs(SM, VM, VM, VM, VM, VM),
        out_specs=_specs(HB, HB, HB),
        scratch_shapes=[
            pltpu.VMEM(full, F32),
            pltpu.VMEM(full, F32),
            pltpu.VMEM((terms, sec, half, states), BF16),
            pltpu.VMEM(full, BF16),
            pltpu.VMEM(full, F32),
            pltpu.SemaphoreType.DMA((3,)),
        ],
        compiler_params=params,
        name="start_vector",
    )(meta, psi, psi_o, precond, pre_o, right_env)

    if direct:
        piece_shapes = [VM((sec, part, width), F32)] + [VM((sec, part, width), BF16)] * (n_term - 1)
    else:
        piece_shapes = [VM((sec, half, width), F32)]
    pieces = pl.pallas_call(
        functools.partial(_second_kernel, cfg, n_left),
        out_shape=tuple(piece_shapes),
        in_specs=_specs(SM, *[HB] * (1 + n_left)),
        out_specs=tuple(_specs(*[VM] * len(piece_shapes))),
        scratch_shapes=[
            pltpu.VMEM((sec, half, width), F32),
            pltpu.VMEM(inner.shape, BF16),
            *[pltpu.VMEM(x.shape, BF16) for x in lefts],
            pltpu.SemaphoreType.DMA((1 + n_left, sec)),
        ],
        compiler_params=params,
        name="first_sigma",
    )(meta, *_hbm(inner, *lefts))

    live_own = lax.dynamic_slice_in_dim(sector_dims, blk_pos * sec, sec)[:, None, None]

    def reduce(pieces):
        if direct:
            got = [_xor("term", n_term, s)(pieces[s]) for s in range(1, n_term)]
            total = pieces[0]
            for g in got:
                total = total + g.astype(F32)
            row = env_pos * half + term_pos * part + lax.broadcasted_iota(jnp.int32, total.shape, 1)
            col = lax.broadcasted_iota(jnp.int32, total.shape, 2)
            return jnp.where((row < live_own) & (col < live_own), total, 0.0).astype(BF16)
        flat_sum = lax.psum_scatter(pieces[0].reshape(sec * half, width), "term", scatter_dimension=0, tiled=True)
        return flat_sum

    def gather(shard):
        if direct:
            along = [shard] + [_xor("term", n_term, s)(shard) for s in range(1, n_term)]
            along = along + [other_env(a) for a in along]
            return along + [other_blk(a) for a in along]
        whole = lax.all_gather(shard, "term", axis=0, tiled=True).reshape(sec, half, width)
        whole = lax.all_gather(whole, "env", axis=1, tiled=True)
        row = lax.broadcasted_iota(jnp.int32, whole.shape, 1)
        col = lax.broadcasted_iota(jnp.int32, whole.shape, 2)
        whole = jnp.where((row < live_own) & (col < live_own), whole, 0.0).astype(BF16)
        return [lax.all_gather(whole, "blk", axis=0, tiled=True)]

    basis, olds, rows_out = [v0], [], []
    chunk = states // n_term
    dots_all = []
    for step in range(1, ITERS):
        last = step + 1 == ITERS
        shards = gather(reduce(pieces))
        if last:
            if direct:
                outs = [VM((sec, chunk, half), F32)] + [VM((sec, chunk, half), BF16)] * (n_term - 1)
                outs.append(VM((sec, states, half), F32))
            else:
                outs = [VM((sec, states, half), F32)]
        else:
            outs = piece_shapes
        cfg_step = dict(cfg, n_out=len(outs))
        moved = [sds(full, F32)] * step + [sds(full, F32)] + [sds(full, BF16)] * (step - 1)
        moved += [sds(right_env.shape, BF16)] + [sds(x.shape, BF16) for x in lefts]
        results = pl.pallas_call(
            functools.partial(_step_kernel, cfg_step, step, n_left, len(shards), last),
            out_shape=(HB(full, F32), HB(full, BF16), VM((16, 128), F32), *outs),
            in_specs=_specs(SM, *[VM] * len(shards), *[HB] * len(moved)),
            out_specs=tuple(_specs(HB, HB, VM, *[VM] * len(outs))),
            scratch_shapes=[pltpu.VMEM(m.shape, m.dtype) for m in moved]
            + [
                pltpu.VMEM(full, F32),
                pltpu.VMEM(full, BF16),
                pltpu.VMEM(full, BF16),
                pltpu.VMEM((sec, half, width), F32),
                pltpu.SemaphoreType.DMA((len(moved) + 2,)),
            ],
            compiler_params=params,
            name=f"vector_and_sigma_{step}",
        )(meta, *_vmem(*shards), *_hbm(*basis, pret, *olds, right_env, *lefts))
        vec, sig, dots = results[:3]
        pieces = results[3:]
        basis.append(vec)
        olds.append(sig)
        dots_all.append(dots)
        mine = lax.dynamic_slice(sig, (blk_pos * sec, 0, term_pos * chunk), (sec, states, chunk))
        rows_out.append(jnp.swapaxes(mine, 1, 2).astype(F32))

    tail = dots_all[-1]
    n_mid = 2 * (ITERS - 1)
    if direct:
        total, scal = pieces[0], tail
        for s in range(1, n_term):
            total = total + _xor("term", n_term, s)(pieces[s]).astype(F32)
            scal = scal + _xor("term", n_term, s)(tail)
        row = term_pos * chunk + lax.broadcasted_iota(jnp.int32, total.shape, 1)
        col = env_pos * half + lax.broadcasted_iota(jnp.int32, total.shape, 2)
        own = jnp.where((row < live_own) & (col < live_own), total, 0.0)
        theirs = other_env(own.astype(BF16)).astype(F32)
        scal = scal + other_env(scal)
        scal = scal + other_blk(scal)
        both = jnp.where(env_pos == 0, jnp.concatenate([own, theirs], 2), jnp.concatenate([theirs, own], 2))
    else:
        own = lax.psum_scatter(pieces[0], "term", scatter_dimension=1, tiled=True)
        both = lax.all_gather(own, "env", axis=2, tiled=True)
        row = term_pos * chunk + lax.broadcasted_iota(jnp.int32, both.shape, 1)
        col = lax.broadcasted_iota(jnp.int32, both.shape, 2)
        both = jnp.where((row < live_own) & (col < live_own), both, 0.0)
        scal = lax.psum(tail, ("term", "env", "blk"))
    rows_out.append(both)
    first, second = dots_all[0][:, 0], tail[:, 0]
    subspace = jnp.stack([
        jnp.stack([first[0], first[1], second[2]]),
        jnp.stack([second[0], second[1], second[3]]),
        scal[n_mid : n_mid + ITERS, 0],
    ])
    return jnp.stack(rows_out), subspace
```

```python
import functools

import jax
import jax.numpy as jnp
from jax import lax
from jax.experimental import pallas as pl
from jax.experimental.pallas import tpu as pltpu
from jax.sharding import PartitionSpec as P

ITERS = 3
EPS = 1e-06
F32, BF16 = jnp.float32, jnp.bfloat16
ROWS = 64
TAIL_ROWS = 16
VMEM_LIMIT = 32 * 1024 * 1024
HB, VM, SM = pltpu.HBM, pltpu.VMEM, pltpu.SMEM


def _specs(*shapes):
    return [pl.BlockSpec(memory_space=s) for s in shapes]


def _hbm(*arrays):
    return [pltpu.with_memory_space_constraint(x, HB) for x in arrays]


def _vmem(*arrays):
    return [pltpu.with_memory_space_constraint(x, VM) for x in arrays]


def _fold(x):
    return jnp.sum(x.reshape(x.shape[0] // 8, 8, x.shape[1]), axis=0)


def _over(n_sec, states, width, n_acc, body):
    blocks = states // ROWS

    def step(i, accs):
        for b in range(blocks):
            accs = tuple(x + y for x, y in zip(accs, body(i, slice(b * ROWS, (b + 1) * ROWS))))
        return accs

    zero = tuple(jnp.zeros((8, width), F32) for _ in range(n_acc))
    return tuple(jnp.sum(a) for a in lax.fori_loop(0, n_sec, step, zero))


def _low(cfg, value, env_pos):
    low = value.astype(BF16)
    if cfg["direct"]:
        half = value.shape[1] // 2
        turned = jnp.concatenate([value[:, half:], value[:, :half]], axis=1).astype(BF16)
        low = jnp.where(env_pos == 0, low, turned)
    return low


def _put_scalars(ref, values):
    shape = ref.shape
    row = lax.broadcasted_iota(jnp.int32, shape, 0)
    out = jnp.zeros(shape, F32)
    for index, value in enumerate(values):
        out = jnp.where(row == index, value, out)
    ref[...] = out


def _emit(cfg, meta, acc, outs):
    if cfg["direct"]:
        part, z = cfg["part"], meta[1]
        for s in range(cfg["n_term"]):
            rows = pl.ds(pl.multiple_of((z ^ s) * part, part), part)
            outs[s][...] = acc[:, rows, :].astype(outs[s].dtype)
    else:
        outs[0][...] = acc[...]


def _first_kernel(cfg, meta, psi, psi_o, pre, pre_o, right, start, pret, inner, scale_ref, vb):
    sec, states, width = psi.shape
    n_sec = sec * cfg["n_blk"]
    blk, env_pos = meta[2], meta[0]
    base = blk * sec
    for part, (p_ref, c_ref) in enumerate(((psi, pre), (psi_o, pre_o))):
        for k in range(p_ref.shape[0]):
            at = lax.rem(base + part * sec + k, n_sec)
            live = meta[cfg["dims_at"] + at]
            row = lax.broadcasted_iota(jnp.int32, (states, width), 0)
            col = lax.broadcasted_iota(jnp.int32, (states, width), 1)
            value = jnp.where((row < live) & (col < live), p_ref[k].astype(F32).T, 0.0)
            start[at] = value.astype(BF16)
            pret[at] = c_ref[k].T

    def square(s, r):
        value = start[s, r, :].astype(F32)
        return (_fold(value * value),)

    (total,) = _over(n_sec, states, width, 1, square)
    scale = lax.rsqrt(total / (n_sec * states * width) + EPS)
    _put_scalars(scale_ref, [scale] * 8)

    def make(s, r):
        vb[s, r, :] = _low(cfg, start[s, r, :].astype(F32) * scale, env_pos)
        return ()

    _over(n_sec, states, width, 0, make)
    for k in range(sec):
        for t in range(right.shape[0]):
            chosen = vb[meta[cfg["pair_at"] + t * sec + k]]
            inner[t, k] = jnp.dot(right[t, k], chosen, preferred_element_type=F32).astype(BF16)


def _second_kernel(cfg, k0, n_left, meta, inner, *refs):
    lefts, far_h, outs = refs[: n_left - 1], refs[n_left - 1], refs[n_left:-3]
    far, acc, sem = refs[-3:]
    terms, count = far.shape[:2]
    move = pltpu.make_async_copy(far_h, far, sem)
    move.start()
    move.wait()
    for k in range(count):
        total = None
        for t in range(terms):
            left = jnp.concatenate([ref[t, k0 + k] for ref in lefts] + [far[t, k]], axis=0)
            got = jnp.dot(inner[t, k0 + k], left, preferred_element_type=F32)
            total = got if total is None else total + got
        acc[k] = total
    _emit(cfg, meta, acc, outs)


def _step_kernel(cfg, step, places, chunks, n_near, last, meta, *refs):
    it = iter(refs)
    take = lambda n: [next(it) for _ in range(n)]
    shards = take(len(places))
    (start, scale_ref), vecs, (pre,) = take(2), take(step - 1), take(1)
    olds_h, (right_h,), near_h, far_h = take(step - 1), take(1), take(n_near), take(len(chunks))
    (sig_h,) = take(1)
    vnew, dots = (None, None) if last else take(2)
    outs = take(cfg["n_out"])
    if last:
        vnew, turned = take(2)
    olds, (right,), near, (far,) = take(step - 1), take(1), take(n_near), take(1)
    sig, vb, acc, sem = take(4)
    env_pos, z, blk = meta[0], meta[1], meta[2]
    n_sec, states, width = vnew.shape
    sec, half, part = cfg["sec"], right.shape[2], cfg["part"]
    count = n_sec * states * width
    moves = [*zip(olds_h, olds), (right_h, right), *zip(near_h, near)]
    moves += [(h, far.at[:, k0 : k0 + nk]) for (k0, nk), h in zip(chunks, far_h)]
    moves = [pltpu.make_async_copy(a, b, sem.at[i]) for i, (a, b) in enumerate(moves)]
    for c in moves:
        c.start()
    save = pltpu.make_async_copy(sig, sig_h, sem.at[len(moves)])
    scale0 = scale_ref[0, 0]
    basis = [lambda s, r: start[s, r, :].astype(F32) * scale0]
    basis += [lambda s, r, v=v: v[s, r, :] for v in vecs]

    pairs = [(j, l) for j in range(step) for l in range(j, step)]
    accs = [jnp.zeros((8, width), F32) for _ in range(2 * step + len(pairs))]
    blocks = []
    for ref, place in zip(shards, places):
        if place is None:
            for s in range(n_sec):
                for r in range(0, states, ROWS):
                    blocks.append((ref, (s, slice(r, r + ROWS)), s, slice(r, r + ROWS)))
            continue
        b, e, hops, k0 = place
        for m, s in enumerate(hops):
            rows = pl.ds(pl.multiple_of((env_pos ^ e) * half + (z ^ s) * part, part), part)
            for k in range(ref.shape[1]):
                blocks.append((ref, (m, k), (blk ^ b) * sec + k0 + k, rows))
    for ref, at, s, r in blocks:
        low = ref[at]
        sig[s, r, :] = low
        value, cond = low.astype(F32), pre[s, r, :]
        scaled = value * cond
        held = [b(s, r) for b in basis]
        terms_ = [_fold(h * value) for h in held] + [_fold(h * scaled) for h in held]
        condh = [h * cond for h in held]
        terms_ += [_fold(condh[j] * held[l]) for j, l in pairs]
        accs = [a + t for a, t in zip(accs, terms_)]
    save.start()
    sums = [jnp.sum(a) / count for a in accs]
    proj = sums[:step]
    gram = {}
    for (j, l), value in zip(pairs, sums[2 * step :]):
        gram[j, l] = gram[l, j] = value
    back = [sums[step + j] - sum(proj[l] * gram[j, l] for l in range(step)) for j in range(step)]

    over = functools.partial(_over, n_sec, states, width)
    for c in moves[: step - 1]:
        c.wait()

    def trial_pass(s, r):
        value = sig[s, r, :].astype(F32)
        held = [b(s, r) for b in basis]
        trial = value
        for h, b in zip(proj, held):
            trial = trial - h * b
        trial = trial * pre[s, r, :]
        for g, b in zip(back, held):
            trial = trial - g * b
        vnew[s, r, :] = trial
        crossed = [o[s, r, :].astype(F32) for o in olds] + [value]
        return (_fold(trial * trial), *[_fold(trial * o) for o in crossed])

    square, *cross = over(1 + step, trial_pass)
    scale = lax.rsqrt(square / count + EPS)
    cross = [x * scale / count for x in cross]

    def final_pass(s, r):
        value = vnew[s, r, :] * scale
        vnew[s, r, :] = value
        vb[s, r, :] = _low(cfg, value, env_pos)
        return ()

    over(0, final_pass)
    for c in moves[step - 1 :]:
        c.wait()
    for k in range(sec):
        total = None
        for t in range(right.shape[0]):
            chosen = vb[meta[cfg["pair_at"] + t * sec + k]]
            inner = jnp.dot(right[t, k], chosen, preferred_element_type=F32).astype(BF16)
            left = jnp.concatenate([ref[t, k] for ref in [*near, far]], axis=0)
            got = jnp.dot(inner, left, preferred_element_type=F32)
            total = got if total is None else total + got
        acc[k] = total
    scalars = proj + cross
    if not last:
        _emit(cfg, meta, acc, outs)
        _put_scalars(dots, scalars)
        save.wait()
        return

    rows = pl.ds(pl.multiple_of(env_pos * half, half), half)
    mine = []
    for b in [*basis, lambda s, r: vnew[s, r, :]]:
        total = jnp.zeros((8, width), F32)
        for k in range(sec):
            total = total + _fold(b(blk * sec + k, rows) * acc[k])
        mine.append(jnp.sum(total) / count)
    known, pieces = outs[0], outs[1:]
    _put_scalars(known, scalars)
    for k in range(sec):
        turned[k] = acc[k].T
    chunk = states // cfg["n_term"]
    if cfg["direct"]:
        for s in range(cfg["n_term"]):
            rows = pl.ds(pl.multiple_of((z ^ s) * chunk, chunk), chunk)
            for k in range(sec):
                pieces[s][k * chunk : (k + 1) * chunk, :] = turned[k, rows, :].astype(pieces[s].dtype)
            row = lax.broadcasted_iota(jnp.int32, (TAIL_ROWS, half), 0)
            tail = jnp.zeros((TAIL_ROWS, half), F32)
            for j, value in enumerate(mine):
                rest = jnp.full((TAIL_ROWS, half), value, F32)
                for p in range(3):
                    cut = rest.astype(BF16).astype(F32)
                    tail = jnp.where(row == 3 * j + p, cut, tail)
                    rest = rest - cut
            pieces[s][sec * chunk :, :] = tail.astype(pieces[s].dtype)
    else:
        pieces[0][...] = turned[...]
        _put_scalars(pieces[1], mine)
    save.wait()


def _rows_kernel(cfg, meta, sig_a, sig_b, out_h, sig, turned, rows, sem):
    chunk = rows.shape[2]
    first = pl.ds(pl.multiple_of(meta[1] * chunk, chunk), chunk)
    own = pl.ds(meta[2] * cfg["sec"], cfg["sec"])
    loads = [pltpu.make_async_copy(ref.at[own], sig.at[i], sem.at[i]) for i, ref in enumerate((sig_a, sig_b))]
    for c in loads:
        c.start()
    for i, c in enumerate(loads):
        c.wait()
        for k in range(rows.shape[1]):
            turned[i, k] = sig[i, k].astype(F32).T
            rows[i, k] = turned[i, k, first, :]
    save = pltpu.make_async_copy(rows, out_h.at[0 : rows.shape[0]], sem.at[2])
    save.start()
    save.wait()


def _final_kernel(cfg, meta, first, known, sums, own, theirs, held_h, out_h, sub, last_rows, sem):
    del held_h
    mine, other = own[...], theirs[...].astype(F32)
    swapped = jnp.where(meta[0] == 0, mine, other), jnp.where(meta[0] == 0, other, mine)
    last_rows[0] = jnp.concatenate(swapped, axis=2)
    save = pltpu.make_async_copy(last_rows, out_h.at[ITERS - 1 : ITERS], sem)
    save.start()
    row = lax.broadcasted_iota(jnp.int32, sub.shape, 0)
    col = lax.broadcasted_iota(jnp.int32, sub.shape, 1)
    out = jnp.zeros(sub.shape, F32)
    for i, j, ref, at in ((0, 0, first, 0), (0, 1, first, 1), (0, 2, known, 2),
                          (1, 0, known, 0), (1, 1, known, 1), (1, 2, known, 3)):
        out = jnp.where((row == i) & (col == j), ref[at : at + 1, 0:1], out)
    for j in range(ITERS):
        value = sum(ref[j : j + 1, 0:1] for ref in sums)
        out = jnp.where((row == ITERS - 1) & (col == j), value, out)
    sub[...] = out
    save.wait()


def solution(mesh):
    n_env, n_term, n_blk = (mesh.shape[a] for a in ("env", "term", "blk"))

    def on_device(psi, left_env, right_env, pairing, sector_dims, precond):
        return _on_device(n_env, n_term, n_blk, psi, left_env, right_env, pairing, sector_dims, precond)

    placed = (
        P(("parts", "blk"), None, None),
        P(("parts", "term"), "blk", "env", None),
        P(("parts", "term"), "blk", "env", None),
        P(("parts", "term"), "blk"),
        P("parts"),
        P(("parts", "blk"), None, None),
    )
    return jax.shard_map(
        on_device,
        mesh=mesh,
        in_specs=placed,
        out_specs=(P(None, ("parts", "blk"), "term", None), P("parts", None)),
        check_vma=False,
    )


def _xor(axis, n, s):
    return functools.partial(lax.ppermute, axis_name=axis, perm=[(i, i ^ s) for i in range(n)])


def _on_device(n_env, n_term, n_blk, psi, left_env, right_env, pairing, sector_dims, precond):
    sec, states, width = psi.shape
    terms = left_env.shape[0]
    n_sec = sec * n_blk
    half = right_env.shape[2]
    direct = n_env == 2 and n_blk == 2 and n_term in (2, 4)
    part, chunk = half // n_term, states // n_term
    cfg = dict(direct=direct, n_term=n_term, n_blk=n_blk, sec=sec, part=part)
    env_pos, term_pos, blk_pos = (lax.axis_index(a) for a in ("env", "term", "blk"))
    other_env = _xor("env", 2, 1)
    other_blk = _xor("blk", 2, 1)
    flat = jnp.stack([x.astype(jnp.int32) for x in (env_pos, term_pos, blk_pos)])
    meta = jnp.concatenate([flat, pairing.reshape(-1), sector_dims.reshape(-1)])
    cfg["pair_at"] = 3
    cfg["dims_at"] = 3 + terms * sec
    chunks = [(0, sec)]
    if direct:
        near = [left_env]
        far = [other_env(left_env[:, k0 : k0 + nk]) for k0, nk in chunks]
        psi_o, pre_o = other_blk(psi), other_blk(precond)
    else:
        near = []
        far = [lax.all_gather(left_env, "env", axis=2, tiled=True)]
        psi_o, pre_o = (
            lax.dynamic_slice_in_dim(
                jnp.concatenate([lax.all_gather(x, "blk", axis=0, tiled=True)] * 2, axis=0),
                (blk_pos + 1) * sec,
                sec * (n_blk - 1),
                0,
            )
            for x in (psi, precond)
        )
    n_near = len(near)

    full = (n_sec, states, width)
    params = pltpu.CompilerParams(vmem_limit_bytes=VMEM_LIMIT)
    start, pret, inner, scale0 = pl.pallas_call(
        functools.partial(_first_kernel, cfg),
        out_shape=(VM(full, BF16), VM(full, F32), VM((terms, sec, half, states), BF16), VM((8, 128), F32)),
        in_specs=_specs(SM, VM, VM, VM, VM, VM),
        out_specs=_specs(VM, VM, VM, VM),
        scratch_shapes=[pltpu.VMEM(full, BF16)],
        compiler_params=params,
        name="start_vector",
    )(meta, psi, psi_o, precond, pre_o, right_env)

    def piece_shapes(nk):
        if direct:
            return [VM((nk, part, width), F32)] + [VM((nk, part, width), BF16)] * (n_term - 1)
        return [VM((nk, half, width), F32)]

    live_own = lax.dynamic_slice_in_dim(sector_dims, blk_pos * sec, sec)

    def reduce(pieces, k0=0):
        if not direct:
            flat_sum = pieces[0].reshape(sec * half, width)
            return lax.psum_scatter(flat_sum, "term", scatter_dimension=0, tiled=True)
        got = [_xor("term", n_term, s)(pieces[s]) for s in range(1, n_term)]
        total = pieces[0]
        for g in got:
            total = total + g.astype(F32)
        live = live_own[k0 : k0 + total.shape[0], None, None]
        row = env_pos * half + term_pos * part + lax.broadcasted_iota(jnp.int32, total.shape, 1)
        col = lax.broadcasted_iota(jnp.int32, total.shape, 2)
        return jnp.where((row < live) & (col < live), total, 0.0).astype(BF16)[None]

    def gather(shard, k0=0):
        if direct:
            hops = range(n_term)
            along = [shard] + [_xor("term", n_term, s)(shard) for s in hops[1:]]
            across = [other_env(a) for a in along]
            here = along + across
            there = [other_blk(a) for a in here]
            places = [(b, e, [s], k0) for b in range(2) for e in range(2) for s in hops]
            return here + there, places
        whole = lax.all_gather(shard, "term", axis=0, tiled=True).reshape(sec, half, width)
        whole = lax.all_gather(whole, "env", axis=1, tiled=True)
        row = lax.broadcasted_iota(jnp.int32, whole.shape, 1)
        col = lax.broadcasted_iota(jnp.int32, whole.shape, 2)
        live = live_own[:, None, None]
        whole = jnp.where((row < live) & (col < live), whole, 0.0).astype(BF16)
        return [lax.all_gather(whole, "blk", axis=0, tiled=True)], [None]

    shards, places = [], []
    for (k0, nk), moved in zip(chunks, far):
        pieces = pl.pallas_call(
            functools.partial(_second_kernel, cfg, k0, n_near + 1),
            out_shape=tuple(piece_shapes(nk)),
            in_specs=_specs(SM, VM, *[VM] * n_near, HB),
            out_specs=tuple(_specs(*[VM] * len(piece_shapes(nk)))),
            scratch_shapes=[
                pltpu.VMEM(moved.shape, BF16),
                pltpu.VMEM((nk, half, width), F32),
                pltpu.SemaphoreType.DMA,
            ],
            compiler_params=params,
            name=f"first_sigma_{k0}",
        )(meta, *_vmem(inner, *near), *_hbm(moved))
        more, at = gather(reduce(pieces, k0), k0)
        shards, places = shards + more, places + at

    vecs, olds = [], []
    far_shape = (terms, sec, *far[0].shape[2:])
    for step in range(1, ITERS):
        last = step + 1 == ITERS
        if step > 1:
            shards, places = gather(reduce(pieces))
        if last:
            if direct:
                size = (sec * chunk + TAIL_ROWS, half)
                outs = [VM((8, 128), F32), VM(size, F32)] + [VM(size, BF16)] * (n_term - 1)
            else:
                outs = [VM((8, 128), F32), VM((sec, states, half), F32), VM((8, 128), F32)]
            made = (HB(full, BF16),)
        else:
            outs = piece_shapes(sec)
            made = (HB(full, BF16), VM(full, F32), VM((8, 128), F32))
        n_fixed = 2 + (step - 1) + 1
        n_moved = (step - 1) + 1 + n_near + len(chunks)
        results = pl.pallas_call(
            functools.partial(_step_kernel, dict(cfg, n_out=len(outs)), step, places, chunks, n_near, last),
            out_shape=(*made, *outs),
            in_specs=_specs(SM, *[VM] * (len(shards) + n_fixed), *[HB] * n_moved),
            out_specs=tuple(_specs(HB, *[VM] * (len(made) - 1 + len(outs)))),
            scratch_shapes=[pltpu.VMEM(full, F32), pltpu.VMEM((sec, states, half), F32)] * last
            + [pltpu.VMEM(full, BF16)] * (step - 1)
            + [
                pltpu.VMEM(right_env.shape, BF16),
                *[pltpu.VMEM(x.shape, BF16) for x in near],
                pltpu.VMEM(far_shape, BF16),
                pltpu.VMEM(full, BF16),
                pltpu.VMEM(full, BF16),
                pltpu.VMEM((sec, half, width), F32),
                pltpu.SemaphoreType.DMA((n_moved + 1,)),
            ],
            compiler_params=params,
            name=f"vector_and_sigma_{step}",
        )(
            meta,
            *_vmem(*shards, start, scale0, *vecs, pret),
            *_hbm(*olds, right_env, *near, *far),
        )
        olds.append(results[0])
        if last:
            known, pieces = results[1], results[2:]
        else:
            vecs.append(results[1])
            first = results[2]
            pieces = results[3:]

    out_shape = (ITERS, sec, chunk, states)
    held = None
    if direct:
        held = pl.pallas_call(
            functools.partial(_rows_kernel, cfg),
            out_shape=HB(out_shape, F32),
            in_specs=_specs(SM, HB, HB),
            out_specs=_specs(HB)[0],
            scratch_shapes=[
                pltpu.VMEM((ITERS - 1, sec, states, states), BF16),
                pltpu.VMEM((ITERS - 1, sec, states, states), F32),
                pltpu.VMEM((ITERS - 1, sec, chunk, states), F32),
                pltpu.SemaphoreType.DMA((3,)),
            ],
            compiler_params=params,
            cost_estimate=pl.CostEstimate(flops=1 << 20, bytes_accessed=1 << 22, transcendentals=0),
            name="first_rows",
        )(meta, *_hbm(*olds))
    live = live_own[:, None, None]
    if direct:
        total = pieces[0]
        for s in range(1, n_term):
            total = total + _xor("term", n_term, s)(pieces[s]).astype(F32)
        cut = total[sec * chunk : sec * chunk + 3 * ITERS, :]
        sent = cut.reshape(ITERS, 3, half).sum(axis=1)
        mine = total[: sec * chunk].reshape(sec, chunk, half)
        row = term_pos * chunk + lax.broadcasted_iota(jnp.int32, mine.shape, 1)
        col = env_pos * half + lax.broadcasted_iota(jnp.int32, mine.shape, 2)
        own = jnp.where((row < live) & (col < live), mine, 0.0)
        theirs = other_env(own.astype(BF16))
        corners = [(i, i ^ 3) for i in range(4)]
        sums = [sent, other_blk(sent), other_env(sent), lax.ppermute(sent, ("env", "blk"), corners)]
        return pl.pallas_call(
            lambda meta, first, known, a, b, c, d, *refs: _final_kernel(cfg, meta, first, known, (a, b, c, d), *refs),
            out_shape=(HB(out_shape, F32), jax.ShapeDtypeStruct((ITERS, ITERS), F32)),
            in_specs=_specs(SM, *[VM] * 8, HB),
            out_specs=tuple(_specs(HB, VM)),
            scratch_shapes=[pltpu.VMEM((1, sec, chunk, states), F32), pltpu.SemaphoreType.DMA],
            input_output_aliases={9: 0},
            compiler_params=params,
            name="last_rows",
        )(meta, *_vmem(first, known, *sums, own, theirs), *_hbm(held))
    own = lax.psum_scatter(pieces[0], "term", scatter_dimension=1, tiled=True)
    both = lax.all_gather(own, "env", axis=2, tiled=True)
    row = term_pos * chunk + lax.broadcasted_iota(jnp.int32, both.shape, 1)
    col = lax.broadcasted_iota(jnp.int32, both.shape, 2)
    both = jnp.where((row < live) & (col < live), both, 0.0)
    scal = lax.psum(pieces[1], ("term", "env", "blk"))[:ITERS, 0]
    rows_out = []
    for sig in olds:
        mine = lax.dynamic_slice(sig, (blk_pos * sec, 0, term_pos * chunk), (sec, states, chunk))
        rows_out.append(jnp.swapaxes(mine, 1, 2).astype(F32))
    rows_out.append(both)
    first, second = first[:, 0], known[:, 0]
    subspace = jnp.stack([
        jnp.stack([first[0], first[1], second[2]]),
        jnp.stack([second[0], second[1], second[3]]),
        scal,
    ])
    return jnp.stack(rows_out), subspace
```

```python
import functools

import jax
import jax.numpy as jnp
from jax import lax
from jax.experimental import pallas as pl
from jax.experimental.pallas import tpu as pltpu
from jax.sharding import PartitionSpec as P

ITERS = 3
EPS = 1e-06
F32, BF16 = jnp.float32, jnp.bfloat16
ROWS = 64
TAIL_ROWS = 16
SPLIT = 4
VMEM_LIMIT = 32 * 1024 * 1024
HB, VM, SM = pltpu.HBM, pltpu.VMEM, pltpu.SMEM


def _specs(*shapes):
    return [pl.BlockSpec(memory_space=s) for s in shapes]


def _hbm(*arrays):
    return [pltpu.with_memory_space_constraint(x, HB) for x in arrays]


def _vmem(*arrays):
    return [pltpu.with_memory_space_constraint(x, VM) for x in arrays]


def _fold(x):
    return jnp.sum(x.reshape(x.shape[0] // 8, 8, x.shape[1]), axis=0)


def _over(n_sec, states, width, n_acc, body):
    blocks = states // ROWS

    def step(i, accs):
        for b in range(blocks):
            accs = tuple(x + y for x, y in zip(accs, body(i, slice(b * ROWS, (b + 1) * ROWS))))
        return accs

    zero = tuple(jnp.zeros((8, width), F32) for _ in range(n_acc))
    return tuple(jnp.sum(a) for a in lax.fori_loop(0, n_sec, step, zero))


def _low(cfg, value, env_pos):
    low = value.astype(BF16)
    if cfg["direct"]:
        half = value.shape[1] // 2
        turned = jnp.concatenate([value[:, half:], value[:, :half]], axis=1).astype(BF16)
        low = jnp.where(env_pos == 0, low, turned)
    return low


def _put_scalars(ref, values):
    shape = ref.shape
    row = lax.broadcasted_iota(jnp.int32, shape, 0)
    out = jnp.zeros(shape, F32)
    for index, value in enumerate(values):
        out = jnp.where(row == index, value, out)
    ref[...] = out


def _first_kernel(cfg, meta, psi, psi_o, pre, pre_o, right_h, start, pret_h, inner, scale_ref, vb, right, pret, sem):
    sec, states, width = psi.shape
    n_sec = sec * cfg["n_blk"]
    blk, env_pos = meta[2], meta[0]
    base = blk * sec
    load = pltpu.make_async_copy(_group(cfg, meta, right_h), right, sem.at[0])
    load.start()
    for part, (p_ref, c_ref) in enumerate(((psi, pre), (psi_o, pre_o))):
        for k in range(p_ref.shape[0]):
            at = lax.rem(base + part * sec + k, n_sec)
            live = meta[cfg["dims_at"] + at]
            row = lax.broadcasted_iota(jnp.int32, (states, width), 0)
            col = lax.broadcasted_iota(jnp.int32, (states, width), 1)
            value = jnp.where((row < live) & (col < live), p_ref[k].astype(F32).T, 0.0)
            start[at] = value.astype(BF16)
            pret[at] = c_ref[k].T
    save = pltpu.make_async_copy(pret, pret_h, sem.at[1])
    save.start()

    def square(s, r):
        value = start[s, r, :].astype(F32)
        return (_fold(value * value),)

    (total,) = _over(n_sec, states, width, 1, square)
    scale = lax.rsqrt(total / (n_sec * states * width) + EPS)
    _put_scalars(scale_ref, [scale] * 8)

    def make(s, r):
        vb[s, r, :] = _low(cfg, start[s, r, :].astype(F32) * scale, env_pos)
        return ()

    _over(n_sec, states, width, 0, make)
    load.wait()
    terms, held = right.shape[:2]
    for k in range(held):
        for t in range(terms):
            chosen = vb[meta[cfg["pair_at"] + t * held + k]]
            inner[t, k] = jnp.dot(right[t, k], chosen, preferred_element_type=F32).astype(BF16)
    save.wait()


def _group(cfg, meta, ref):
    return ref.at[:, pl.ds(meta[3] * cfg["held"], cfg["held"])]


def _env_moves(cfg, meta, places, refs, right, left, sem, first=0):
    moves = []
    for ref, (kind, t0, r0, own) in zip(refs, places):
        src = _group(cfg, meta, ref) if own else ref
        step = ref.shape[0] // SPLIT
        for i in range(SPLIT):
            t = pl.ds(t0 + i * step, step)
            dst = right.at[t] if kind == "right" else left.at[t, :, pl.ds(r0, ref.shape[2]), :]
            moves.append(pltpu.make_async_copy(src.at[pl.ds(i * step, step)], dst, sem.at[first + len(moves)]))
            moves[-1].start()
    return moves


def _own_sigma_kernel(cfg, places, meta, inner, *refs):
    lefts, acc, left, sem = refs[: len(places)], refs[-3], refs[-2], refs[-1]
    for c in _env_moves(cfg, meta, places, lefts, None, left, sem):
        c.wait()
    for k in range(inner.shape[1]):
        total = None
        for t in range(inner.shape[0]):
            got = jnp.dot(inner[t, k], left[t, k], preferred_element_type=F32)
            total = got if total is None else total + got
        acc[k] = total


def _far_sigma_kernel(cfg, places, t0, meta, vb, acc, *refs):
    envs, out, right, left, sem = refs[: len(places)], refs[-4], refs[-3], refs[-2], refs[-1]
    terms, held = right.shape[:2]
    moves = _env_moves(cfg, meta, places, envs, right, left, sem)
    for c in moves[:SPLIT]:
        c.wait()
    inner = []
    for k in range(held):
        for t in range(terms):
            chosen = vb[meta[cfg["pair_at"] + (t0 + t) * held + k]]
            inner.append(jnp.dot(right[t, k], chosen, preferred_element_type=F32).astype(BF16))
    for c in moves[SPLIT:]:
        c.wait()
    for k in range(held):
        total = acc[k]
        for t in range(terms):
            total = total + jnp.dot(inner[k * terms + t], left[t, k], preferred_element_type=F32)
        out[k] = total.astype(out.dtype)


def _step_kernel(cfg, step, places, env_places, last, meta, *refs):
    it = iter(refs)
    take = lambda n: [next(it) for _ in range(n)]
    shards = take(len(places))
    (start, scale_ref), vecs, (pre_h,) = take(2), take(step - 1), take(1)
    olds_h, envs_h, (sig_h,) = take(step - 1), take(len(env_places)), take(1)
    vnew, dots = (None, None) if last else take(2)
    outs = take(cfg["n_out"])
    if last:
        vnew, turned = take(2)
    olds = take(step - 1)
    right, left, pre, sig, vb, acc, sem = take(7)
    env_pos, z, blk, mine_at = meta[0], meta[1], meta[2], meta[3]
    n_sec, states, width = vnew.shape
    sec, held_sec, half = cfg["sec"], cfg["held"], right.shape[2]
    count = n_sec * states * width
    n_held = sec // held_sec

    def sector(b, h, k):
        if not cfg["direct"]:
            return b * sec + k
        return (blk ^ b) * sec + (mine_at ^ h) * held_sec + k

    order = [(b, h, k) for b in range(cfg["n_blk"]) for h in range(n_held) for k in range(held_sec)]
    pre_moves = [pltpu.make_async_copy(pre_h.at[sector(*o)], pre.at[sector(*o)], sem.at[i]) for i, o in enumerate(order)]
    old_moves = [pltpu.make_async_copy(a, b, sem.at[n_sec + i]) for i, (a, b) in enumerate(zip(olds_h, olds))]
    for c in pre_moves + old_moves:
        c.start()
    env_moves = _env_moves(cfg, meta, env_places, envs_h, right, left, sem, n_sec + step)
    save = pltpu.make_async_copy(sig, sig_h, sem.at[n_sec + step - 1])
    scale0 = scale_ref[0, 0]
    basis = [lambda s, r: start[s, r, :].astype(F32) * scale0]
    basis += [lambda s, r, v=v: v[s, r, :] for v in vecs]

    pairs = [(j, l) for j in range(step) for l in range(j, step)]
    accs = [jnp.zeros((8, width), F32) for _ in range(2 * step + len(pairs))]
    blocks = {o: [] for o in order}
    for ref, place in zip(shards, places):
        if place is None:
            for b, h, k in order:
                for r in range(0, states, ROWS):
                    at = b * sec + k
                    blocks[b, h, k].append((ref, at, slice(r, r + ROWS), at, slice(r, r + ROWS)))
            continue
        b, e, h = place
        for k in range(held_sec):
            for r in range(0, half, ROWS):
                rows = pl.ds(pl.multiple_of((env_pos ^ e) * half + r, ROWS), ROWS)
                blocks[b, h, k].append((ref, k, slice(r, r + ROWS), sector(b, h, k), rows))
    for ready, o in zip(pre_moves, order):
        ready.wait()
        for ref, k, r, s, rows in blocks[o]:
            low = ref[k, r, :]
            sig[s, rows, :] = low
            value, cond = low.astype(F32), pre[s, rows, :]
            scaled = value * cond
            held = [b(s, rows) for b in basis]
            found = [_fold(h * value) for h in held] + [_fold(h * scaled) for h in held]
            condh = [h * cond for h in held]
            found += [_fold(condh[j] * held[l]) for j, l in pairs]
            accs = [a + t for a, t in zip(accs, found)]
    save.start()
    sums = [jnp.sum(a) / count for a in accs]
    proj = sums[:step]
    gram = {}
    for (j, l), value in zip(pairs, sums[2 * step :]):
        gram[j, l] = gram[l, j] = value
    back = [sums[step + j] - sum(proj[l] * gram[j, l] for l in range(step)) for j in range(step)]

    over = functools.partial(_over, n_sec, states, width)
    for c in old_moves:
        c.wait()

    def trial_pass(s, r):
        value = sig[s, r, :].astype(F32)
        held = [b(s, r) for b in basis]
        trial = value
        for h, b in zip(proj, held):
            trial = trial - h * b
        trial = trial * pre[s, r, :]
        for g, b in zip(back, held):
            trial = trial - g * b
        vnew[s, r, :] = trial
        crossed = [o[s, r, :].astype(F32) for o in olds] + [value]
        return (_fold(trial * trial), *[_fold(trial * o) for o in crossed])

    square, *cross = over(1 + step, trial_pass)
    scale = lax.rsqrt(square / count + EPS)
    cross = [x * scale / count for x in cross]

    def final_pass(s, r):
        value = vnew[s, r, :] * scale
        vnew[s, r, :] = value
        vb[s, r, :] = _low(cfg, value, env_pos)
        return ()

    over(0, final_pass)
    for c in env_moves:
        c.wait()
    for k in range(held_sec):
        total = None
        for t in range(right.shape[0]):
            chosen = vb[meta[cfg["pair_at"] + t * held_sec + k]]
            inner = jnp.dot(right[t, k], chosen, preferred_element_type=F32).astype(BF16)
            got = jnp.dot(inner, left[t, k], preferred_element_type=F32)
            total = got if total is None else total + got
        acc[k] = total
    scalars = proj + cross
    if not last:
        outs[0][...] = acc[...].astype(outs[0].dtype)
        _put_scalars(dots, scalars)
        save.wait()
        return

    rows = pl.ds(pl.multiple_of(env_pos * half, half), half)
    mine = []
    for b in [*basis, lambda s, r: vnew[s, r, :]]:
        total = jnp.zeros((8, width), F32)
        for k in range(held_sec):
            total = total + _fold(b(sector(0, 0, k) if cfg["direct"] else blk * sec + k, rows) * acc[k])
        mine.append(jnp.sum(total) / count)
    _put_scalars(outs[0], scalars)
    if cfg["direct"]:
        for k in range(held_sec):
            turned[k] = acc[k].T
        span = states // 2
        side = lax.div(z, 2)
        tail = _addends(mine, half)
        for out, at in ((outs[1], side), (outs[2], 1 - side)):
            for k in range(held_sec):
                rows = pl.ds(pl.multiple_of(at * span, span), span)
                out[k * span : (k + 1) * span, :] = turned[k, rows, :].astype(out.dtype)
            out[held_sec * span :, :] = tail.astype(out.dtype)
    else:
        _put_scalars(outs[1], mine)
        for k in range(held_sec):
            outs[2][k] = acc[k].T
    save.wait()


def _addends(values, width):
    row = lax.broadcasted_iota(jnp.int32, (TAIL_ROWS, width), 0)
    tail = jnp.zeros((TAIL_ROWS, width), F32)
    for j, value in enumerate(values):
        rest = jnp.broadcast_to(value, (TAIL_ROWS, width))
        for p in range(3):
            cut = rest.astype(BF16).astype(F32)
            tail = jnp.where(row == 3 * j + p, cut, tail)
            rest = rest - cut
    return tail


def _added(*tails):
    return [
        sum(tail[3 * j + p : 3 * j + p + 1, 0:1].astype(F32) for tail in tails for p in range(3)) for j in range(ITERS)
    ]


def _rows_kernel(cfg, meta, sig_a, sig_b, out_h, sig, turned, rows, sem):
    chunk = rows.shape[2]
    first = pl.ds(pl.multiple_of(meta[1] * chunk, chunk), chunk)
    own = pl.ds(meta[2] * cfg["sec"], cfg["sec"])
    loads = [pltpu.make_async_copy(ref.at[own], sig.at[i], sem.at[i]) for i, ref in enumerate((sig_a, sig_b))]
    for c in loads:
        c.start()
    for i, c in enumerate(loads):
        c.wait()
        for k in range(rows.shape[1]):
            turned[i, k] = sig[i, k].astype(F32).T
            rows[i, k] = turned[i, k, first, :]
    save = pltpu.make_async_copy(rows, out_h.at[0 : rows.shape[0]], sem.at[2])
    save.start()
    save.wait()


def _merge_kernel(cfg, meta, kept, got, own, keep_out, give_out):
    held, chunk, half = own.shape
    span = 2 * chunk
    z = meta[1]
    at_tail = slice(held * span, held * span + TAIL_ROWS)
    tail = _addends(_added(kept[at_tail, :], got[at_tail, :]), half)
    side = lax.rem(z, 2)
    for which, out in ((side, keep_out), (1 - side, give_out)):
        first = pl.multiple_of(which * chunk, chunk)
        for k in range(held):
            rows = pl.ds(pl.multiple_of(k * span + first, chunk), chunk)
            live = meta[cfg["dims_at"] + meta[2] * cfg["sec"] + meta[3] * held + k]
            at_row = lax.div(z, 2) * span + first + lax.broadcasted_iota(jnp.int32, (chunk, half), 0)
            at_col = meta[0] * half + lax.broadcasted_iota(jnp.int32, (chunk, half), 1)
            value = kept[rows, :] + got[rows, :].astype(F32)
            value = jnp.where((at_row < live) & (at_col < live), value, 0.0)
            out[k * chunk : (k + 1) * chunk, :] = value.astype(BF16)
            if out is keep_out:
                own[k] = value
        out[held * chunk :, :] = tail.astype(BF16)


def _final_kernel(cfg, meta, own, by_env, by_term, by_both, held_h, out_h, rows, sem):
    del held_h
    held, chunk, half = own.shape
    for k in range(held):
        at = slice(k * chunk, (k + 1) * chunk)
        pairs = (own[k], by_env[at, :].astype(F32)), (by_term[at, :].astype(F32), by_both[at, :].astype(F32))
        for h, (mine, other) in enumerate(pairs):
            both = jnp.where(meta[0] == 0, mine, other), jnp.where(meta[0] == 0, other, mine)
            rows[0, (meta[3] ^ h) * held + k] = jnp.concatenate(both, axis=1)
    save = pltpu.make_async_copy(rows, out_h.at[ITERS - 1 : ITERS], sem)
    save.start()
    save.wait()


def _dots_kernel(at, own, by_env, by_term, by_both, out):
    found = _added(*(ref[at : at + TAIL_ROWS, :] for ref in (own, by_env, by_term, by_both)))
    _put_scalars(out, found)


def _subspace_kernel(first, known, dots, other, sub):
    row = lax.broadcasted_iota(jnp.int32, sub.shape, 0)
    col = lax.broadcasted_iota(jnp.int32, sub.shape, 1)
    out = jnp.zeros(sub.shape, F32)
    for i, j, ref, at in ((0, 0, first, 0), (0, 1, first, 1), (0, 2, known, 2),
                          (1, 0, known, 0), (1, 1, known, 1), (1, 2, known, 3)):
        out = jnp.where((row == i) & (col == j), ref[at : at + 1, 0:1], out)
    for j in range(ITERS):
        value = dots[j : j + 1, 0:1] + other[j : j + 1, 0:1]
        out = jnp.where((row == ITERS - 1) & (col == j), value, out)
    sub[...] = out


def solution(mesh):
    n_env, n_term, n_blk = (mesh.shape[a] for a in ("env", "term", "blk"))

    def on_device(psi, left_env, right_env, pairing, sector_dims, precond):
        return _on_device(n_env, n_term, n_blk, psi, left_env, right_env, pairing, sector_dims, precond)

    placed = (
        P(("parts", "blk"), None, None),
        P(("parts", "term"), "blk", "env", None),
        P(("parts", "term"), "blk", "env", None),
        P(("parts", "term"), "blk"),
        P("parts"),
        P(("parts", "blk"), None, None),
    )
    return jax.shard_map(
        on_device,
        mesh=mesh,
        in_specs=placed,
        out_specs=(P(None, ("parts", "blk"), "term", None), P("parts", None)),
        check_vma=False,
    )


def _xor(axis, n, s):
    return functools.partial(lax.ppermute, axis_name=axis, perm=[(i, i ^ s) for i in range(n)])


def _cut_kernel(held, which, env_h, *refs):
    count = (len(refs) - 1) // 2
    outs, bufs, sem = refs[:count], refs[count:-1], refs[-1]
    loads, saves = [], []
    for i, (out, buf) in enumerate(zip(outs, bufs)):
        at = (1 - which[0] if i == 0 else which[0]) * held
        loads.append(pltpu.make_async_copy(env_h.at[:, pl.ds(at, held)], buf, sem.at[0, i]))
        saves.append(pltpu.make_async_copy(buf, out, sem.at[1, i]))
        loads[-1].start()
    for load, save in zip(loads, saves):
        load.wait()
        save.start()
    for save in saves:
        save.wait()


def _cut(env, mine, held, count):
    shape = (env.shape[0], held, *env.shape[2:])
    return pl.pallas_call(
        functools.partial(_cut_kernel, held),
        out_shape=tuple(HB(shape, BF16) for _ in range(count)),
        in_specs=_specs(SM, HB),
        out_specs=tuple(_specs(*[HB] * count)),
        scratch_shapes=[pltpu.VMEM(shape, BF16) for _ in range(count)] + [pltpu.SemaphoreType.DMA((2, count))],
        compiler_params=pltpu.CompilerParams(vmem_limit_bytes=VMEM_LIMIT),
        name="sectors_to_send",
    )(mine.astype(jnp.int32).reshape(1), *_hbm(env))


def _on_device(n_env, n_term, n_blk, psi, left_env, right_env, pairing, sector_dims, precond):
    sec, states, width = psi.shape
    terms = left_env.shape[0]
    n_sec = sec * n_blk
    half = right_env.shape[2]
    direct = n_env == 2 and n_blk == 2 and n_term == 4 and sec % 2 == 0 and terms % 2 == 0
    chunk = states // n_term
    held = sec // 2 if direct else sec
    cfg = dict(direct=direct, n_blk=n_blk, sec=sec, held=held)
    env_pos, term_pos, blk_pos = (lax.axis_index(a) for a in ("env", "term", "blk"))
    mine = (term_pos ^ (term_pos >> 1)) & 1 if direct else jnp.zeros_like(term_pos)
    next_term, far_term = _xor("term", 4, 1), _xor("term", 4, 3)
    other_env, other_blk = _xor("env", 2, 1), _xor("blk", 2, 1)
    corners = functools.partial(
        lax.ppermute, axis_name=("term", "env"), perm=[(2 * t + e, 2 * (t ^ 1) + (e ^ 1)) for t in range(4) for e in range(2)]
    )
    group = lambda x, which: lax.dynamic_slice_in_dim(x, which * held, held, 1)

    if direct:
        to_next, to_env = _cut(left_env, mine, held, 2)
        (right_to_next,) = _cut(right_env, mine, held, 1)
        psi_o, pre_o = other_blk(psi), other_blk(precond)
        next_left = next_term(to_next)
        far_left = other_env(to_env)
        next_right = next_term(right_to_next)
        next_far_left = other_env(next_left)
        own_table = group(pairing, mine)
        own_places = [("left", 0, 0, True), ("left", 0, half, False)]
        next_places = [("right", 0, 0, False), ("left", 0, 0, False), ("left", 0, half, False)]
        own_envs, next_envs = [left_env, far_left], [next_right, next_left, next_far_left]
        n_terms = 2 * terms
        shift = lambda place: (place[0], place[1] + terms, *place[2:])
        env_places = [("right", 0, 0, True), *own_places, *map(shift, next_places)]
        envs = [right_env, *own_envs, *next_envs]
    else:
        own_envs = [lax.all_gather(left_env, "env", axis=2, tiled=True)]
        own_places = [("left", 0, 0, False)]
        own_table = pairing
        n_terms = terms
        env_places, envs = [("right", 0, 0, True), *own_places], [right_env, *own_envs]
        psi_o, pre_o = (
            lax.dynamic_slice_in_dim(
                jnp.concatenate([lax.all_gather(x, "blk", axis=0, tiled=True)] * 2, axis=0),
                (blk_pos + 1) * sec,
                sec * (n_blk - 1),
                0,
            )
            for x in (psi, precond)
        )
    flat = jnp.stack([x.astype(jnp.int32) for x in (env_pos, term_pos, blk_pos, mine)])
    own_meta = jnp.concatenate([flat, sector_dims.reshape(-1), own_table.reshape(-1)])
    cfg["dims_at"] = 4
    cfg["pair_at"] = 4 + n_sec

    full = (n_sec, states, width)
    params = pltpu.CompilerParams(vmem_limit_bytes=VMEM_LIMIT)
    dma = pltpu.SemaphoreType.DMA
    start, pret, inner, scale0, vb0 = pl.pallas_call(
        functools.partial(_first_kernel, cfg),
        out_shape=(
            VM(full, BF16),
            HB(full, F32),
            VM((terms, held, half, states), BF16),
            VM((8, 128), F32),
            VM(full, BF16),
        ),
        in_specs=_specs(SM, VM, VM, VM, VM, HB),
        out_specs=_specs(VM, HB, VM, VM, VM),
        scratch_shapes=[pltpu.VMEM((terms, held, half, states), BF16), pltpu.VMEM(full, F32), dma((2,))],
        compiler_params=params,
        name="start_vector",
    )(own_meta, psi, psi_o, precond, pre_o, *_hbm(right_env))

    partial = pl.pallas_call(
        functools.partial(_own_sigma_kernel, cfg, own_places),
        out_shape=VM((held, half, width), F32),
        in_specs=_specs(SM, VM, *[HB] * len(own_envs)),
        out_specs=_specs(VM)[0],
        scratch_shapes=[pltpu.VMEM((terms, held, states, width), BF16), dma((SPLIT * len(own_envs),))],
        compiler_params=params,
        name="first_sigma_own_terms",
    )(own_meta, *_vmem(inner), *_hbm(*own_envs))
    meta = own_meta
    if direct:
        next_pairing = next_term(lax.optimization_barrier((pairing, partial))[0])
        meta = jnp.concatenate([own_meta, group(next_pairing, mine).reshape(-1)])
        partial = pl.pallas_call(
            functools.partial(_far_sigma_kernel, cfg, next_places, terms),
            out_shape=VM((held, half, width), BF16),
            in_specs=_specs(SM, VM, VM, *[HB] * len(next_envs)),
            out_specs=_specs(VM)[0],
            scratch_shapes=[
                pltpu.VMEM((terms, held, half, states), BF16),
                pltpu.VMEM((terms, held, states, width), BF16),
                dma((SPLIT * len(next_envs),)),
            ],
            compiler_params=params,
            name="first_sigma_next_terms",
        )(meta, *_vmem(vb0, partial), *_hbm(*next_envs))

    live_own = lax.dynamic_slice_in_dim(sector_dims, blk_pos * sec, sec)

    def masked(value, row0, live):
        row = row0 + lax.broadcasted_iota(jnp.int32, value.shape, 1)
        col = lax.broadcasted_iota(jnp.int32, value.shape, 2)
        live = live[:, None, None]
        return jnp.where((row < live) & (col < live), value, 0.0).astype(BF16)

    def combine(partial):
        if direct:
            total = partial.astype(F32) + far_term(partial).astype(F32)
            shard = masked(total, env_pos * half, lax.dynamic_slice_in_dim(live_own, mine * held, held))
            here = [shard, next_term(shard), other_env(shard), corners(shard)]
            there = [other_blk(x) for x in here]
            return here + there, [(b, e, h) for b in range(2) for e, h in ((0, 0), (0, 1), (1, 0), (1, 1))]
        flat_sum = lax.psum_scatter(partial.reshape(sec * half, width), "term", scatter_dimension=0, tiled=True)
        whole = lax.all_gather(flat_sum, "term", axis=0, tiled=True).reshape(sec, half, width)
        whole = masked(lax.all_gather(whole, "env", axis=1, tiled=True), 0, live_own)
        return [lax.all_gather(whole, "blk", axis=0, tiled=True)], [None]

    vecs, olds = [], []
    for step in range(1, ITERS):
        last = step + 1 == ITERS
        shards, places = combine(partial)
        if last:
            outs = [VM((8, 128), F32)]
            if direct:
                size = (held * states // 2 + TAIL_ROWS, half)
                outs += [VM(size, F32), VM(size, BF16)]
            else:
                outs += [VM((8, 128), F32), VM((sec, states, half), F32)]
            made = (HB(full, BF16),)
        else:
            outs = [VM((held, half, width), BF16 if direct else F32)]
            made = (HB(full, BF16), VM(full, F32), VM((8, 128), F32))
        n_hbm = 1 + (step - 1) + len(envs)
        results = pl.pallas_call(
            functools.partial(_step_kernel, dict(cfg, n_out=len(outs)), step, places, env_places, last),
            out_shape=(*made, *outs),
            in_specs=_specs(SM, *[VM] * (len(shards) + 2 + len(vecs)), *[HB] * n_hbm),
            out_specs=tuple(_specs(HB, *[VM] * (len(made) - 1 + len(outs)))),
            scratch_shapes=[pltpu.VMEM(full, F32), pltpu.VMEM((held, states, half), F32)] * last
            + [pltpu.VMEM(full, BF16)] * (step - 1)
            + [
                pltpu.VMEM((n_terms, held, half, states), BF16),
                pltpu.VMEM((n_terms, held, states, width), BF16),
                pltpu.VMEM(full, F32),
                pltpu.VMEM(full, BF16),
                pltpu.VMEM(full, BF16),
                pltpu.VMEM((held, half, width), F32),
                dma((n_sec + step + SPLIT * len(envs),)),
            ],
            compiler_params=params,
            name=f"vector_and_sigma_{step}",
        )(
            meta,
            *_vmem(*shards, start, scale0, *vecs),
            *_hbm(pret, *olds, *envs),
        )
        olds.append(results[0])
        if last:
            known, *pieces = results[1:]
        else:
            vecs.append(results[1])
            first, partial = results[2:]

    out_shape = (ITERS, sec, chunk, states)
    if direct:
        rows01 = pl.pallas_call(
            functools.partial(_rows_kernel, cfg),
            out_shape=HB(out_shape, F32),
            in_specs=_specs(SM, HB, HB),
            out_specs=_specs(HB)[0],
            scratch_shapes=[
                pltpu.VMEM((ITERS - 1, sec, states, states), BF16),
                pltpu.VMEM((ITERS - 1, sec, states, states), F32),
                pltpu.VMEM((ITERS - 1, sec, chunk, states), F32),
                dma((3,)),
            ],
            compiler_params=params,
            cost_estimate=pl.CostEstimate(flops=1 << 20, bytes_accessed=1 << 22, transcendentals=0),
            name="first_rows",
        )(meta, *_hbm(*olds))
        kept, given = pieces
        got = far_term(given)
        size = (held * chunk + TAIL_ROWS, half)
        own, keep, give = pl.pallas_call(
            functools.partial(_merge_kernel, cfg),
            out_shape=(VM((held, chunk, half), F32), VM(size, BF16), VM(size, BF16)),
            in_specs=_specs(SM, VM, VM),
            out_specs=tuple(_specs(VM, VM, VM)),
            compiler_params=params,
            name="last_sums",
        )(meta, *_vmem(lax.optimization_barrier((kept, rows01))[0], got))
        parts = [other_env(keep), next_term(give), corners(give)]
        dots = pl.pallas_call(
            functools.partial(_dots_kernel, held * chunk),
            out_shape=VM((8, 128), F32),
            in_specs=_specs(*[VM] * 4),
            out_specs=_specs(VM)[0],
            compiler_params=params,
            name="last_dots",
        )(*_vmem(keep, *parts))
        other_dots = other_blk(dots)
        sigmas = pl.pallas_call(
            functools.partial(_final_kernel, cfg),
            out_shape=HB(out_shape, F32),
            in_specs=_specs(SM, *[VM] * 4, HB),
            out_specs=_specs(HB)[0],
            scratch_shapes=[pltpu.VMEM((1, sec, chunk, states), F32), dma],
            input_output_aliases={5: 0},
            compiler_params=params,
            name="last_rows",
        )(meta, *_vmem(own, *parts), *_hbm(rows01))
        subspace = pl.pallas_call(
            _subspace_kernel,
            out_shape=jax.ShapeDtypeStruct((ITERS, ITERS), F32),
            in_specs=_specs(*[VM] * 4),
            out_specs=_specs(VM)[0],
            compiler_params=params,
            name="subspace",
        )(*_vmem(first, known, dots, other_dots))
        return sigmas, subspace
    dots = pieces.pop(0)
    own = lax.psum_scatter(pieces[0], "term", scatter_dimension=1, tiled=True)
    both = lax.all_gather(own, "env", axis=2, tiled=True)
    row = term_pos * chunk + lax.broadcasted_iota(jnp.int32, both.shape, 1)
    col = lax.broadcasted_iota(jnp.int32, both.shape, 2)
    live = live_own[:, None, None]
    both = jnp.where((row < live) & (col < live), both, 0.0)
    rows_out = []
    for sig in olds:
        part = lax.dynamic_slice(sig, (blk_pos * sec, 0, term_pos * chunk), (sec, states, chunk))
        rows_out.append(jnp.swapaxes(part, 1, 2).astype(F32))
    rows_out.append(both)
    scal = lax.psum(dots, ("term", "env", "blk"))[:ITERS, 0]
    first, second = first[:, 0], known[:, 0]
    subspace = jnp.stack([
        jnp.stack([first[0], first[1], second[2]]),
        jnp.stack([second[0], second[1], second[3]]),
        scal,
    ])
    return jnp.stack(rows_out), subspace
```

```python
import functools

import jax
import jax.numpy as jnp
from jax import lax
from jax.experimental import pallas as pl
from jax.experimental.pallas import tpu as pltpu
from jax.sharding import PartitionSpec as P

ITERS = 3
EPS = 1e-06
F32, BF16 = jnp.float32, jnp.bfloat16
ROWS = 64
TAIL_ROWS = 16
SPAN = 8
VMEM_LIMIT = 16 * 1024 * 1024
HB, VM, SM = pltpu.HBM, pltpu.VMEM, pltpu.SMEM


def _specs(*shapes):
    return [pl.BlockSpec(memory_space=s) for s in shapes]


def _hbm(*arrays):
    return [pltpu.with_memory_space_constraint(x, HB) for x in arrays]


def _vmem(*arrays):
    return [pltpu.with_memory_space_constraint(x, VM) for x in arrays]


def _fold(x):
    return jnp.sum(x.reshape(x.shape[0] // 8, 8, x.shape[1]), axis=0)


def _over(n_sec, states, width, n_acc, body):
    blocks = states // ROWS

    def step(i, accs):
        for b in range(blocks):
            accs = tuple(x + y for x, y in zip(accs, body(i, slice(b * ROWS, (b + 1) * ROWS))))
        return accs

    zero = tuple(jnp.zeros((8, width), F32) for _ in range(n_acc))
    return tuple(jnp.sum(a) for a in lax.fori_loop(0, n_sec, step, zero))


def _put_scalars(ref, values):
    shape = ref.shape
    row = lax.broadcasted_iota(jnp.int32, shape, 0)
    out = jnp.zeros(shape, F32)
    for index, value in enumerate(values):
        out = jnp.where(row == index, value, out)
    ref[...] = out


def _first_kernel(cfg, places, meta, psi, psi_o, pre, pre_o, *refs):
    envs, (start, pret, scale_ref, vb_h, acc, vb, right, left, sem) = refs[: len(places)], refs[len(places) :]
    sec, states, width = psi.shape
    n_sec = sec * cfg["n_blk"]
    base = meta[2] * sec
    moves = _env_moves(cfg, meta, places, envs, right, left, sem)
    for part, (p_ref, c_ref) in enumerate(((psi, pre), (psi_o, pre_o))):
        for k in range(p_ref.shape[0]):
            at = lax.rem(base + part * sec + k, n_sec)
            live = meta[cfg["dims_at"] + at]
            row = lax.broadcasted_iota(jnp.int32, (states, width), 0)
            col = lax.broadcasted_iota(jnp.int32, (states, width), 1)
            value = jnp.where((row < live) & (col < live), p_ref[k].astype(F32).T, 0.0)
            start[at] = value.astype(BF16)
            pret[at] = c_ref[k].T
    def square(s, r):
        value = start[s, r, :].astype(F32)
        return (_fold(value * value),)

    (total,) = _over(n_sec, states, width, 1, square)
    scale = lax.rsqrt(total / (n_sec * states * width) + EPS)
    count = n_sec * states * width

    def cond(s, r):
        value = start[s, r, :].astype(F32)
        return (_fold(value * value * pret[s, r, :]),)

    (damped,) = _over(n_sec, states, width, 1, cond)
    _put_scalars(scale_ref, [scale, damped * scale * scale / count])

    def make(s, r):
        vb[s, r, :] = (start[s, r, :].astype(F32) * scale).astype(BF16)
        return ()

    _over(n_sec, states, width, 0, make)
    save = pltpu.make_async_copy(vb, vb_h, sem.at[len(moves)])
    save.start()
    for _, c in moves:
        c.wait()
    for k in range(acc.shape[0]):
        total = None
        for t in range(right.shape[0]):
            chosen = vb[meta[cfg["pair_at"] + t * acc.shape[0] + k]]
            inner = jnp.dot(right[t, k], chosen, preferred_element_type=F32).astype(BF16)
            got = jnp.dot(inner, left[t, k], preferred_element_type=F32)
            total = got if total is None else total + got
        acc[k] = total
    save.wait()


def _group(cfg, meta, ref):
    return ref.at[:, pl.ds(meta[3] * cfg["held"], cfg["held"])]


def _env_moves(cfg, meta, places, refs, right, left, sem, first=0):
    moves = []
    for ref, (kind, t0, far, own) in zip(refs, places):
        src = _group(cfg, meta, ref) if own else ref
        step = cfg["span"]
        for i in range(0, ref.shape[0], step):
            t = pl.ds(t0 + i, step)
            side = meta[0] ^ far if cfg["direct"] else 0
            rows = pl.ds(pl.multiple_of(side * ref.shape[2], ref.shape[2]), ref.shape[2])
            dst = right.at[t] if kind == "right" else left.at[t, :, rows, :]
            moves.append((t0 + i, src.at[pl.ds(i, step)], dst))
    moves.sort(key=lambda m: m[0])
    moves = [(t, pltpu.make_async_copy(a, b, sem.at[first + i])) for i, (t, a, b) in enumerate(moves)]
    for _, c in moves:
        c.start()
    return moves


def _near_sigma_kernel(cfg, t0, meta, acc, vb_h, right_h, near_h, out, inner_far, vb, right, near, inner, sem):
    moves = [(vb_h, vb), (right_h, right), (near_h, near)]
    moves = [pltpu.make_async_copy(a, b, sem.at[i]) for i, (a, b) in enumerate(moves)]
    for c in moves:
        c.start()
    moves[0].wait()
    moves[1].wait()
    terms, held, half = right.shape[:3]
    for k in range(held):
        for t in range(terms):
            chosen = vb[meta[cfg["pair_at"] + (t0 + t) * held + k]]
            inner[t, k] = jnp.dot(right[t, k], chosen, preferred_element_type=F32).astype(BF16)
    moves[2].wait()
    own, other = (pl.ds(pl.multiple_of(side * half, half), half) for side in (meta[0], 1 - meta[0]))
    for k in range(held):
        total = acc[k]
        for t in range(terms):
            total = total + jnp.dot(inner[t, k, :, own], near[t, k], preferred_element_type=F32)
            inner_far[t, k] = inner[t, k, :, other]
        out[k] = total


def _far_sigma_kernel(acc, inner, far_h, out, far, sem):
    held = far.shape[1]
    moves = [pltpu.make_async_copy(far_h.at[:, k], far.at[:, k], sem.at[k]) for k in range(held)]
    for c in moves:
        c.start()
    for k in range(held):
        moves[k].wait()
        total = acc[k]
        for t in range(far.shape[0]):
            total = total + jnp.dot(inner[t, k], far[t, k], preferred_element_type=F32)
        out[k] = total.astype(out.dtype)


def _step_kernel(cfg, step, places, env_places, last, meta, *refs):
    it = iter(refs)
    take = lambda n: [next(it) for _ in range(n)]
    shards = take(len(places))
    (start, scale_ref), vecs, (pre,) = take(2), take(step - 1), take(1)
    olds_h, envs_h, (sig_h,) = take(step - 1), take(len(env_places)), take(1)
    vnew, dots = (None, None) if last else take(2)
    outs = take(cfg["n_out"])
    if last:
        vnew, turned = take(2)
    olds = take(step - 1)
    right, left, sig, vb, acc, sem = take(6)
    by_rows = take(2) if last and cfg["direct"] else None
    env_pos, z, blk, mine_at = meta[0], meta[1], meta[2], meta[3]
    n_sec, states, width = vnew.shape
    sec, held_sec, half = cfg["sec"], cfg["held"], right.shape[2]
    count = n_sec * states * width
    n_held = sec // held_sec

    def sector(b, h, k):
        if not cfg["direct"]:
            return b * sec + k
        return (blk ^ b) * sec + (mine_at ^ h) * held_sec + k

    order = [(b, h, k) for b in range(cfg["n_blk"]) for h in range(n_held) for k in range(held_sec)]
    old_moves = [pltpu.make_async_copy(a, b, sem.at[i]) for i, (a, b) in enumerate(zip(olds_h, olds))]
    for c in old_moves:
        c.start()
    env_moves = _env_moves(cfg, meta, env_places, envs_h, right, left, sem, step)
    if by_rows:
        save = pltpu.make_async_copy(by_rows[1], sig_h.at[0 : ITERS - 1], sem.at[step - 1])
    else:
        save = pltpu.make_async_copy(sig, sig_h, sem.at[step - 1])
    scales = [scale_ref[0, 0]] + [1.0] * (step - 1)
    basis = [lambda s, r: start[s, r, :].astype(F32)]
    basis += [lambda s, r, v=v: v[s, r, :] for v in vecs]

    pairs = [(j, l) for l in range(1, step) for j in range(l + 1)]
    accs = [jnp.zeros((8, width), F32) for _ in range(2 * step + len(pairs))]
    blocks = {o: [] for o in order}
    for ref, place in zip(shards, places):
        if place is None:
            for b, h, k in order:
                for r in range(0, states, ROWS):
                    at = b * sec + k
                    blocks[b, h, k].append((ref, at, slice(r, r + ROWS), at, slice(r, r + ROWS)))
            continue
        b, e, h = place
        for k in range(held_sec):
            for r in range(0, half, ROWS):
                rows = pl.ds(pl.multiple_of((env_pos ^ e) * half + r, ROWS), ROWS)
                blocks[b, h, k].append((ref, k, slice(r, r + ROWS), sector(b, h, k), rows))
    for o in order:
        for ref, k, r, s, rows in blocks[o]:
            low = ref[k, r, :]
            sig[s, rows, :] = low
            value, cond = low.astype(F32), pre[s, rows, :]
            scaled = value * cond
            held = [b(s, rows) for b in basis]
            found = [_fold(h * value) for h in held] + [_fold(h * scaled) for h in held]
            condh = [h * cond for h in held[1:]]
            found += [_fold(held[j] * condh[l - 1]) for j, l in pairs]
            accs = [a + t for a, t in zip(accs, found)]
    if not by_rows:
        save.start()
    sums = [jnp.sum(a) / count for a in accs]
    proj = [sums[j] * scales[j] for j in range(step)]
    gram = {(0, 0): scale_ref[1, 0]}
    for (j, l), value in zip(pairs, sums[2 * step :]):
        gram[j, l] = gram[l, j] = value * scales[j] * scales[l]
    back = [sums[step + j] * scales[j] - sum(proj[l] * gram[j, l] for l in range(step)) for j in range(step)]
    proj_scaled = [h * x for h, x in zip(proj, scales)]
    back_scaled = [g * x for g, x in zip(back, scales)]

    over = functools.partial(_over, n_sec, states, width)
    for c in old_moves:
        c.wait()

    def trial_pass(s, r):
        value = sig[s, r, :].astype(F32)
        held = [b(s, r) for b in basis]
        trial = value
        for h, b in zip(proj_scaled, held):
            trial = trial - h * b
        trial = trial * pre[s, r, :]
        for g, b in zip(back_scaled, held):
            trial = trial - g * b
        vnew[s, r, :] = trial
        crossed = [o[s, r, :].astype(F32) for o in olds] + [value]
        return (_fold(trial * trial), *[_fold(trial * o) for o in crossed])

    square, *cross = over(1 + step, trial_pass)
    scale = lax.rsqrt(square / count + EPS)
    cross = [x * scale / count for x in cross]

    def final_pass(s, r):
        value = vnew[s, r, :] * scale
        vnew[s, r, :] = value
        vb[s, r, :] = value.astype(BF16)
        return ()

    over(0, final_pass)
    if by_rows:
        turned_sig, sig_rows = by_rows
        chunk, lanes = sig_rows.shape[2], turned_sig.shape[2]
        side = pl.ds(pl.multiple_of(lax.div(z * chunk, lanes) * lanes, lanes), lanes)
        first = pl.ds(pl.multiple_of(lax.rem(z * chunk, lanes), chunk), chunk)
        for i, ref in enumerate([*olds, sig]):
            for k in range(sec):
                turned_sig[i, k] = ref[blk * sec + k, :, side].astype(F32).T
                sig_rows[i, k] = turned_sig[i, k, first, :]
        save.start()
    span = cfg["span"]
    for t0 in range(0, right.shape[0], span):
        for t_move, c in env_moves:
            if t0 <= t_move < t0 + span:
                c.wait()
        for k in range(held_sec):
            total = None if t0 == 0 else acc[k]
            for t in range(t0, t0 + span):
                chosen = vb[meta[cfg["pair_at"] + t * held_sec + k]]
                inner = jnp.dot(right[t, k], chosen, preferred_element_type=F32).astype(BF16)
                got = jnp.dot(inner, left[t, k], preferred_element_type=F32)
                total = got if total is None else total + got
            acc[k] = total
    scalars = proj + cross
    if not last:
        outs[0][...] = acc[...].astype(outs[0].dtype)
        _put_scalars(dots, scalars)
        save.wait()
        return

    rows = pl.ds(pl.multiple_of(env_pos * half, half), half)
    mine = []
    for b, scaled in zip([*basis, lambda s, r: vnew[s, r, :]], [*scales, 1.0]):
        total = jnp.zeros((8, width), F32)
        for k in range(held_sec):
            total = total + _fold(b(sector(0, 0, k) if cfg["direct"] else blk * sec + k, rows) * acc[k])
        mine.append(jnp.sum(total) * scaled / count)
    _put_scalars(outs[0], scalars)
    if cfg["direct"]:
        for k in range(held_sec):
            turned[k] = acc[k].T
        span = states // 2
        side = lax.div(z, 2)
        tail = _addends(mine, half)
        for out, at in ((outs[1], side), (outs[2], 1 - side)):
            for k in range(held_sec):
                rows = pl.ds(pl.multiple_of(at * span, span), span)
                out[k * span : (k + 1) * span, :] = turned[k, rows, :].astype(out.dtype)
            out[held_sec * span :, :] = tail.astype(out.dtype)
    else:
        _put_scalars(outs[1], mine)
        for k in range(held_sec):
            outs[2][k] = acc[k].T
    save.wait()


def _addends(values, width):
    row = lax.broadcasted_iota(jnp.int32, (TAIL_ROWS, width), 0)
    tail = jnp.zeros((TAIL_ROWS, width), F32)
    for j, value in enumerate(values):
        rest = jnp.broadcast_to(value, (TAIL_ROWS, width))
        for p in range(3):
            cut = rest.astype(BF16).astype(F32)
            tail = jnp.where(row == 3 * j + p, cut, tail)
            rest = rest - cut
    return tail


def _added(*tails):
    return [
        sum(tail[3 * j + p : 3 * j + p + 1, 0:1].astype(F32) for tail in tails for p in range(3)) for j in range(ITERS)
    ]


def _merge_kernel(cfg, meta, kept, got, own, keep_out, give_out):
    held, chunk, half = own.shape
    span = 2 * chunk
    z = meta[1]
    at_tail = slice(held * span, held * span + TAIL_ROWS)
    tail = _addends(_added(kept[at_tail, :], got[at_tail, :]), half)
    side = lax.rem(z, 2)
    for which, out in ((side, keep_out), (1 - side, give_out)):
        first = pl.multiple_of(which * chunk, chunk)
        for k in range(held):
            rows = pl.ds(pl.multiple_of(k * span + first, chunk), chunk)
            live = meta[cfg["dims_at"] + meta[2] * cfg["sec"] + meta[3] * held + k]
            at_row = lax.div(z, 2) * span + first + lax.broadcasted_iota(jnp.int32, (chunk, half), 0)
            at_col = meta[0] * half + lax.broadcasted_iota(jnp.int32, (chunk, half), 1)
            value = kept[rows, :] + got[rows, :].astype(F32)
            value = jnp.where((at_row < live) & (at_col < live), value, 0.0)
            out[k * chunk : (k + 1) * chunk, :] = value.astype(BF16)
            if out is keep_out:
                own[k] = value
        out[held * chunk :, :] = tail.astype(BF16)


def _final_kernel(cfg, meta, own, by_env, by_term, by_both, held_h, out_h, rows, sem):
    del held_h
    held, chunk, half = own.shape
    for k in range(held):
        at = slice(k * chunk, (k + 1) * chunk)
        pairs = (own[k], by_env[at, :].astype(F32)), (by_term[at, :].astype(F32), by_both[at, :].astype(F32))
        for h, (mine, other) in enumerate(pairs):
            both = jnp.where(meta[0] == 0, mine, other), jnp.where(meta[0] == 0, other, mine)
            rows[0, (meta[3] ^ h) * held + k] = jnp.concatenate(both, axis=1)
    save = pltpu.make_async_copy(rows, out_h.at[ITERS - 1 : ITERS], sem)
    save.start()
    save.wait()


def _dots_kernel(at, own, by_env, by_term, by_both, out):
    found = _added(*(ref[at : at + TAIL_ROWS, :] for ref in (own, by_env, by_term, by_both)))
    _put_scalars(out, found)


def _subspace_kernel(first, known, dots, other, sub):
    row = lax.broadcasted_iota(jnp.int32, sub.shape, 0)
    col = lax.broadcasted_iota(jnp.int32, sub.shape, 1)
    out = jnp.zeros(sub.shape, F32)
    for i, j, ref, at in ((0, 0, first, 0), (0, 1, first, 1), (0, 2, known, 2),
                          (1, 0, known, 0), (1, 1, known, 1), (1, 2, known, 3)):
        out = jnp.where((row == i) & (col == j), ref[at : at + 1, 0:1], out)
    for j in range(ITERS):
        value = dots[j : j + 1, 0:1] + other[j : j + 1, 0:1]
        out = jnp.where((row == ITERS - 1) & (col == j), value, out)
    sub[...] = out


def solution(mesh):
    n_env, n_term, n_blk = (mesh.shape[a] for a in ("env", "term", "blk"))

    def on_device(psi, left_env, right_env, pairing, sector_dims, precond):
        return _on_device(n_env, n_term, n_blk, psi, left_env, right_env, pairing, sector_dims, precond)

    placed = (
        P(("parts", "blk"), None, None),
        P(("parts", "term"), "blk", "env", None),
        P(("parts", "term"), "blk", "env", None),
        P(("parts", "term"), "blk"),
        P("parts"),
        P(("parts", "blk"), None, None),
    )
    return jax.shard_map(
        on_device,
        mesh=mesh,
        in_specs=placed,
        out_specs=(P(None, ("parts", "blk"), "term", None), P("parts", None)),
        check_vma=False,
    )


def _xor(axis, n, s):
    return functools.partial(lax.ppermute, axis_name=axis, perm=[(i, i ^ s) for i in range(n)])


def _cut_kernel(held, which, env_h, *refs):
    count = (len(refs) - 1) // 2
    outs, bufs, sem = refs[:count], refs[count:-1], refs[-1]
    loads, saves = [], []
    for i, (out, buf) in enumerate(zip(outs, bufs)):
        at = (1 - which[0] if i == 0 else which[0]) * held
        loads.append(pltpu.make_async_copy(env_h.at[:, pl.ds(at, held)], buf, sem.at[0, i]))
        saves.append(pltpu.make_async_copy(buf, out, sem.at[1, i]))
        loads[-1].start()
    for load, save in zip(loads, saves):
        load.wait()
        save.start()
    for save in saves:
        save.wait()


def _cut(env, mine, held, count):
    shape = (env.shape[0], held, *env.shape[2:])
    return pl.pallas_call(
        functools.partial(_cut_kernel, held),
        out_shape=tuple(HB(shape, BF16) for _ in range(count)),
        in_specs=_specs(SM, HB),
        out_specs=tuple(_specs(*[HB] * count)),
        scratch_shapes=[pltpu.VMEM(shape, BF16) for _ in range(count)] + [pltpu.SemaphoreType.DMA((2, count))],
        compiler_params=pltpu.CompilerParams(vmem_limit_bytes=VMEM_LIMIT),
        name="sectors_to_send",
    )(mine.astype(jnp.int32).reshape(1), *_hbm(env))


def _on_device(n_env, n_term, n_blk, psi, left_env, right_env, pairing, sector_dims, precond):
    sec, states, width = psi.shape
    terms = left_env.shape[0]
    n_sec = sec * n_blk
    half = right_env.shape[2]
    direct = n_env == 2 and n_blk == 2 and n_term == 4 and sec % 2 == 0 and terms % 2 == 0
    chunk = states // n_term
    held = sec // 2 if direct else sec
    span = SPAN if terms % SPAN == 0 else 1
    cfg = dict(direct=direct, n_blk=n_blk, sec=sec, held=held, span=span)
    env_pos, term_pos, blk_pos = (lax.axis_index(a) for a in ("env", "term", "blk"))
    mine = (term_pos ^ (term_pos >> 1)) & 1 if direct else jnp.zeros_like(term_pos)
    next_term, far_term = _xor("term", 4, 1), _xor("term", 4, 3)
    other_env, other_blk = _xor("env", 2, 1), _xor("blk", 2, 1)
    corners = functools.partial(
        lax.ppermute, axis_name=("term", "env"), perm=[(2 * t + e, 2 * (t ^ 1) + (e ^ 1)) for t in range(4) for e in range(2)]
    )
    group = lambda x, which: lax.dynamic_slice_in_dim(x, which * held, held, 1)

    if direct:
        to_next, to_env = _cut(left_env, mine, held, 2)
        (right_to_next,) = _cut(right_env, mine, held, 1)
        psi_o, pre_o = other_blk(psi), other_blk(precond)
        next_left = next_term(to_next)
        far_left = other_env(to_env)
        next_right = next_term(right_to_next)
        next_far_left = other_env(next_left)
        own_table = group(pairing, mine)
        own_places = [("left", 0, 0, True), ("left", 0, 1, False)]
        next_places = [("right", 0, 0, False), ("left", 0, 0, False), ("left", 0, 1, False)]
        own_envs, next_envs = [left_env, far_left], [next_right, next_left, next_far_left]
        n_terms = 2 * terms
        shift = lambda place: (place[0], place[1] + terms, *place[2:])
        env_places = [("right", 0, 0, True), *own_places, *map(shift, next_places)]
        envs = [right_env, *own_envs, *next_envs]
    else:
        own_envs = [lax.all_gather(left_env, "env", axis=2, tiled=True)]
        own_places = [("left", 0, 0, False)]
        own_table = pairing
        n_terms = terms
        env_places, envs = [("right", 0, 0, True), *own_places], [right_env, *own_envs]
        psi_o, pre_o = (
            lax.dynamic_slice_in_dim(
                jnp.concatenate([lax.all_gather(x, "blk", axis=0, tiled=True)] * 2, axis=0),
                (blk_pos + 1) * sec,
                sec * (n_blk - 1),
                0,
            )
            for x in (psi, precond)
        )
    flat = jnp.stack([x.astype(jnp.int32) for x in (env_pos, term_pos, blk_pos, mine)])
    own_meta = jnp.concatenate([flat, sector_dims.reshape(-1), own_table.reshape(-1)])
    cfg["dims_at"] = 4
    cfg["pair_at"] = 4 + n_sec

    full = (n_sec, states, width)
    params = pltpu.CompilerParams(vmem_limit_bytes=VMEM_LIMIT)
    dma = pltpu.SemaphoreType.DMA
    n_moves = 3 * terms // span
    first_places, first_envs = [("right", 0, 0, True), *own_places], [right_env, *own_envs]
    start, pret, scale0, vb0, partial = pl.pallas_call(
        functools.partial(_first_kernel, cfg, first_places),
        out_shape=(VM(full, BF16), VM(full, F32), VM((8, 128), F32), HB(full, BF16), VM((held, half, width), F32)),
        in_specs=_specs(SM, VM, VM, VM, VM, *[HB] * len(first_envs)),
        out_specs=_specs(VM, VM, VM, HB, VM),
        scratch_shapes=[
            pltpu.VMEM(full, BF16),
            pltpu.VMEM((terms, held, half, states), BF16),
            pltpu.VMEM((terms, held, states, width), BF16),
            dma((n_moves + 1,)),
        ],
        compiler_params=params,
        name="start_vector",
    )(own_meta, psi, psi_o, precond, pre_o, *_hbm(*first_envs))

    meta = own_meta
    if direct:
        next_pairing = next_term(lax.optimization_barrier((pairing, partial))[0])
        meta = jnp.concatenate([own_meta, group(next_pairing, mine).reshape(-1)])
        piece = (terms, held, half, states)
        partial, inner_far = pl.pallas_call(
            functools.partial(_near_sigma_kernel, cfg, terms),
            out_shape=(VM((held, half, width), F32), VM((terms, held, half, half), BF16)),
            in_specs=_specs(SM, VM, HB, HB, HB),
            out_specs=tuple(_specs(VM, VM)),
            scratch_shapes=[pltpu.VMEM(full, BF16), *[pltpu.VMEM(piece, BF16)] * 3, dma((3,))],
            compiler_params=params,
            name="first_sigma_next_terms",
        )(meta, *_vmem(partial), *_hbm(vb0, next_right, next_left))
        partial = pl.pallas_call(
            _far_sigma_kernel,
            out_shape=VM((held, half, width), BF16),
            in_specs=_specs(VM, VM, HB),
            out_specs=_specs(VM)[0],
            scratch_shapes=[pltpu.VMEM(piece, BF16), dma((held,))],
            compiler_params=params,
            name="first_sigma_far_rows",
        )(*_vmem(partial, inner_far), *_hbm(next_far_left))

    live_own = lax.dynamic_slice_in_dim(sector_dims, blk_pos * sec, sec)

    def masked(value, row0, live):
        row = row0 + lax.broadcasted_iota(jnp.int32, value.shape, 1)
        col = lax.broadcasted_iota(jnp.int32, value.shape, 2)
        live = live[:, None, None]
        return jnp.where((row < live) & (col < live), value, 0.0).astype(BF16)

    def combine(partial):
        if direct:
            total = partial.astype(F32) + far_term(partial).astype(F32)
            shard = masked(total, env_pos * half, lax.dynamic_slice_in_dim(live_own, mine * held, held))
            here = [shard, next_term(shard), other_env(shard), corners(shard)]
            there = [other_blk(x) for x in here]
            return here + there, [(b, e, h) for b in range(2) for e, h in ((0, 0), (0, 1), (1, 0), (1, 1))]
        flat_sum = lax.psum_scatter(partial.reshape(sec * half, width), "term", scatter_dimension=0, tiled=True)
        whole = lax.all_gather(flat_sum, "term", axis=0, tiled=True).reshape(sec, half, width)
        whole = masked(lax.all_gather(whole, "env", axis=1, tiled=True), 0, live_own)
        return [lax.all_gather(whole, "blk", axis=0, tiled=True)], [None]

    out_shape = (ITERS, sec, chunk, states)
    vecs, olds = [], []
    for step in range(1, ITERS):
        last = step + 1 == ITERS
        shards, places = combine(partial)
        if last:
            outs = [VM((8, 128), F32)]
            if direct:
                size = (held * states // 2 + TAIL_ROWS, half)
                outs += [VM(size, F32), VM(size, BF16)]
            else:
                outs += [VM((8, 128), F32), VM((sec, states, half), F32)]
            made = (HB(out_shape, F32) if direct else HB(full, BF16),)
        else:
            outs = [VM((held, half, width), BF16 if direct else F32)]
            made = (HB(full, BF16), VM(full, F32), VM((8, 128), F32))
        n_hbm = (step - 1) + len(envs)
        results = pl.pallas_call(
            functools.partial(_step_kernel, dict(cfg, n_out=len(outs)), step, places, env_places, last),
            out_shape=(*made, *outs),
            in_specs=_specs(SM, *[VM] * (len(shards) + 3 + len(vecs)), *[HB] * n_hbm),
            out_specs=tuple(_specs(HB, *[VM] * (len(made) - 1 + len(outs)))),
            scratch_shapes=[pltpu.VMEM(full, F32), pltpu.VMEM((held, states, half), F32)] * last
            + [pltpu.VMEM(full, BF16)] * (step - 1)
            + [
                pltpu.VMEM((n_terms, held, half, states), BF16),
                pltpu.VMEM((n_terms, held, states, width), BF16),
                pltpu.VMEM(full, BF16),
                pltpu.VMEM(full, BF16),
                pltpu.VMEM((held, half, width), F32),
                dma((step + len(envs) * n_moves,)),
            ]
            + [pltpu.VMEM((step, sec, 2 * chunk, states), F32), pltpu.VMEM((step, sec, chunk, states), F32)] * (last and direct),
            compiler_params=params,
            name=f"vector_and_sigma_{step}",
        )(
            meta,
            *_vmem(*shards, start, scale0, *vecs, pret),
            *_hbm(*olds, *envs),
        )
        olds.append(results[0])
        if last:
            known, *pieces = results[1:]
        else:
            vecs.append(results[1])
            first, partial = results[2:]

    if direct:
        kept, given = pieces
        got = far_term(given)
        size = (held * chunk + TAIL_ROWS, half)
        own, keep, give = pl.pallas_call(
            functools.partial(_merge_kernel, cfg),
            out_shape=(VM((held, chunk, half), F32), VM(size, BF16), VM(size, BF16)),
            in_specs=_specs(SM, VM, VM),
            out_specs=tuple(_specs(VM, VM, VM)),
            compiler_params=params,
            name="last_sums",
        )(meta, *_vmem(kept, got))
        parts = [other_env(keep), next_term(give), corners(give)]
        dots = pl.pallas_call(
            functools.partial(_dots_kernel, held * chunk),
            out_shape=VM((8, 128), F32),
            in_specs=_specs(*[VM] * 4),
            out_specs=_specs(VM)[0],
            compiler_params=params,
            name="last_dots",
        )(*_vmem(keep, *parts))
        other_dots = other_blk(dots)
        sigmas = pl.pallas_call(
            functools.partial(_final_kernel, cfg),
            out_shape=HB(out_shape, F32),
            in_specs=_specs(SM, *[VM] * 4, HB),
            out_specs=_specs(HB)[0],
            scratch_shapes=[pltpu.VMEM((1, sec, chunk, states), F32), dma],
            input_output_aliases={5: 0},
            compiler_params=params,
            name="last_rows",
        )(meta, *_vmem(own, *parts), *_hbm(olds[-1]))
        subspace = pl.pallas_call(
            _subspace_kernel,
            out_shape=jax.ShapeDtypeStruct((ITERS, ITERS), F32),
            in_specs=_specs(*[VM] * 4),
            out_specs=_specs(VM)[0],
            compiler_params=params,
            name="subspace",
        )(*_vmem(first, known, dots, other_dots))
        return sigmas, subspace
    dots = pieces.pop(0)
    own = lax.psum_scatter(pieces[0], "term", scatter_dimension=1, tiled=True)
    both = lax.all_gather(own, "env", axis=2, tiled=True)
    row = term_pos * chunk + lax.broadcasted_iota(jnp.int32, both.shape, 1)
    col = lax.broadcasted_iota(jnp.int32, both.shape, 2)
    live = live_own[:, None, None]
    both = jnp.where((row < live) & (col < live), both, 0.0)
    rows_out = []
    for sig in olds:
        part = lax.dynamic_slice(sig, (blk_pos * sec, 0, term_pos * chunk), (sec, states, chunk))
        rows_out.append(jnp.swapaxes(part, 1, 2).astype(F32))
    rows_out.append(both)
    scal = lax.psum(dots, ("term", "env", "blk"))[:ITERS, 0]
    first, second = first[:, 0], known[:, 0]
    subspace = jnp.stack([
        jnp.stack([first[0], first[1], second[2]]),
        jnp.stack([second[0], second[1], second[3]]),
        scal,
    ])
    return jnp.stack(rows_out), subspace
```

```python
import functools

import jax
import jax.numpy as jnp
from jax import lax
from jax.experimental import pallas as pl
from jax.experimental.pallas import tpu as pltpu
from jax.sharding import PartitionSpec as P

ITERS = 3
EPS = 1e-06
F32, BF16 = jnp.float32, jnp.bfloat16
ROWS = 128
TAIL_ROWS = 16
SPAN = 8
VMEM_LIMIT = 16 * 1024 * 1024
HB, VM, SM = pltpu.HBM, pltpu.VMEM, pltpu.SMEM


def _specs(*shapes):
    return [pl.BlockSpec(memory_space=s) for s in shapes]


def _hbm(*arrays):
    return [pltpu.with_memory_space_constraint(x, HB) for x in arrays]


def _vmem(*arrays):
    return [pltpu.with_memory_space_constraint(x, VM) for x in arrays]


def _fold(x):
    return jnp.sum(x.reshape(x.shape[0] // 8, 8, x.shape[1]), axis=0)


def _over(n_sec, states, width, n_acc, body):
    blocks = states // ROWS

    def step(i, accs):
        for b in range(blocks):
            accs = tuple(x + y for x, y in zip(accs, body(i, slice(b * ROWS, (b + 1) * ROWS))))
        return accs

    zero = tuple(jnp.zeros((8, width), F32) for _ in range(n_acc))
    return tuple(jnp.sum(a) for a in lax.fori_loop(0, n_sec, step, zero))


def _put_scalars(ref, values):
    shape = ref.shape
    row = lax.broadcasted_iota(jnp.int32, shape, 0)
    out = jnp.zeros(shape, F32)
    for index, value in enumerate(values):
        out = jnp.where(row == index, value, out)
    ref[...] = out


def _first_kernel(cfg, places, meta, psi, psi_o, pre, pre_o, *refs):
    envs, (start, pret, scale_ref, acc, vb, right, left, sem) = refs[: len(places)], refs[len(places) :]
    sec, states, width = psi.shape
    n_sec = sec * cfg["n_blk"]
    base = meta[2] * sec
    moves = _env_moves(cfg, meta, places, envs, right, left, sem)
    for part, (p_ref, c_ref) in enumerate(((psi, pre), (psi_o, pre_o))):
        for k in range(p_ref.shape[0]):
            at = lax.rem(base + part * sec + k, n_sec)
            live = meta[cfg["dims_at"] + at]
            row = lax.broadcasted_iota(jnp.int32, (states, width), 0)
            col = lax.broadcasted_iota(jnp.int32, (states, width), 1)
            value = jnp.where((row < live) & (col < live), p_ref[k].astype(F32).T, 0.0)
            start[at] = value.astype(BF16)
            pret[at] = c_ref[k].T
    def square(s, r):
        value = start[s, r, :].astype(F32)
        return (_fold(value * value),)

    (total,) = _over(n_sec, states, width, 1, square)
    scale = lax.rsqrt(total / (n_sec * states * width) + EPS)
    count = n_sec * states * width

    def cond(s, r):
        value = start[s, r, :].astype(F32)
        return (_fold(value * value * pret[s, r, :]),)

    (damped,) = _over(n_sec, states, width, 1, cond)
    _put_scalars(scale_ref, [scale, damped * scale * scale / count])

    def make(s, r):
        vb[s, r, :] = (start[s, r, :].astype(F32) * scale).astype(BF16)
        return ()

    _over(n_sec, states, width, 0, make)
    for _, c in moves:
        c.wait()
    for k in range(acc.shape[0]):
        total = None
        for t in range(right.shape[0]):
            chosen = vb[meta[cfg["pair_at"] + t * acc.shape[0] + k]]
            inner = jnp.dot(right[t, k], chosen, preferred_element_type=F32).astype(BF16)
            got = jnp.dot(inner, left[t, k], preferred_element_type=F32)
            total = got if total is None else total + got
        acc[k] = total


def _group(cfg, meta, ref):
    return ref.at[:, pl.ds(meta[3] * cfg["held"], cfg["held"])]


def _env_moves(cfg, meta, places, refs, right, left, sem, first=0):
    moves = []
    for ref, (kind, t0, far, own) in zip(refs, places):
        src = _group(cfg, meta, ref) if own else ref
        step = cfg["span"]
        for i in range(0, ref.shape[0], step):
            t = pl.ds(t0 + i, step)
            side = meta[0] ^ far if cfg["direct"] else 0
            rows = pl.ds(pl.multiple_of(side * ref.shape[2], ref.shape[2]), ref.shape[2])
            dst = right.at[t] if kind == "right" else left.at[t, :, rows, :]
            moves.append((t0 + i, src.at[pl.ds(i, step)], dst))
    moves.sort(key=lambda m: m[0])
    moves = [(t, pltpu.make_async_copy(a, b, sem.at[first + i])) for i, (t, a, b) in enumerate(moves)]
    for _, c in moves:
        c.start()
    return moves


def _near_sigma_kernel(cfg, t0, meta, acc, start, scale_ref, right_h, near_h, out, inner_far, vb, right, near, inner, sem):
    moves = [(right_h, right), (near_h, near)]
    moves = [pltpu.make_async_copy(a, b, sem.at[i]) for i, (a, b) in enumerate(moves)]
    for c in moves:
        c.start()
    scale = scale_ref[0, 0]

    def make(s, r):
        vb[s, r, :] = (start[s, r, :].astype(F32) * scale).astype(BF16)
        return ()

    _over(*vb.shape, 0, make)
    moves[0].wait()
    terms, held, half = right.shape[:3]
    for k in range(held):
        for t in range(terms):
            chosen = vb[meta[cfg["pair_at"] + (t0 + t) * held + k]]
            inner[t, k] = jnp.dot(right[t, k], chosen, preferred_element_type=F32).astype(BF16)
    moves[1].wait()
    own, other = (pl.ds(pl.multiple_of(side * half, half), half) for side in (meta[0], 1 - meta[0]))
    for k in range(held):
        total = acc[k]
        for t in range(terms):
            total = total + jnp.dot(inner[t, k, :, own], near[t, k], preferred_element_type=F32)
            inner_far[t, k] = inner[t, k, :, other]
        out[k] = total


def _far_sigma_kernel(acc, inner, far_h, out, far, sem):
    held = far.shape[1]
    moves = [pltpu.make_async_copy(far_h.at[:, k], far.at[:, k], sem.at[k]) for k in range(held)]
    for c in moves:
        c.start()
    for k in range(held):
        moves[k].wait()
        total = acc[k]
        for t in range(far.shape[0]):
            total = total + jnp.dot(inner[t, k], far[t, k], preferred_element_type=F32)
        out[k] = total.astype(out.dtype)


def _step_kernel(cfg, step, places, env_places, last, meta, *refs):
    it = iter(refs)
    take = lambda n: [next(it) for _ in range(n)]
    shards = take(len(places))
    (start, scale_ref), vecs, (pre,) = take(2), take(step - 1), take(1)
    olds_h, envs_h, (sig_h,) = take(step - 1), take(len(env_places)), take(1)
    vnew, dots = (None, None) if last else take(2)
    outs = take(cfg["n_out"])
    if last:
        vnew, turned = take(2)
    olds = take(step - 1)
    right, left, sig, vb, acc, sem = take(6)
    by_rows = take(2) if last and cfg["direct"] else None
    env_pos, z, blk, mine_at = meta[0], meta[1], meta[2], meta[3]
    n_sec, states, width = vnew.shape
    sec, held_sec, half = cfg["sec"], cfg["held"], right.shape[2]
    count = n_sec * states * width
    n_held = sec // held_sec

    def sector(b, h, k):
        if not cfg["direct"]:
            return b * sec + k
        return (blk ^ b) * sec + (mine_at ^ h) * held_sec + k

    order = [(b, h, k) for b in range(cfg["n_blk"]) for h in range(n_held) for k in range(held_sec)]
    old_moves = [pltpu.make_async_copy(a, b, sem.at[i]) for i, (a, b) in enumerate(zip(olds_h, olds))]
    for c in old_moves:
        c.start()
    env_moves = _env_moves(cfg, meta, env_places, envs_h, right, left, sem, step)
    if by_rows:
        save = pltpu.make_async_copy(by_rows[1], sig_h.at[0 : ITERS - 1], sem.at[step - 1])
    else:
        save = pltpu.make_async_copy(sig, sig_h, sem.at[step - 1])
    scales = [scale_ref[0, 0]] + [1.0] * (step - 1)
    basis = [lambda s, r: start[s, r, :].astype(F32)]
    basis += [lambda s, r, v=v: v[s, r, :] for v in vecs]

    pairs = [(j, l) for l in range(1, step) for j in range(l + 1)]
    accs = [jnp.zeros((8, width), F32) for _ in range(2 * step + len(pairs))]
    blocks = {o: [] for o in order}
    for ref, place in zip(shards, places):
        if place is None:
            for b, h, k in order:
                for r in range(0, states, ROWS):
                    at = b * sec + k
                    blocks[b, h, k].append((ref, at, slice(r, r + ROWS), at, slice(r, r + ROWS)))
            continue
        b, e, h = place
        for k in range(held_sec):
            for r in range(0, half, ROWS):
                rows = pl.ds(pl.multiple_of((env_pos ^ e) * half + r, ROWS), ROWS)
                blocks[b, h, k].append((ref, k, slice(r, r + ROWS), sector(b, h, k), rows))
    for o in order:
        for ref, k, r, s, rows in blocks[o]:
            low = ref[k, r, :]
            sig[s, rows, :] = low
            value, cond = low.astype(F32), pre[s, rows, :]
            scaled = value * cond
            held = [b(s, rows) for b in basis]
            found = [_fold(h * value) for h in held] + [_fold(h * scaled) for h in held]
            condh = [h * cond for h in held[1:]]
            found += [_fold(held[j] * condh[l - 1]) for j, l in pairs]
            accs = [a + t for a, t in zip(accs, found)]
    if not by_rows:
        save.start()
    sums = [jnp.sum(a) / count for a in accs]
    proj = [sums[j] * scales[j] for j in range(step)]
    gram = {(0, 0): scale_ref[1, 0]}
    for (j, l), value in zip(pairs, sums[2 * step :]):
        gram[j, l] = gram[l, j] = value * scales[j] * scales[l]
    back = [sums[step + j] * scales[j] - sum(proj[l] * gram[j, l] for l in range(step)) for j in range(step)]
    proj_scaled = [h * x for h, x in zip(proj, scales)]
    back_scaled = [g * x for g, x in zip(back, scales)]

    over = functools.partial(_over, n_sec, states, width)
    for c in old_moves:
        c.wait()

    def trial_pass(s, r):
        value = sig[s, r, :].astype(F32)
        held = [b(s, r) for b in basis]
        trial = value
        for h, b in zip(proj_scaled, held):
            trial = trial - h * b
        trial = trial * pre[s, r, :]
        for g, b in zip(back_scaled, held):
            trial = trial - g * b
        vnew[s, r, :] = trial
        crossed = [o[s, r, :].astype(F32) for o in olds] + [value]
        return (_fold(trial * trial), *[_fold(trial * o) for o in crossed])

    square, *cross = over(1 + step, trial_pass)
    scale = lax.rsqrt(square / count + EPS)
    cross = [x * scale / count for x in cross]

    def final_pass(s, r):
        value = vnew[s, r, :] * scale
        vnew[s, r, :] = value
        vb[s, r, :] = value.astype(BF16)
        return ()

    over(0, final_pass)
    if by_rows:
        turned_sig, sig_rows = by_rows
        chunk, lanes = sig_rows.shape[2], turned_sig.shape[2]
        side = pl.ds(pl.multiple_of(lax.div(z * chunk, lanes) * lanes, lanes), lanes)
        first = pl.ds(pl.multiple_of(lax.rem(z * chunk, lanes), chunk), chunk)
        for i, ref in enumerate([*olds, sig]):
            for k in range(sec):
                turned_sig[i, k] = ref[blk * sec + k, :, side].astype(F32).T
                sig_rows[i, k] = turned_sig[i, k, first, :]
        save.start()
    span = cfg["span"]
    for t0 in range(0, right.shape[0], span):
        for t_move, c in env_moves:
            if t0 <= t_move < t0 + span:
                c.wait()
        for k in range(held_sec):
            total = None if t0 == 0 else acc[k]
            for t in range(t0, t0 + span):
                chosen = vb[meta[cfg["pair_at"] + t * held_sec + k]]
                inner = jnp.dot(right[t, k], chosen, preferred_element_type=F32).astype(BF16)
                got = jnp.dot(inner, left[t, k], preferred_element_type=F32)
                total = got if total is None else total + got
            acc[k] = total
    scalars = proj + cross
    if not last:
        outs[0][...] = acc[...].astype(outs[0].dtype)
        _put_scalars(dots, scalars)
        save.wait()
        return

    rows = pl.ds(pl.multiple_of(env_pos * half, half), half)
    mine = []
    for b, scaled in zip([*basis, lambda s, r: vnew[s, r, :]], [*scales, 1.0]):
        total = jnp.zeros((8, width), F32)
        for k in range(held_sec):
            total = total + _fold(b(sector(0, 0, k) if cfg["direct"] else blk * sec + k, rows) * acc[k])
        mine.append(jnp.sum(total) * scaled / count)
    _put_scalars(outs[0], scalars)
    if cfg["direct"]:
        for k in range(held_sec):
            turned[k] = acc[k].T
        span = states // 2
        side = lax.div(z, 2)
        tail = _addends(mine, half)
        for out, at in ((outs[1], side), (outs[2], 1 - side)):
            for k in range(held_sec):
                rows = pl.ds(pl.multiple_of(at * span, span), span)
                out[k * span : (k + 1) * span, :] = turned[k, rows, :].astype(out.dtype)
            out[held_sec * span :, :] = tail.astype(out.dtype)
    else:
        _put_scalars(outs[1], mine)
        for k in range(held_sec):
            outs[2][k] = acc[k].T
    save.wait()


def _addends(values, width):
    row = lax.broadcasted_iota(jnp.int32, (TAIL_ROWS, width), 0)
    tail = jnp.zeros((TAIL_ROWS, width), F32)
    for j, value in enumerate(values):
        rest = jnp.broadcast_to(value, (TAIL_ROWS, width))
        for p in range(3):
            cut = rest.astype(BF16).astype(F32)
            tail = jnp.where(row == 3 * j + p, cut, tail)
            rest = rest - cut
    return tail


def _added(*tails):
    return [
        sum(tail[3 * j + p : 3 * j + p + 1, 0:1].astype(F32) for tail in tails for p in range(3)) for j in range(ITERS)
    ]


def _merge_kernel(cfg, meta, kept, got, own, keep_out, give_out):
    held, chunk, half = own.shape
    span = 2 * chunk
    z = meta[1]
    at_tail = slice(held * span, held * span + TAIL_ROWS)
    tail = _addends(_added(kept[at_tail, :], got[at_tail, :]), half)
    side = lax.rem(z, 2)
    for which, out in ((side, keep_out), (1 - side, give_out)):
        first = pl.multiple_of(which * chunk, chunk)
        for k in range(held):
            rows = pl.ds(pl.multiple_of(k * span + first, chunk), chunk)
            live = meta[cfg["dims_at"] + meta[2] * cfg["sec"] + meta[3] * held + k]
            at_row = lax.div(z, 2) * span + first + lax.broadcasted_iota(jnp.int32, (chunk, half), 0)
            at_col = meta[0] * half + lax.broadcasted_iota(jnp.int32, (chunk, half), 1)
            value = kept[rows, :] + got[rows, :].astype(F32)
            value = jnp.where((at_row < live) & (at_col < live), value, 0.0)
            out[k * chunk : (k + 1) * chunk, :] = value.astype(BF16)
            if out is keep_out:
                own[k] = value
        out[held * chunk :, :] = tail.astype(BF16)


def _final_kernel(cfg, meta, own, by_env, by_term, by_both, held_h, out_h, rows, sem):
    del held_h
    held, chunk, half = own.shape
    for k in range(held):
        at = slice(k * chunk, (k + 1) * chunk)
        pairs = (own[k], by_env[at, :].astype(F32)), (by_term[at, :].astype(F32), by_both[at, :].astype(F32))
        for h, (mine, other) in enumerate(pairs):
            both = jnp.where(meta[0] == 0, mine, other), jnp.where(meta[0] == 0, other, mine)
            rows[0, (meta[3] ^ h) * held + k] = jnp.concatenate(both, axis=1)
    save = pltpu.make_async_copy(rows, out_h.at[ITERS - 1 : ITERS], sem)
    save.start()
    save.wait()


def _dots_kernel(at, own, by_env, by_term, by_both, out):
    found = _added(*(ref[at : at + TAIL_ROWS, :] for ref in (own, by_env, by_term, by_both)))
    _put_scalars(out, found)


def _subspace_kernel(first, known, dots, other, sub):
    row = lax.broadcasted_iota(jnp.int32, sub.shape, 0)
    col = lax.broadcasted_iota(jnp.int32, sub.shape, 1)
    out = jnp.zeros(sub.shape, F32)
    for i, j, ref, at in ((0, 0, first, 0), (0, 1, first, 1), (0, 2, known, 2),
                          (1, 0, known, 0), (1, 1, known, 1), (1, 2, known, 3)):
        out = jnp.where((row == i) & (col == j), ref[at : at + 1, 0:1], out)
    for j in range(ITERS):
        value = dots[j : j + 1, 0:1] + other[j : j + 1, 0:1]
        out = jnp.where((row == ITERS - 1) & (col == j), value, out)
    sub[...] = out


def solution(mesh):
    n_env, n_term, n_blk = (mesh.shape[a] for a in ("env", "term", "blk"))

    def on_device(psi, left_env, right_env, pairing, sector_dims, precond):
        return _on_device(n_env, n_term, n_blk, psi, left_env, right_env, pairing, sector_dims, precond)

    placed = (
        P(("parts", "blk"), None, None),
        P(("parts", "term"), "blk", "env", None),
        P(("parts", "term"), "blk", "env", None),
        P(("parts", "term"), "blk"),
        P("parts"),
        P(("parts", "blk"), None, None),
    )
    return jax.shard_map(
        on_device,
        mesh=mesh,
        in_specs=placed,
        out_specs=(P(None, ("parts", "blk"), "term", None), P("parts", None)),
        check_vma=False,
    )


def _xor(axis, n, s):
    return functools.partial(lax.ppermute, axis_name=axis, perm=[(i, i ^ s) for i in range(n)])


def _cut_kernel(held, which, env_h, *refs):
    count = (len(refs) - 1) // 2
    outs, bufs, sem = refs[:count], refs[count:-1], refs[-1]
    loads, saves = [], []
    for i, (out, buf) in enumerate(zip(outs, bufs)):
        at = (1 - which[0] if i == 0 else which[0]) * held
        loads.append(pltpu.make_async_copy(env_h.at[:, pl.ds(at, held)], buf, sem.at[0, i]))
        saves.append(pltpu.make_async_copy(buf, out, sem.at[1, i]))
        loads[-1].start()
    for load, save in zip(loads, saves):
        load.wait()
        save.start()
    for save in saves:
        save.wait()


def _cut(env, mine, held, count):
    shape = (env.shape[0], held, *env.shape[2:])
    return pl.pallas_call(
        functools.partial(_cut_kernel, held),
        out_shape=tuple(HB(shape, BF16) for _ in range(count)),
        in_specs=_specs(SM, HB),
        out_specs=tuple(_specs(*[HB] * count)),
        scratch_shapes=[pltpu.VMEM(shape, BF16) for _ in range(count)] + [pltpu.SemaphoreType.DMA((2, count))],
        compiler_params=pltpu.CompilerParams(vmem_limit_bytes=VMEM_LIMIT),
        name="sectors_to_send",
    )(mine.astype(jnp.int32).reshape(1), *_hbm(env))


def _on_device(n_env, n_term, n_blk, psi, left_env, right_env, pairing, sector_dims, precond):
    sec, states, width = psi.shape
    terms = left_env.shape[0]
    n_sec = sec * n_blk
    half = right_env.shape[2]
    direct = n_env == 2 and n_blk == 2 and n_term == 4 and sec % 2 == 0 and terms % 2 == 0
    chunk = states // n_term
    held = sec // 2 if direct else sec
    span = SPAN if terms % SPAN == 0 else 1
    cfg = dict(direct=direct, n_blk=n_blk, sec=sec, held=held, span=span)
    env_pos, term_pos, blk_pos = (lax.axis_index(a) for a in ("env", "term", "blk"))
    mine = (term_pos ^ (term_pos >> 1)) & 1 if direct else jnp.zeros_like(term_pos)
    next_term, far_term = _xor("term", 4, 1), _xor("term", 4, 3)
    other_env, other_blk = _xor("env", 2, 1), _xor("blk", 2, 1)
    corners = functools.partial(
        lax.ppermute, axis_name=("term", "env"), perm=[(2 * t + e, 2 * (t ^ 1) + (e ^ 1)) for t in range(4) for e in range(2)]
    )
    group = lambda x, which: lax.dynamic_slice_in_dim(x, which * held, held, 1)

    if direct:
        to_next, to_env = _cut(left_env, mine, held, 2)
        (right_to_next,) = _cut(right_env, mine, held, 1)
        psi_o, pre_o = other_blk(psi), other_blk(precond)
        next_left = next_term(to_next)
        far_left = other_env(to_env)
        next_right = next_term(right_to_next)
        next_far_left = other_env(next_left)
        own_table = group(pairing, mine)
        own_places = [("left", 0, 0, True), ("left", 0, 1, False)]
        next_places = [("right", 0, 0, False), ("left", 0, 0, False), ("left", 0, 1, False)]
        own_envs, next_envs = [left_env, far_left], [next_right, next_left, next_far_left]
        n_terms = 2 * terms
        shift = lambda place: (place[0], place[1] + terms, *place[2:])
        env_places = [("right", 0, 0, True), *own_places, *map(shift, next_places)]
        envs = [right_env, *own_envs, *next_envs]
    else:
        own_envs = [lax.all_gather(left_env, "env", axis=2, tiled=True)]
        own_places = [("left", 0, 0, False)]
        own_table = pairing
        n_terms = terms
        env_places, envs = [("right", 0, 0, True), *own_places], [right_env, *own_envs]
        psi_o, pre_o = (
            lax.dynamic_slice_in_dim(
                jnp.concatenate([lax.all_gather(x, "blk", axis=0, tiled=True)] * 2, axis=0),
                (blk_pos + 1) * sec,
                sec * (n_blk - 1),
                0,
            )
            for x in (psi, precond)
        )
    flat = jnp.stack([x.astype(jnp.int32) for x in (env_pos, term_pos, blk_pos, mine)])
    own_meta = jnp.concatenate([flat, sector_dims.reshape(-1), own_table.reshape(-1)])
    cfg["dims_at"] = 4
    cfg["pair_at"] = 4 + n_sec

    full = (n_sec, states, width)
    params = pltpu.CompilerParams(vmem_limit_bytes=VMEM_LIMIT)
    dma = pltpu.SemaphoreType.DMA
    n_moves = 3 * terms // span
    first_places, first_envs = [("right", 0, 0, True), *own_places], [right_env, *own_envs]
    start, pret, scale0, partial = pl.pallas_call(
        functools.partial(_first_kernel, cfg, first_places),
        out_shape=(VM(full, BF16), VM(full, F32), VM((8, 128), F32), VM((held, half, width), F32)),
        in_specs=_specs(SM, VM, VM, VM, VM, *[HB] * len(first_envs)),
        out_specs=_specs(VM, VM, VM, VM),
        scratch_shapes=[
            pltpu.VMEM(full, BF16),
            pltpu.VMEM((terms, held, half, states), BF16),
            pltpu.VMEM((terms, held, states, width), BF16),
            dma((n_moves,)),
        ],
        compiler_params=params,
        name="start_vector",
    )(own_meta, psi, psi_o, precond, pre_o, *_hbm(*first_envs))

    meta = own_meta
    if direct:
        next_pairing = next_term(lax.optimization_barrier((pairing, partial))[0])
        meta = jnp.concatenate([own_meta, group(next_pairing, mine).reshape(-1)])
        piece = (terms, held, half, states)
        partial, inner_far = pl.pallas_call(
            functools.partial(_near_sigma_kernel, cfg, terms),
            out_shape=(VM((held, half, width), F32), VM((terms, held, half, half), BF16)),
            in_specs=_specs(SM, VM, VM, VM, HB, HB),
            out_specs=tuple(_specs(VM, VM)),
            scratch_shapes=[pltpu.VMEM(full, BF16), *[pltpu.VMEM(piece, BF16)] * 3, dma((2,))],
            compiler_params=params,
            name="first_sigma_next_terms",
        )(meta, *_vmem(partial, start, scale0), *_hbm(next_right, next_left))
        partial = pl.pallas_call(
            _far_sigma_kernel,
            out_shape=VM((held, half, width), BF16),
            in_specs=_specs(VM, VM, HB),
            out_specs=_specs(VM)[0],
            scratch_shapes=[pltpu.VMEM(piece, BF16), dma((held,))],
            compiler_params=params,
            name="first_sigma_far_rows",
        )(*_vmem(partial, inner_far), *_hbm(next_far_left))

    live_own = lax.dynamic_slice_in_dim(sector_dims, blk_pos * sec, sec)

    def masked(value, row0, live):
        row = row0 + lax.broadcasted_iota(jnp.int32, value.shape, 1)
        col = lax.broadcasted_iota(jnp.int32, value.shape, 2)
        live = live[:, None, None]
        return jnp.where((row < live) & (col < live), value, 0.0).astype(BF16)

    def combine(partial):
        if direct:
            total = partial.astype(F32) + far_term(partial).astype(F32)
            shard = masked(total, env_pos * half, lax.dynamic_slice_in_dim(live_own, mine * held, held))
            here = [shard, next_term(shard), other_env(shard), corners(shard)]
            there = [other_blk(x) for x in here]
            return here + there, [(b, e, h) for b in range(2) for e, h in ((0, 0), (0, 1), (1, 0), (1, 1))]
        flat_sum = lax.psum_scatter(partial.reshape(sec * half, width), "term", scatter_dimension=0, tiled=True)
        whole = lax.all_gather(flat_sum, "term", axis=0, tiled=True).reshape(sec, half, width)
        whole = masked(lax.all_gather(whole, "env", axis=1, tiled=True), 0, live_own)
        return [lax.all_gather(whole, "blk", axis=0, tiled=True)], [None]

    out_shape = (ITERS, sec, chunk, states)
    vecs, olds = [], []
    for step in range(1, ITERS):
        last = step + 1 == ITERS
        shards, places = combine(partial)
        if last:
            outs = [VM((8, 128), F32)]
            if direct:
                size = (held * states // 2 + TAIL_ROWS, half)
                outs += [VM(size, F32), VM(size, BF16)]
            else:
                outs += [VM((8, 128), F32), VM((sec, states, half), F32)]
            made = (HB(out_shape, F32) if direct else HB(full, BF16),)
        else:
            outs = [VM((held, half, width), BF16 if direct else F32)]
            made = (HB(full, BF16), VM(full, F32), VM((8, 128), F32))
        n_hbm = (step - 1) + len(envs)
        results = pl.pallas_call(
            functools.partial(_step_kernel, dict(cfg, n_out=len(outs)), step, places, env_places, last),
            out_shape=(*made, *outs),
            in_specs=_specs(SM, *[VM] * (len(shards) + 3 + len(vecs)), *[HB] * n_hbm),
            out_specs=tuple(_specs(HB, *[VM] * (len(made) - 1 + len(outs)))),
            scratch_shapes=[pltpu.VMEM(full, F32), pltpu.VMEM((held, states, half), F32)] * last
            + [pltpu.VMEM(full, BF16)] * (step - 1)
            + [
                pltpu.VMEM((n_terms, held, half, states), BF16),
                pltpu.VMEM((n_terms, held, states, width), BF16),
                pltpu.VMEM(full, BF16),
                pltpu.VMEM(full, BF16),
                pltpu.VMEM((held, half, width), F32),
                dma((step + len(envs) * n_moves,)),
            ]
            + [pltpu.VMEM((step, sec, 2 * chunk, states), F32), pltpu.VMEM((step, sec, chunk, states), F32)] * (last and direct),
            compiler_params=params,
            name=f"vector_and_sigma_{step}",
        )(
            meta,
            *_vmem(*shards, start, scale0, *vecs, pret),
            *_hbm(*olds, *envs),
        )
        olds.append(results[0])
        if last:
            known, *pieces = results[1:]
        else:
            vecs.append(results[1])
            first, partial = results[2:]

    if direct:
        kept, given = pieces
        got = far_term(given)
        size = (held * chunk + TAIL_ROWS, half)
        own, keep, give = pl.pallas_call(
            functools.partial(_merge_kernel, cfg),
            out_shape=(VM((held, chunk, half), F32), VM(size, BF16), VM(size, BF16)),
            in_specs=_specs(SM, VM, VM),
            out_specs=tuple(_specs(VM, VM, VM)),
            compiler_params=params,
            name="last_sums",
        )(meta, *_vmem(kept, got))
        parts = [other_env(keep), next_term(give), corners(give)]
        dots = pl.pallas_call(
            functools.partial(_dots_kernel, held * chunk),
            out_shape=VM((8, 128), F32),
            in_specs=_specs(*[VM] * 4),
            out_specs=_specs(VM)[0],
            compiler_params=params,
            name="last_dots",
        )(*_vmem(keep, *parts))
        other_dots = other_blk(dots)
        sigmas = pl.pallas_call(
            functools.partial(_final_kernel, cfg),
            out_shape=HB(out_shape, F32),
            in_specs=_specs(SM, *[VM] * 4, HB),
            out_specs=_specs(HB)[0],
            scratch_shapes=[pltpu.VMEM((1, sec, chunk, states), F32), dma],
            input_output_aliases={5: 0},
            compiler_params=params,
            name="last_rows",
        )(meta, *_vmem(own, *parts), *_hbm(olds[-1]))
        subspace = pl.pallas_call(
            _subspace_kernel,
            out_shape=jax.ShapeDtypeStruct((ITERS, ITERS), F32),
            in_specs=_specs(*[VM] * 4),
            out_specs=_specs(VM)[0],
            compiler_params=params,
            name="subspace",
        )(*_vmem(first, known, dots, other_dots))
        return sigmas, subspace
    dots = pieces.pop(0)
    own = lax.psum_scatter(pieces[0], "term", scatter_dimension=1, tiled=True)
    both = lax.all_gather(own, "env", axis=2, tiled=True)
    row = term_pos * chunk + lax.broadcasted_iota(jnp.int32, both.shape, 1)
    col = lax.broadcasted_iota(jnp.int32, both.shape, 2)
    live = live_own[:, None, None]
    both = jnp.where((row < live) & (col < live), both, 0.0)
    rows_out = []
    for sig in olds:
        part = lax.dynamic_slice(sig, (blk_pos * sec, 0, term_pos * chunk), (sec, states, chunk))
        rows_out.append(jnp.swapaxes(part, 1, 2).astype(F32))
    rows_out.append(both)
    scal = lax.psum(dots, ("term", "env", "blk"))[:ITERS, 0]
    first, second = first[:, 0], known[:, 0]
    subspace = jnp.stack([
        jnp.stack([first[0], first[1], second[2]]),
        jnp.stack([second[0], second[1], second[3]]),
        scal,
    ])
    return jnp.stack(rows_out), subspace
```

```python
import functools

import jax
import jax.numpy as jnp
from jax import lax
from jax.experimental import pallas as pl
from jax.experimental.pallas import tpu as pltpu
from jax.sharding import PartitionSpec as P

ITERS = 3
EPS = 1e-06
F32, BF16 = jnp.float32, jnp.bfloat16
ROWS = 128
TAIL_ROWS = 16
SPAN = 8
VMEM_LIMIT = 16 * 1024 * 1024
HB, VM, SM = pltpu.HBM, pltpu.VMEM, pltpu.SMEM


def _specs(*shapes):
    return [pl.BlockSpec(memory_space=s) for s in shapes]


def _hbm(*arrays):
    return [pltpu.with_memory_space_constraint(x, HB) for x in arrays]


def _vmem(*arrays):
    return [pltpu.with_memory_space_constraint(x, VM) for x in arrays]


def _fold(x):
    return jnp.sum(x.reshape(x.shape[0] // 8, 8, x.shape[1]), axis=0)


def _over(n_sec, states, width, n_acc, body):
    blocks = states // ROWS

    def step(i, accs):
        for b in range(blocks):
            accs = tuple(x + y for x, y in zip(accs, body(i, slice(b * ROWS, (b + 1) * ROWS))))
        return accs

    zero = tuple(jnp.zeros((8, width), F32) for _ in range(n_acc))
    return tuple(jnp.sum(a) for a in lax.fori_loop(0, n_sec, step, zero))


def _put_scalars(ref, values):
    shape = ref.shape
    row = lax.broadcasted_iota(jnp.int32, shape, 0)
    out = jnp.zeros(shape, F32)
    for index, value in enumerate(values):
        out = jnp.where(row == index, value, out)
    ref[...] = out


def _first_kernel(cfg, places, meta, psi, psi_o, pre, pre_o, *refs):
    envs, (start, pret, scale_ref, acc, vb, right, left, sem) = refs[: len(places)], refs[len(places) :]
    sec, states, width = psi.shape
    n_sec = sec * cfg["n_blk"]
    base = meta[2] * sec
    moves = _env_moves(cfg, meta, places, envs, right, left, sem)
    for part, (p_ref, c_ref) in enumerate(((psi, pre), (psi_o, pre_o))):
        for k in range(p_ref.shape[0]):
            at = lax.rem(base + part * sec + k, n_sec)
            live = meta[cfg["dims_at"] + at]
            row = lax.broadcasted_iota(jnp.int32, (states, width), 0)
            col = lax.broadcasted_iota(jnp.int32, (states, width), 1)
            value = jnp.where((row < live) & (col < live), p_ref[k].astype(F32).T, 0.0)
            start[at] = value.astype(BF16)
            pret[at] = c_ref[k].T
    def square(s, r):
        value = start[s, r, :].astype(F32)
        return (_fold(value * value),)

    (total,) = _over(n_sec, states, width, 1, square)
    scale = lax.rsqrt(total / (n_sec * states * width) + EPS)
    count = n_sec * states * width

    def cond(s, r):
        value = start[s, r, :].astype(F32)
        return (_fold(value * value * pret[s, r, :]),)

    (damped,) = _over(n_sec, states, width, 1, cond)
    _put_scalars(scale_ref, [scale, damped * scale * scale / count])

    def make(s, r):
        vb[s, r, :] = (start[s, r, :].astype(F32) * scale).astype(BF16)
        return ()

    _over(n_sec, states, width, 0, make)
    for _, c in moves:
        c.wait()
    for k in range(acc.shape[0]):
        total = None
        for t in range(right.shape[0]):
            chosen = vb[meta[cfg["pair_at"] + t * acc.shape[0] + k]]
            inner = jnp.dot(right[t, k], chosen, preferred_element_type=F32).astype(BF16)
            got = jnp.dot(inner, left[t, k], preferred_element_type=F32)
            total = got if total is None else total + got
        acc[k] = total


def _group(cfg, meta, ref):
    return ref.at[:, pl.ds(meta[3] * cfg["held"], cfg["held"])]


def _env_moves(cfg, meta, places, refs, right, left, sem, first=0):
    moves = []
    for ref, (kind, t0, far, own) in zip(refs, places):
        src = _group(cfg, meta, ref) if own else ref
        step = cfg["span"]
        for i in range(0, ref.shape[0], step):
            t = pl.ds(t0 + i, step)
            side = meta[0] ^ far if cfg["direct"] else 0
            rows = pl.ds(pl.multiple_of(side * ref.shape[2], ref.shape[2]), ref.shape[2])
            dst = right.at[t] if kind == "right" else left.at[t, :, rows, :]
            moves.append((t0 + i, src.at[pl.ds(i, step)], dst))
    moves.sort(key=lambda m: m[0])
    moves = [(t, pltpu.make_async_copy(a, b, sem.at[first + i])) for i, (t, a, b) in enumerate(moves)]
    for _, c in moves:
        c.start()
    return moves


def _near_sigma_kernel(cfg, t0, meta, acc, start, scale_ref, right_h, near_h, out, inner_far, vb, right, near, inner, sem):
    moves = [(right_h, right), (near_h, near)]
    moves = [pltpu.make_async_copy(a, b, sem.at[i]) for i, (a, b) in enumerate(moves)]
    for c in moves:
        c.start()
    scale = scale_ref[0, 0]

    def make(s, r):
        vb[s, r, :] = (start[s, r, :].astype(F32) * scale).astype(BF16)
        return ()

    _over(*vb.shape, 0, make)
    moves[0].wait()
    terms, held, half = right.shape[:3]
    for k in range(held):
        for t in range(terms):
            chosen = vb[meta[cfg["pair_at"] + (t0 + t) * held + k]]
            inner[t, k] = jnp.dot(right[t, k], chosen, preferred_element_type=F32).astype(BF16)
    moves[1].wait()
    own, other = (pl.ds(pl.multiple_of(side * half, half), half) for side in (meta[0], 1 - meta[0]))
    for k in range(held):
        total = acc[k]
        for t in range(terms):
            total = total + jnp.dot(inner[t, k, :, own], near[t, k], preferred_element_type=F32)
            inner_far[t, k] = inner[t, k, :, other]
        out[k] = total


def _far_sigma_kernel(acc, inner, far_h, out, far, sem):
    held = far.shape[1]
    moves = [pltpu.make_async_copy(far_h.at[:, k], far.at[:, k], sem.at[k]) for k in range(held)]
    for c in moves:
        c.start()
    for k in range(held):
        moves[k].wait()
        total = acc[k]
        for t in range(far.shape[0]):
            total = total + jnp.dot(inner[t, k], far[t, k], preferred_element_type=F32)
        out[k] = total.astype(out.dtype)


def _step_kernel(cfg, step, places, env_places, last, meta, *refs):
    it = iter(refs)
    take = lambda n: [next(it) for _ in range(n)]
    shards = take(len(places))
    (start, scale_ref), vecs, (pre,) = take(2), take(step - 1), take(1)
    olds_h, envs_h, (sig_h,) = take(step - 1), take(len(env_places)), take(1)
    vnew, dots = (None, None) if last else take(2)
    outs = take(cfg["n_out"])
    if last:
        vnew, turned = take(2)
    olds = take(step - 1)
    right, left, sig, vb, acc, sem = take(6)
    by_rows = take(2) if last and cfg["direct"] else None
    env_pos, z, blk, mine_at = meta[0], meta[1], meta[2], meta[3]
    n_sec, states, width = vnew.shape
    sec, held_sec, half = cfg["sec"], cfg["held"], right.shape[2]
    count = n_sec * states * width
    n_held = sec // held_sec

    def sector(b, h, k):
        if not cfg["direct"]:
            return b * sec + k
        return (blk ^ b) * sec + (mine_at ^ h) * held_sec + k

    order = [(b, h, k) for b in range(cfg["n_blk"]) for h in range(n_held) for k in range(held_sec)]
    old_moves = [pltpu.make_async_copy(a, b, sem.at[i]) for i, (a, b) in enumerate(zip(olds_h, olds))]
    for c in old_moves:
        c.start()
    env_moves = _env_moves(cfg, meta, env_places, envs_h, right, left, sem, step)
    if by_rows:
        save = pltpu.make_async_copy(by_rows[1], sig_h.at[0 : ITERS - 1], sem.at[step - 1])
    else:
        save = pltpu.make_async_copy(sig, sig_h, sem.at[step - 1])
    scales = [scale_ref[0, 0]] + [1.0] * (step - 1)
    basis = [lambda s, r: start[s, r, :].astype(F32)]
    basis += [lambda s, r, v=v: v[s, r, :] for v in vecs]

    pairs = [(j, l) for l in range(1, step) for j in range(l + 1)]
    accs = [jnp.zeros((8, width), F32) for _ in range(2 * step + len(pairs))]
    blocks = {o: [] for o in order}
    for ref, place in zip(shards, places):
        if place is None:
            for b, h, k in order:
                for r in range(0, states, ROWS):
                    at = b * sec + k
                    blocks[b, h, k].append((ref, at, slice(r, r + ROWS), at, slice(r, r + ROWS)))
            continue
        b, e, h = place
        for k in range(held_sec):
            for r in range(0, half, ROWS):
                rows = pl.ds(pl.multiple_of((env_pos ^ e) * half + r, ROWS), ROWS)
                blocks[b, h, k].append((ref, k, slice(r, r + ROWS), sector(b, h, k), rows))
    for o in order:
        for ref, k, r, s, rows in blocks[o]:
            low = ref[k, r, :]
            sig[s, rows, :] = low
            value, cond = low.astype(F32), pre[s, rows, :]
            scaled = value * cond
            held = [b(s, rows) for b in basis]
            found = [_fold(h * value) for h in held] + [_fold(h * scaled) for h in held]
            condh = [h * cond for h in held[1:]]
            found += [_fold(held[j] * condh[l - 1]) for j, l in pairs]
            accs = [a + t for a, t in zip(accs, found)]
    if not by_rows:
        save.start()
    sums = [jnp.sum(a) / count for a in accs]
    proj = [sums[j] * scales[j] for j in range(step)]
    gram = {(0, 0): scale_ref[1, 0]}
    for (j, l), value in zip(pairs, sums[2 * step :]):
        gram[j, l] = gram[l, j] = value * scales[j] * scales[l]
    back = [sums[step + j] * scales[j] - sum(proj[l] * gram[j, l] for l in range(step)) for j in range(step)]
    proj_scaled = [h * x for h, x in zip(proj, scales)]
    back_scaled = [g * x for g, x in zip(back, scales)]

    over = functools.partial(_over, n_sec, states, width)
    for c in old_moves:
        c.wait()

    def trial_pass(s, r):
        value = sig[s, r, :].astype(F32)
        held = [b(s, r) for b in basis]
        trial = value
        for h, b in zip(proj_scaled, held):
            trial = trial - h * b
        trial = trial * pre[s, r, :]
        for g, b in zip(back_scaled, held):
            trial = trial - g * b
        vnew[s, r, :] = trial
        crossed = [o[s, r, :].astype(F32) for o in olds] + [value]
        return (_fold(trial * trial), *[_fold(trial * o) for o in crossed])

    square, *cross = over(1 + step, trial_pass)
    scale = lax.rsqrt(square / count + EPS)
    cross = [x * scale / count for x in cross]

    def final_pass(s, r):
        value = vnew[s, r, :] * scale
        vnew[s, r, :] = value
        vb[s, r, :] = value.astype(BF16)
        return ()

    over(0, final_pass)
    if by_rows:
        turned_sig, sig_rows = by_rows
        chunk, lanes = sig_rows.shape[2], turned_sig.shape[2]
        side = pl.ds(pl.multiple_of(lax.div(z * chunk, lanes) * lanes, lanes), lanes)
        first = pl.ds(pl.multiple_of(lax.rem(z * chunk, lanes), chunk), chunk)
        for i, ref in enumerate([*olds, sig]):
            for k in range(sec):
                turned_sig[i, k] = ref[blk * sec + k, :, side].astype(F32).T
                sig_rows[i, k] = turned_sig[i, k, first, :]
        save.start()
    span = cfg["span"]
    for t0 in range(0, right.shape[0], span):
        for t_move, c in env_moves:
            if t0 <= t_move < t0 + span:
                c.wait()
        for k in range(held_sec):
            total = None if t0 == 0 else acc[k]
            for t in range(t0, t0 + span):
                chosen = vb[meta[cfg["pair_at"] + t * held_sec + k]]
                inner = jnp.dot(right[t, k], chosen, preferred_element_type=F32).astype(BF16)
                got = jnp.dot(inner, left[t, k], preferred_element_type=F32)
                total = got if total is None else total + got
            acc[k] = total
    scalars = proj + cross
    if not last:
        outs[0][...] = acc[...].astype(outs[0].dtype)
        _put_scalars(dots, scalars)
        save.wait()
        return

    rows = pl.ds(pl.multiple_of(env_pos * half, half), half)
    mine = []
    for b, scaled in zip([*basis, lambda s, r: vnew[s, r, :]], [*scales, 1.0]):
        total = jnp.zeros((8, width), F32)
        for k in range(held_sec):
            total = total + _fold(b(sector(0, 0, k) if cfg["direct"] else blk * sec + k, rows) * acc[k])
        mine.append(jnp.sum(total) * scaled / count)
    _put_scalars(outs[0], scalars)
    if cfg["direct"]:
        for k in range(held_sec):
            turned[k] = acc[k].T
        span = states // 2
        side = lax.div(z, 2)
        tail = _addends(mine, half)
        for out, at in ((outs[1], side), (outs[2], 1 - side)):
            for k in range(held_sec):
                rows = pl.ds(pl.multiple_of(at * span, span), span)
                out[k * span : (k + 1) * span, :] = turned[k, rows, :].astype(out.dtype)
            out[held_sec * span :, :] = tail.astype(out.dtype)
    else:
        _put_scalars(outs[1], mine)
        for k in range(held_sec):
            outs[2][k] = acc[k].T
    save.wait()


def _addends(values, width):
    row = lax.broadcasted_iota(jnp.int32, (TAIL_ROWS, width), 0)
    tail = jnp.zeros((TAIL_ROWS, width), F32)
    for j, value in enumerate(values):
        rest = jnp.broadcast_to(value, (TAIL_ROWS, width))
        for p in range(3):
            cut = rest.astype(BF16).astype(F32)
            tail = jnp.where(row == 3 * j + p, cut, tail)
            rest = rest - cut
    return tail


def _added(*tails):
    return [
        sum(tail[3 * j + p : 3 * j + p + 1, 0:1].astype(F32) for tail in tails for p in range(3)) for j in range(ITERS)
    ]


def _merge_kernel(cfg, meta, kept, got, own, keep_out, give_out):
    held, chunk, half = own.shape
    span = 2 * chunk
    z = meta[1]
    at_tail = slice(held * span, held * span + TAIL_ROWS)
    tail = _addends(_added(kept[at_tail, :], got[at_tail, :]), half)
    side = lax.rem(z, 2)
    for which, out in ((side, keep_out), (1 - side, give_out)):
        first = pl.multiple_of(which * chunk, chunk)
        for k in range(held):
            rows = pl.ds(pl.multiple_of(k * span + first, chunk), chunk)
            live = meta[cfg["dims_at"] + meta[2] * cfg["sec"] + meta[3] * held + k]
            at_row = lax.div(z, 2) * span + first + lax.broadcasted_iota(jnp.int32, (chunk, half), 0)
            at_col = meta[0] * half + lax.broadcasted_iota(jnp.int32, (chunk, half), 1)
            value = kept[rows, :] + got[rows, :].astype(F32)
            value = jnp.where((at_row < live) & (at_col < live), value, 0.0)
            out[k * chunk : (k + 1) * chunk, :] = value.astype(BF16)
            if out is keep_out:
                own[k] = value
        out[held * chunk :, :] = tail.astype(BF16)


def _final_kernel(cfg, meta, own, by_env, by_term, by_both, held_h, out_h, rows, sem):
    del held_h
    held, chunk, half = own.shape
    for k in range(held):
        at = slice(k * chunk, (k + 1) * chunk)
        pairs = (own[k], by_env[at, :].astype(F32)), (by_term[at, :].astype(F32), by_both[at, :].astype(F32))
        for h, (mine, other) in enumerate(pairs):
            both = jnp.where(meta[0] == 0, mine, other), jnp.where(meta[0] == 0, other, mine)
            rows[0, (meta[3] ^ h) * held + k] = jnp.concatenate(both, axis=1)
    save = pltpu.make_async_copy(rows, out_h.at[ITERS - 1 : ITERS], sem)
    save.start()
    save.wait()


def _dots_kernel(at, own, by_env, by_term, by_both, out):
    found = _added(*(ref[at : at + TAIL_ROWS, :] for ref in (own, by_env, by_term, by_both)))
    _put_scalars(out, found)


def _subspace_kernel(first, known, dots, other, sub):
    row = lax.broadcasted_iota(jnp.int32, sub.shape, 0)
    col = lax.broadcasted_iota(jnp.int32, sub.shape, 1)
    out = jnp.zeros(sub.shape, F32)
    for i, j, ref, at in ((0, 0, first, 0), (0, 1, first, 1), (0, 2, known, 2),
                          (1, 0, known, 0), (1, 1, known, 1), (1, 2, known, 3)):
        out = jnp.where((row == i) & (col == j), ref[at : at + 1, 0:1], out)
    for j in range(ITERS):
        value = dots[j : j + 1, 0:1] + other[j : j + 1, 0:1]
        out = jnp.where((row == ITERS - 1) & (col == j), value, out)
    sub[...] = out


def solution(mesh):
    n_env, n_term, n_blk = (mesh.shape[a] for a in ("env", "term", "blk"))

    def on_device(psi, left_env, right_env, pairing, sector_dims, precond):
        return _on_device(n_env, n_term, n_blk, psi, left_env, right_env, pairing, sector_dims, precond)

    placed = (
        P(("parts", "blk"), None, None),
        P(("parts", "term"), "blk", "env", None),
        P(("parts", "term"), "blk", "env", None),
        P(("parts", "term"), "blk"),
        P("parts"),
        P(("parts", "blk"), None, None),
    )
    return jax.shard_map(
        on_device,
        mesh=mesh,
        in_specs=placed,
        out_specs=(P(None, ("parts", "blk"), "term", None), P("parts", None)),
        check_vma=False,
    )


def _xor(axis, n, s):
    return functools.partial(lax.ppermute, axis_name=axis, perm=[(i, i ^ s) for i in range(n)])


def _cut_kernel(held, which, env_h, out, sem):
    half = env_h.shape[0] // 2
    moves = []
    for i in range(2):
        t = pl.ds(i * half, half)
        moves.append(pltpu.make_async_copy(env_h.at[t, pl.ds(which[0] * held, held)], out.at[t], sem.at[i]))
        moves[-1].start()
    for c in moves:
        c.wait()


def _cut(env, which, held):
    shape = (env.shape[0], held, *env.shape[2:])
    return pl.pallas_call(
        functools.partial(_cut_kernel, held),
        out_shape=VM(shape, BF16),
        in_specs=_specs(SM, HB),
        out_specs=_specs(VM)[0],
        scratch_shapes=[pltpu.SemaphoreType.DMA((2,))],
        compiler_params=pltpu.CompilerParams(vmem_limit_bytes=VMEM_LIMIT),
        name="sectors_to_send",
    )(which.astype(jnp.int32).reshape(1), *_hbm(env))


def _on_device(n_env, n_term, n_blk, psi, left_env, right_env, pairing, sector_dims, precond):
    sec, states, width = psi.shape
    terms = left_env.shape[0]
    n_sec = sec * n_blk
    half = right_env.shape[2]
    direct = n_env == 2 and n_blk == 2 and n_term == 4 and sec % 2 == 0 and terms % 2 == 0
    chunk = states // n_term
    held = sec // 2 if direct else sec
    span = SPAN if terms % SPAN == 0 else 1
    cfg = dict(direct=direct, n_blk=n_blk, sec=sec, held=held, span=span)
    env_pos, term_pos, blk_pos = (lax.axis_index(a) for a in ("env", "term", "blk"))
    mine = (term_pos ^ (term_pos >> 1)) & 1 if direct else jnp.zeros_like(term_pos)
    next_term, far_term = _xor("term", 4, 1), _xor("term", 4, 3)
    other_env, other_blk = _xor("env", 2, 1), _xor("blk", 2, 1)
    corners = functools.partial(
        lax.ppermute, axis_name=("term", "env"), perm=[(2 * t + e, 2 * (t ^ 1) + (e ^ 1)) for t in range(4) for e in range(2)]
    )
    group = lambda x, which: lax.dynamic_slice_in_dim(x, which * held, held, 1)

    if direct:
        to_next = _cut(left_env, 1 - mine, held)
        to_env = _cut(left_env, lax.optimization_barrier((mine, to_next))[0], held)
        right_to_next = _cut(right_env, lax.optimization_barrier((1 - mine, to_env))[0], held)
        psi_o, pre_o = other_blk(psi), other_blk(precond)
        next_left = next_term(to_next)
        far_left = other_env(to_env)
        next_right = next_term(right_to_next)
        next_far_left = other_env(next_left)
        own_table = group(pairing, mine)
        own_places = [("left", 0, 0, True), ("left", 0, 1, False)]
        next_places = [("right", 0, 0, False), ("left", 0, 0, False), ("left", 0, 1, False)]
        own_envs, next_envs = [left_env, far_left], [next_right, next_left, next_far_left]
        n_terms = 2 * terms
        shift = lambda place: (place[0], place[1] + terms, *place[2:])
        env_places = [("right", 0, 0, True), *own_places, *map(shift, next_places)]
        envs = [right_env, *own_envs, *next_envs]
    else:
        own_envs = [lax.all_gather(left_env, "env", axis=2, tiled=True)]
        own_places = [("left", 0, 0, False)]
        own_table = pairing
        n_terms = terms
        env_places, envs = [("right", 0, 0, True), *own_places], [right_env, *own_envs]
        psi_o, pre_o = (
            lax.dynamic_slice_in_dim(
                jnp.concatenate([lax.all_gather(x, "blk", axis=0, tiled=True)] * 2, axis=0),
                (blk_pos + 1) * sec,
                sec * (n_blk - 1),
                0,
            )
            for x in (psi, precond)
        )
    flat = jnp.stack([x.astype(jnp.int32) for x in (env_pos, term_pos, blk_pos, mine)])
    own_meta = jnp.concatenate([flat, sector_dims.reshape(-1), own_table.reshape(-1)])
    cfg["dims_at"] = 4
    cfg["pair_at"] = 4 + n_sec

    full = (n_sec, states, width)
    params = pltpu.CompilerParams(vmem_limit_bytes=VMEM_LIMIT)
    dma = pltpu.SemaphoreType.DMA
    n_moves = 3 * terms // span
    first_places, first_envs = [("right", 0, 0, True), *own_places], [right_env, *own_envs]
    start, pret, scale0, partial = pl.pallas_call(
        functools.partial(_first_kernel, cfg, first_places),
        out_shape=(VM(full, BF16), VM(full, F32), VM((8, 128), F32), VM((held, half, width), F32)),
        in_specs=_specs(SM, VM, VM, VM, VM, *[HB] * len(first_envs)),
        out_specs=_specs(VM, VM, VM, VM),
        scratch_shapes=[
            pltpu.VMEM(full, BF16),
            pltpu.VMEM((terms, held, half, states), BF16),
            pltpu.VMEM((terms, held, states, width), BF16),
            dma((n_moves,)),
        ],
        compiler_params=params,
        name="start_vector",
    )(own_meta, psi, psi_o, precond, pre_o, *_hbm(*first_envs))

    meta = own_meta
    if direct:
        next_pairing = next_term(lax.optimization_barrier((pairing, partial))[0])
        meta = jnp.concatenate([own_meta, group(next_pairing, mine).reshape(-1)])
        piece = (terms, held, half, states)
        partial, inner_far = pl.pallas_call(
            functools.partial(_near_sigma_kernel, cfg, terms),
            out_shape=(VM((held, half, width), F32), VM((terms, held, half, half), BF16)),
            in_specs=_specs(SM, VM, VM, VM, HB, HB),
            out_specs=tuple(_specs(VM, VM)),
            scratch_shapes=[pltpu.VMEM(full, BF16), *[pltpu.VMEM(piece, BF16)] * 3, dma((2,))],
            compiler_params=params,
            name="first_sigma_next_terms",
        )(meta, *_vmem(partial, start, scale0), *_hbm(next_right, next_left))
        partial = pl.pallas_call(
            _far_sigma_kernel,
            out_shape=VM((held, half, width), BF16),
            in_specs=_specs(VM, VM, HB),
            out_specs=_specs(VM)[0],
            scratch_shapes=[pltpu.VMEM(piece, BF16), dma((held,))],
            compiler_params=params,
            name="first_sigma_far_rows",
        )(*_vmem(partial, inner_far), *_hbm(next_far_left))

    live_own = lax.dynamic_slice_in_dim(sector_dims, blk_pos * sec, sec)

    def masked(value, row0, live):
        row = row0 + lax.broadcasted_iota(jnp.int32, value.shape, 1)
        col = lax.broadcasted_iota(jnp.int32, value.shape, 2)
        live = live[:, None, None]
        return jnp.where((row < live) & (col < live), value, 0.0).astype(BF16)

    def combine(partial):
        if direct:
            total = partial.astype(F32) + far_term(partial).astype(F32)
            shard = masked(total, env_pos * half, lax.dynamic_slice_in_dim(live_own, mine * held, held))
            here = [shard, next_term(shard), other_env(shard), corners(shard)]
            there = [other_blk(x) for x in here]
            return here + there, [(b, e, h) for b in range(2) for e, h in ((0, 0), (0, 1), (1, 0), (1, 1))]
        flat_sum = lax.psum_scatter(partial.reshape(sec * half, width), "term", scatter_dimension=0, tiled=True)
        whole = lax.all_gather(flat_sum, "term", axis=0, tiled=True).reshape(sec, half, width)
        whole = masked(lax.all_gather(whole, "env", axis=1, tiled=True), 0, live_own)
        return [lax.all_gather(whole, "blk", axis=0, tiled=True)], [None]

    out_shape = (ITERS, sec, chunk, states)
    vecs, olds = [], []
    for step in range(1, ITERS):
        last = step + 1 == ITERS
        shards, places = combine(partial)
        if last:
            outs = [VM((8, 128), F32)]
            if direct:
                size = (held * states // 2 + TAIL_ROWS, half)
                outs += [VM(size, F32), VM(size, BF16)]
            else:
                outs += [VM((8, 128), F32), VM((sec, states, half), F32)]
            made = (HB(out_shape, F32) if direct else HB(full, BF16),)
        else:
            outs = [VM((held, half, width), BF16 if direct else F32)]
            made = (HB(full, BF16), VM(full, F32), VM((8, 128), F32))
        n_hbm = (step - 1) + len(envs)
        results = pl.pallas_call(
            functools.partial(_step_kernel, dict(cfg, n_out=len(outs)), step, places, env_places, last),
            out_shape=(*made, *outs),
            in_specs=_specs(SM, *[VM] * (len(shards) + 3 + len(vecs)), *[HB] * n_hbm),
            out_specs=tuple(_specs(HB, *[VM] * (len(made) - 1 + len(outs)))),
            scratch_shapes=[pltpu.VMEM(full, F32), pltpu.VMEM((held, states, half), F32)] * last
            + [pltpu.VMEM(full, BF16)] * (step - 1)
            + [
                pltpu.VMEM((n_terms, held, half, states), BF16),
                pltpu.VMEM((n_terms, held, states, width), BF16),
                pltpu.VMEM(full, BF16),
                pltpu.VMEM(full, BF16),
                pltpu.VMEM((held, half, width), F32),
                dma((step + len(envs) * n_moves,)),
            ]
            + [pltpu.VMEM((step, sec, 2 * chunk, states), F32), pltpu.VMEM((step, sec, chunk, states), F32)] * (last and direct),
            compiler_params=params,
            name=f"vector_and_sigma_{step}",
        )(
            meta,
            *_vmem(*shards, start, scale0, *vecs, pret),
            *_hbm(*olds, *envs),
        )
        olds.append(results[0])
        if last:
            known, *pieces = results[1:]
        else:
            vecs.append(results[1])
            first, partial = results[2:]

    if direct:
        kept, given = pieces
        got = far_term(given)
        size = (held * chunk + TAIL_ROWS, half)
        own, keep, give = pl.pallas_call(
            functools.partial(_merge_kernel, cfg),
            out_shape=(VM((held, chunk, half), F32), VM(size, BF16), VM(size, BF16)),
            in_specs=_specs(SM, VM, VM),
            out_specs=tuple(_specs(VM, VM, VM)),
            compiler_params=params,
            name="last_sums",
        )(meta, *_vmem(kept, got))
        parts = [other_env(keep), next_term(give), corners(give)]
        dots = pl.pallas_call(
            functools.partial(_dots_kernel, held * chunk),
            out_shape=VM((8, 128), F32),
            in_specs=_specs(*[VM] * 4),
            out_specs=_specs(VM)[0],
            compiler_params=params,
            name="last_dots",
        )(*_vmem(keep, *parts))
        other_dots = other_blk(dots)
        sigmas = pl.pallas_call(
            functools.partial(_final_kernel, cfg),
            out_shape=HB(out_shape, F32),
            in_specs=_specs(SM, *[VM] * 4, HB),
            out_specs=_specs(HB)[0],
            scratch_shapes=[pltpu.VMEM((1, sec, chunk, states), F32), dma],
            input_output_aliases={5: 0},
            compiler_params=params,
            name="last_rows",
        )(meta, *_vmem(own, *parts), *_hbm(olds[-1]))
        subspace = pl.pallas_call(
            _subspace_kernel,
            out_shape=jax.ShapeDtypeStruct((ITERS, ITERS), F32),
            in_specs=_specs(*[VM] * 4),
            out_specs=_specs(VM)[0],
            compiler_params=params,
            name="subspace",
        )(*_vmem(first, known, dots, other_dots))
        return sigmas, subspace
    dots = pieces.pop(0)
    own = lax.psum_scatter(pieces[0], "term", scatter_dimension=1, tiled=True)
    both = lax.all_gather(own, "env", axis=2, tiled=True)
    row = term_pos * chunk + lax.broadcasted_iota(jnp.int32, both.shape, 1)
    col = lax.broadcasted_iota(jnp.int32, both.shape, 2)
    live = live_own[:, None, None]
    both = jnp.where((row < live) & (col < live), both, 0.0)
    rows_out = []
    for sig in olds:
        part = lax.dynamic_slice(sig, (blk_pos * sec, 0, term_pos * chunk), (sec, states, chunk))
        rows_out.append(jnp.swapaxes(part, 1, 2).astype(F32))
    rows_out.append(both)
    scal = lax.psum(dots, ("term", "env", "blk"))[:ITERS, 0]
    first, second = first[:, 0], known[:, 0]
    subspace = jnp.stack([
        jnp.stack([first[0], first[1], second[2]]),
        jnp.stack([second[0], second[1], second[3]]),
        scal,
    ])
    return jnp.stack(rows_out), subspace
```

```python
import functools

import jax
import jax.numpy as jnp
from jax import lax
from jax.experimental import pallas as pl
from jax.experimental.pallas import tpu as pltpu
from jax.sharding import PartitionSpec as P

ITERS = 3
EPS = 1e-06
F32, BF16 = jnp.float32, jnp.bfloat16
ROWS = 128
TAIL_ROWS = 16
SPAN = 8
VMEM_LIMIT = 16 * 1024 * 1024
HB, VM, SM = pltpu.HBM, pltpu.VMEM, pltpu.SMEM


def _specs(*shapes):
    return [pl.BlockSpec(memory_space=s) for s in shapes]


def _hbm(*arrays):
    return [pltpu.with_memory_space_constraint(x, HB) for x in arrays]


def _vmem(*arrays):
    return [pltpu.with_memory_space_constraint(x, VM) for x in arrays]


def _fold(x):
    return jnp.sum(x.reshape(x.shape[0] // 8, 8, x.shape[1]), axis=0)


def _over(n_sec, states, width, n_acc, body):
    blocks = states // ROWS

    def step(i, accs):
        for b in range(blocks):
            accs = tuple(x + y for x, y in zip(accs, body(i, slice(b * ROWS, (b + 1) * ROWS))))
        return accs

    zero = tuple(jnp.zeros((8, width), F32) for _ in range(n_acc))
    return tuple(jnp.sum(a) for a in lax.fori_loop(0, n_sec, step, zero))


def _put_scalars(ref, values):
    shape = ref.shape
    row = lax.broadcasted_iota(jnp.int32, shape, 0)
    out = jnp.zeros(shape, F32)
    for index, value in enumerate(values):
        out = jnp.where(row == index, value, out)
    ref[...] = out


def _first_kernel(cfg, places, meta, psi, psi_o, pre, pre_o, *refs):
    envs, (start, pret, scale_ref, acc, vb, right, left, sem) = refs[: len(places)], refs[len(places) :]
    sec, states, width = psi.shape
    n_sec = sec * cfg["n_blk"]
    base = meta[2] * sec
    moves = _env_moves(cfg, meta, places, envs, right, left, sem)
    for part, (p_ref, c_ref) in enumerate(((psi, pre), (psi_o, pre_o))):
        for k in range(p_ref.shape[0]):
            at = lax.rem(base + part * sec + k, n_sec)
            live = meta[cfg["dims_at"] + at]
            row = lax.broadcasted_iota(jnp.int32, (states, width), 0)
            col = lax.broadcasted_iota(jnp.int32, (states, width), 1)
            value = jnp.where((row < live) & (col < live), p_ref[k].astype(F32).T, 0.0)
            start[at] = value.astype(BF16)
            pret[at] = c_ref[k].T
    def square(s, r):
        value = start[s, r, :].astype(F32)
        return (_fold(value * value),)

    (total,) = _over(n_sec, states, width, 1, square)
    scale = lax.rsqrt(total / (n_sec * states * width) + EPS)
    count = n_sec * states * width

    def cond(s, r):
        value = start[s, r, :].astype(F32)
        return (_fold(value * value * pret[s, r, :]),)

    (damped,) = _over(n_sec, states, width, 1, cond)
    _put_scalars(scale_ref, [scale, damped * scale * scale / count])

    def make(s, r):
        vb[s, r, :] = (start[s, r, :].astype(F32) * scale).astype(BF16)
        return ()

    _over(n_sec, states, width, 0, make)
    for _, c in moves:
        c.wait()
    for k in range(acc.shape[0]):
        total = None
        for t in range(right.shape[0]):
            chosen = vb[meta[cfg["pair_at"] + t * acc.shape[0] + k]]
            inner = jnp.dot(right[t, k], chosen, preferred_element_type=F32).astype(BF16)
            got = jnp.dot(inner, left[t, k], preferred_element_type=F32)
            total = got if total is None else total + got
        acc[k] = total


def _group(cfg, meta, ref):
    return ref.at[:, pl.ds(meta[3] * cfg["held"], cfg["held"])]


def _env_moves(cfg, meta, places, refs, right, left, sem, first=0):
    moves = []
    for ref, (kind, t0, far, own) in zip(refs, places):
        src = _group(cfg, meta, ref) if own else ref
        step = cfg["span"]
        for i in range(0, ref.shape[0], step):
            t = pl.ds(t0 + i, step)
            side = meta[0] ^ far if cfg["direct"] else 0
            rows = pl.ds(pl.multiple_of(side * ref.shape[2], ref.shape[2]), ref.shape[2])
            dst = right.at[t] if kind == "right" else left.at[t, :, rows, :]
            moves.append((t0 + i, src.at[pl.ds(i, step)], dst))
    moves.sort(key=lambda m: m[0])
    moves = [(t, pltpu.make_async_copy(a, b, sem.at[first + i])) for i, (t, a, b) in enumerate(moves)]
    for _, c in moves:
        c.start()
    return moves


def _next_inner_kernel(cfg, t0, meta, start, scale_ref, right_h, near_h, inner, near, vb, right, sem):
    cut = right.shape[0] // 2
    parts = [(a.at[t], b.at[t]) for a, b in ((right_h, right), (near_h, near)) for t in (pl.ds(0, cut), pl.ds(cut, cut))]
    moves = [pltpu.make_async_copy(a, b, sem.at[i]) for i, (a, b) in enumerate(parts)]
    for c in moves:
        c.start()
    scale = scale_ref[0, 0]

    def make(s, r):
        vb[s, r, :] = (start[s, r, :].astype(F32) * scale).astype(BF16)
        return ()

    _over(*vb.shape, 0, make)
    moves[0].wait()
    moves[1].wait()
    terms, held = right.shape[:2]
    for k in range(held):
        for t in range(terms):
            chosen = vb[meta[cfg["pair_at"] + (t0 + t) * held + k]]
            inner[t, k] = jnp.dot(right[t, k], chosen, preferred_element_type=F32).astype(BF16)
    moves[2].wait()
    moves[3].wait()


def _next_sigma_kernel(cfg, meta, acc, inner, near, far_h, out, far, sem):
    terms, held, half = far.shape[:3]
    cut = terms // 2
    parts = [pl.ds(0, cut), pl.ds(cut, cut)]
    moves = [pltpu.make_async_copy(far_h.at[t], far.at[t], sem.at[i]) for i, t in enumerate(parts)]
    for c in moves:
        c.start()
    own, other = (pl.ds(pl.multiple_of(side * half, half), half) for side in (meta[0], 1 - meta[0]))
    totals = []
    for k in range(held):
        total = acc[k]
        for t in range(terms):
            total = total + jnp.dot(inner[t, k, :, own], near[t, k], preferred_element_type=F32)
        totals.append(total)
    for c in moves:
        c.wait()
    for k, total in enumerate(totals):
        for t in range(terms):
            total = total + jnp.dot(inner[t, k, :, other], far[t, k], preferred_element_type=F32)
        out[k] = total.astype(out.dtype)


def _step_kernel(cfg, step, places, env_places, last, meta, *refs):
    it = iter(refs)
    take = lambda n: [next(it) for _ in range(n)]
    shards = take(len(places))
    (start, scale_ref), vecs, (pre,) = take(2), take(step - 1), take(1)
    olds_h, envs_h, (sig_h,) = take(step - 1), take(len(env_places)), take(1)
    vnew, dots = (None, None) if last else take(2)
    outs = take(cfg["n_out"])
    if last:
        vnew, turned = take(2)
    olds = take(step - 1)
    right, left, sig, vb, acc, sem = take(6)
    by_rows = take(2) if last and cfg["direct"] else None
    env_pos, z, blk, mine_at = meta[0], meta[1], meta[2], meta[3]
    n_sec, states, width = vnew.shape
    sec, held_sec, half = cfg["sec"], cfg["held"], right.shape[2]
    count = n_sec * states * width
    n_held = sec // held_sec

    def sector(b, h, k):
        if not cfg["direct"]:
            return b * sec + k
        return (blk ^ b) * sec + (mine_at ^ h) * held_sec + k

    order = [(b, h, k) for b in range(cfg["n_blk"]) for h in range(n_held) for k in range(held_sec)]
    old_moves = [pltpu.make_async_copy(a, b, sem.at[i]) for i, (a, b) in enumerate(zip(olds_h, olds))]
    for c in old_moves:
        c.start()
    env_moves = _env_moves(cfg, meta, env_places, envs_h, right, left, sem, step)
    if by_rows:
        save = pltpu.make_async_copy(by_rows[1], sig_h.at[0 : ITERS - 1], sem.at[step - 1])
    else:
        save = pltpu.make_async_copy(sig, sig_h, sem.at[step - 1])
    scales = [scale_ref[0, 0]] + [1.0] * (step - 1)
    basis = [lambda s, r: start[s, r, :].astype(F32)]
    basis += [lambda s, r, v=v: v[s, r, :] for v in vecs]

    pairs = [(j, l) for l in range(1, step) for j in range(l + 1)]
    accs = [jnp.zeros((8, width), F32) for _ in range(2 * step + len(pairs))]
    blocks = {o: [] for o in order}
    for ref, place in zip(shards, places):
        if place is None:
            for b, h, k in order:
                for r in range(0, states, ROWS):
                    at = b * sec + k
                    blocks[b, h, k].append((ref, at, slice(r, r + ROWS), at, slice(r, r + ROWS)))
            continue
        b, e, h = place
        for k in range(held_sec):
            for r in range(0, half, ROWS):
                rows = pl.ds(pl.multiple_of((env_pos ^ e) * half + r, ROWS), ROWS)
                blocks[b, h, k].append((ref, k, slice(r, r + ROWS), sector(b, h, k), rows))
    for o in order:
        for ref, k, r, s, rows in blocks[o]:
            low = ref[k, r, :]
            sig[s, rows, :] = low
            value, cond = low.astype(F32), pre[s, rows, :]
            scaled = value * cond
            held = [b(s, rows) for b in basis]
            found = [_fold(h * value) for h in held] + [_fold(h * scaled) for h in held]
            condh = [h * cond for h in held[1:]]
            found += [_fold(held[j] * condh[l - 1]) for j, l in pairs]
            accs = [a + t for a, t in zip(accs, found)]
    if not by_rows:
        save.start()
    sums = [jnp.sum(a) / count for a in accs]
    proj = [sums[j] * scales[j] for j in range(step)]
    gram = {(0, 0): scale_ref[1, 0]}
    for (j, l), value in zip(pairs, sums[2 * step :]):
        gram[j, l] = gram[l, j] = value * scales[j] * scales[l]
    back = [sums[step + j] * scales[j] - sum(proj[l] * gram[j, l] for l in range(step)) for j in range(step)]
    proj_scaled = [h * x for h, x in zip(proj, scales)]
    back_scaled = [g * x for g, x in zip(back, scales)]

    over = functools.partial(_over, n_sec, states, width)
    for c in old_moves:
        c.wait()

    def trial_pass(s, r):
        value = sig[s, r, :].astype(F32)
        held = [b(s, r) for b in basis]
        trial = value
        for h, b in zip(proj_scaled, held):
            trial = trial - h * b
        trial = trial * pre[s, r, :]
        for g, b in zip(back_scaled, held):
            trial = trial - g * b
        vnew[s, r, :] = trial
        crossed = [o[s, r, :].astype(F32) for o in olds] + [value]
        return (_fold(trial * trial), *[_fold(trial * o) for o in crossed])

    square, *cross = over(1 + step, trial_pass)
    scale = lax.rsqrt(square / count + EPS)
    cross = [x * scale / count for x in cross]

    def final_pass(s, r):
        value = vnew[s, r, :] * scale
        vnew[s, r, :] = value
        vb[s, r, :] = value.astype(BF16)
        return ()

    over(0, final_pass)
    if by_rows:
        turned_sig, sig_rows = by_rows
        chunk, lanes = sig_rows.shape[2], turned_sig.shape[2]
        side = pl.ds(pl.multiple_of(lax.div(z * chunk, lanes) * lanes, lanes), lanes)
        first = pl.ds(pl.multiple_of(lax.rem(z * chunk, lanes), chunk), chunk)
        for i, ref in enumerate([*olds, sig]):
            for k in range(sec):
                turned_sig[i, k] = ref[blk * sec + k, :, side].astype(F32).T
                sig_rows[i, k] = turned_sig[i, k, first, :]
        save.start()
    span = cfg["span"]
    for t0 in range(0, right.shape[0], span):
        for t_move, c in env_moves:
            if t0 <= t_move < t0 + span:
                c.wait()
        for k in range(held_sec):
            total = None if t0 == 0 else acc[k]
            for t in range(t0, t0 + span):
                chosen = vb[meta[cfg["pair_at"] + t * held_sec + k]]
                inner = jnp.dot(right[t, k], chosen, preferred_element_type=F32).astype(BF16)
                got = jnp.dot(inner, left[t, k], preferred_element_type=F32)
                total = got if total is None else total + got
            acc[k] = total
    scalars = proj + cross
    if not last:
        outs[0][...] = acc[...].astype(outs[0].dtype)
        _put_scalars(dots, scalars)
        save.wait()
        return

    rows = pl.ds(pl.multiple_of(env_pos * half, half), half)
    mine = []
    for b, scaled in zip([*basis, lambda s, r: vnew[s, r, :]], [*scales, 1.0]):
        total = jnp.zeros((8, width), F32)
        for k in range(held_sec):
            total = total + _fold(b(sector(0, 0, k) if cfg["direct"] else blk * sec + k, rows) * acc[k])
        mine.append(jnp.sum(total) * scaled / count)
    _put_scalars(outs[0], scalars)
    if cfg["direct"]:
        for k in range(held_sec):
            turned[k] = acc[k].T
        span = states // 2
        side = lax.div(z, 2)
        tail = _addends(mine, half)
        for out, at in ((outs[1], side), (outs[2], 1 - side)):
            for k in range(held_sec):
                rows = pl.ds(pl.multiple_of(at * span, span), span)
                out[k * span : (k + 1) * span, :] = turned[k, rows, :].astype(out.dtype)
            out[held_sec * span :, :] = tail.astype(out.dtype)
    else:
        _put_scalars(outs[1], mine)
        for k in range(held_sec):
            outs[2][k] = acc[k].T
    save.wait()


def _addends(values, width):
    row = lax.broadcasted_iota(jnp.int32, (TAIL_ROWS, width), 0)
    tail = jnp.zeros((TAIL_ROWS, width), F32)
    for j, value in enumerate(values):
        rest = jnp.broadcast_to(value, (TAIL_ROWS, width))
        for p in range(3):
            cut = rest.astype(BF16).astype(F32)
            tail = jnp.where(row == 3 * j + p, cut, tail)
            rest = rest - cut
    return tail


def _added(*tails):
    return [
        sum(tail[3 * j + p : 3 * j + p + 1, 0:1].astype(F32) for tail in tails for p in range(3)) for j in range(ITERS)
    ]


def _merge_kernel(cfg, meta, kept, got, own, keep_out, give_out):
    held, chunk, half = own.shape
    span = 2 * chunk
    z = meta[1]
    at_tail = slice(held * span, held * span + TAIL_ROWS)
    tail = _addends(_added(kept[at_tail, :], got[at_tail, :]), half)
    side = lax.rem(z, 2)
    for which, out in ((side, keep_out), (1 - side, give_out)):
        first = pl.multiple_of(which * chunk, chunk)
        for k in range(held):
            rows = pl.ds(pl.multiple_of(k * span + first, chunk), chunk)
            live = meta[cfg["dims_at"] + meta[2] * cfg["sec"] + meta[3] * held + k]
            at_row = lax.div(z, 2) * span + first + lax.broadcasted_iota(jnp.int32, (chunk, half), 0)
            at_col = meta[0] * half + lax.broadcasted_iota(jnp.int32, (chunk, half), 1)
            value = kept[rows, :] + got[rows, :].astype(F32)
            value = jnp.where((at_row < live) & (at_col < live), value, 0.0)
            out[k * chunk : (k + 1) * chunk, :] = value.astype(BF16)
            if out is keep_out:
                own[k] = value
        out[held * chunk :, :] = tail.astype(BF16)


def _final_kernel(cfg, meta, own, by_env, by_term, by_both, held_h, out_h, rows, sem):
    del held_h
    held, chunk, half = own.shape
    for k in range(held):
        at = slice(k * chunk, (k + 1) * chunk)
        pairs = (own[k], by_env[at, :].astype(F32)), (by_term[at, :].astype(F32), by_both[at, :].astype(F32))
        for h, (mine, other) in enumerate(pairs):
            both = jnp.where(meta[0] == 0, mine, other), jnp.where(meta[0] == 0, other, mine)
            rows[0, (meta[3] ^ h) * held + k] = jnp.concatenate(both, axis=1)
    save = pltpu.make_async_copy(rows, out_h.at[ITERS - 1 : ITERS], sem)
    save.start()
    save.wait()


def _dots_kernel(at, own, by_env, by_term, by_both, out):
    found = _added(*(ref[at : at + TAIL_ROWS, :] for ref in (own, by_env, by_term, by_both)))
    _put_scalars(out, found)


def _subspace_kernel(first, known, dots, other, sub):
    row = lax.broadcasted_iota(jnp.int32, sub.shape, 0)
    col = lax.broadcasted_iota(jnp.int32, sub.shape, 1)
    out = jnp.zeros(sub.shape, F32)
    for i, j, ref, at in ((0, 0, first, 0), (0, 1, first, 1), (0, 2, known, 2),
                          (1, 0, known, 0), (1, 1, known, 1), (1, 2, known, 3)):
        out = jnp.where((row == i) & (col == j), ref[at : at + 1, 0:1], out)
    for j in range(ITERS):
        value = dots[j : j + 1, 0:1] + other[j : j + 1, 0:1]
        out = jnp.where((row == ITERS - 1) & (col == j), value, out)
    sub[...] = out


def solution(mesh):
    n_env, n_term, n_blk = (mesh.shape[a] for a in ("env", "term", "blk"))

    def on_device(psi, left_env, right_env, pairing, sector_dims, precond):
        return _on_device(n_env, n_term, n_blk, psi, left_env, right_env, pairing, sector_dims, precond)

    placed = (
        P(("parts", "blk"), None, None),
        P(("parts", "term"), "blk", "env", None),
        P(("parts", "term"), "blk", "env", None),
        P(("parts", "term"), "blk"),
        P("parts"),
        P(("parts", "blk"), None, None),
    )
    return jax.shard_map(
        on_device,
        mesh=mesh,
        in_specs=placed,
        out_specs=(P(None, ("parts", "blk"), "term", None), P("parts", None)),
        check_vma=False,
    )


def _xor(axis, n, s):
    return functools.partial(lax.ppermute, axis_name=axis, perm=[(i, i ^ s) for i in range(n)])


def _cut_kernel(held, which, env_h, out, sem):
    half = env_h.shape[0] // 2
    moves = []
    for i in range(2):
        t = pl.ds(i * half, half)
        moves.append(pltpu.make_async_copy(env_h.at[t, pl.ds(which[0] * held, held)], out.at[t], sem.at[i]))
        moves[-1].start()
    for c in moves:
        c.wait()


def _cut(env, which, held):
    shape = (env.shape[0], held, *env.shape[2:])
    return pl.pallas_call(
        functools.partial(_cut_kernel, held),
        out_shape=VM(shape, BF16),
        in_specs=_specs(SM, HB),
        out_specs=_specs(VM)[0],
        scratch_shapes=[pltpu.SemaphoreType.DMA((2,))],
        compiler_params=pltpu.CompilerParams(vmem_limit_bytes=VMEM_LIMIT),
        name="sectors_to_send",
    )(which.astype(jnp.int32).reshape(1), *_hbm(env))


def _on_device(n_env, n_term, n_blk, psi, left_env, right_env, pairing, sector_dims, precond):
    sec, states, width = psi.shape
    terms = left_env.shape[0]
    n_sec = sec * n_blk
    half = right_env.shape[2]
    direct = n_env == 2 and n_blk == 2 and n_term == 4 and sec % 2 == 0 and terms % 2 == 0
    chunk = states // n_term
    held = sec // 2 if direct else sec
    span = SPAN if terms % SPAN == 0 else 1
    cfg = dict(direct=direct, n_blk=n_blk, sec=sec, held=held, span=span)
    env_pos, term_pos, blk_pos = (lax.axis_index(a) for a in ("env", "term", "blk"))
    mine = (term_pos ^ (term_pos >> 1)) & 1 if direct else jnp.zeros_like(term_pos)
    next_term, far_term = _xor("term", 4, 1), _xor("term", 4, 3)
    other_env, other_blk = _xor("env", 2, 1), _xor("blk", 2, 1)
    corners = functools.partial(
        lax.ppermute, axis_name=("term", "env"), perm=[(2 * t + e, 2 * (t ^ 1) + (e ^ 1)) for t in range(4) for e in range(2)]
    )
    group = lambda x, which: lax.dynamic_slice_in_dim(x, which * held, held, 1)

    if direct:
        to_next = _cut(left_env, 1 - mine, held)
        to_env = _cut(left_env, lax.optimization_barrier((mine, to_next))[0], held)
        right_to_next = _cut(right_env, lax.optimization_barrier((1 - mine, to_env))[0], held)
        psi_o, pre_o = other_blk(psi), other_blk(precond)
        next_left = next_term(to_next)
        far_left = other_env(to_env)
        next_right = next_term(right_to_next)
        next_far_left = other_env(next_left)
        own_table = group(pairing, mine)
        own_places = [("left", 0, 0, True), ("left", 0, 1, False)]
        next_places = [("right", 0, 0, False), ("left", 0, 0, False), ("left", 0, 1, False)]
        own_envs, next_envs = [left_env, far_left], [next_right, next_left, next_far_left]
        n_terms = 2 * terms
        shift = lambda place: (place[0], place[1] + terms, *place[2:])
        env_places = [("right", 0, 0, True), *own_places, *map(shift, next_places)]
        envs = [right_env, *own_envs, *next_envs]
    else:
        own_envs = [lax.all_gather(left_env, "env", axis=2, tiled=True)]
        own_places = [("left", 0, 0, False)]
        own_table = pairing
        n_terms = terms
        env_places, envs = [("right", 0, 0, True), *own_places], [right_env, *own_envs]
        psi_o, pre_o = (
            lax.dynamic_slice_in_dim(
                jnp.concatenate([lax.all_gather(x, "blk", axis=0, tiled=True)] * 2, axis=0),
                (blk_pos + 1) * sec,
                sec * (n_blk - 1),
                0,
            )
            for x in (psi, precond)
        )
    flat = jnp.stack([x.astype(jnp.int32) for x in (env_pos, term_pos, blk_pos, mine)])
    own_meta = jnp.concatenate([flat, sector_dims.reshape(-1), own_table.reshape(-1)])
    cfg["dims_at"] = 4
    cfg["pair_at"] = 4 + n_sec

    full = (n_sec, states, width)
    params = pltpu.CompilerParams(vmem_limit_bytes=VMEM_LIMIT)
    dma = pltpu.SemaphoreType.DMA
    n_moves = 3 * terms // span
    first_places, first_envs = [("right", 0, 0, True), *own_places], [right_env, *own_envs]
    start, pret, scale0, partial = pl.pallas_call(
        functools.partial(_first_kernel, cfg, first_places),
        out_shape=(VM(full, BF16), VM(full, F32), VM((8, 128), F32), VM((held, half, width), F32)),
        in_specs=_specs(SM, VM, VM, VM, VM, *[HB] * len(first_envs)),
        out_specs=_specs(VM, VM, VM, VM),
        scratch_shapes=[
            pltpu.VMEM(full, BF16),
            pltpu.VMEM((terms, held, half, states), BF16),
            pltpu.VMEM((terms, held, states, width), BF16),
            dma((n_moves,)),
        ],
        compiler_params=params,
        name="start_vector",
    )(own_meta, psi, psi_o, precond, pre_o, *_hbm(*first_envs))

    meta = own_meta
    if direct:
        next_pairing = next_term(lax.optimization_barrier((pairing, partial))[0])
        meta = jnp.concatenate([own_meta, group(next_pairing, mine).reshape(-1)])
        piece = (terms, held, half, states)
        inner, near = pl.pallas_call(
            functools.partial(_next_inner_kernel, cfg, terms),
            out_shape=(VM((terms, held, half, states), BF16), VM(piece, BF16)),
            in_specs=_specs(SM, VM, VM, HB, HB),
            out_specs=tuple(_specs(VM, VM)),
            scratch_shapes=[pltpu.VMEM(full, BF16), pltpu.VMEM(piece, BF16), dma((4,))],
            compiler_params=params,
            name="next_terms_inner",
        )(meta, *_vmem(start, scale0), *_hbm(next_right, next_left))
        partial = pl.pallas_call(
            functools.partial(_next_sigma_kernel, cfg),
            out_shape=VM((held, half, width), BF16),
            in_specs=_specs(SM, VM, VM, VM, HB),
            out_specs=_specs(VM)[0],
            scratch_shapes=[pltpu.VMEM(piece, BF16), dma((2,))],
            compiler_params=params,
            name="next_terms_sigma",
        )(meta, *_vmem(partial, inner, near), *_hbm(next_far_left))

    live_own = lax.dynamic_slice_in_dim(sector_dims, blk_pos * sec, sec)

    def masked(value, row0, live):
        row = row0 + lax.broadcasted_iota(jnp.int32, value.shape, 1)
        col = lax.broadcasted_iota(jnp.int32, value.shape, 2)
        live = live[:, None, None]
        return jnp.where((row < live) & (col < live), value, 0.0).astype(BF16)

    def combine(partial):
        if direct:
            total = partial.astype(F32) + far_term(partial).astype(F32)
            shard = masked(total, env_pos * half, lax.dynamic_slice_in_dim(live_own, mine * held, held))
            here = [shard, next_term(shard), other_env(shard), corners(shard)]
            there = [other_blk(x) for x in here]
            return here + there, [(b, e, h) for b in range(2) for e, h in ((0, 0), (0, 1), (1, 0), (1, 1))]
        flat_sum = lax.psum_scatter(partial.reshape(sec * half, width), "term", scatter_dimension=0, tiled=True)
        whole = lax.all_gather(flat_sum, "term", axis=0, tiled=True).reshape(sec, half, width)
        whole = masked(lax.all_gather(whole, "env", axis=1, tiled=True), 0, live_own)
        return [lax.all_gather(whole, "blk", axis=0, tiled=True)], [None]

    out_shape = (ITERS, sec, chunk, states)
    vecs, olds = [], []
    for step in range(1, ITERS):
        last = step + 1 == ITERS
        shards, places = combine(partial)
        if last:
            outs = [VM((8, 128), F32)]
            if direct:
                size = (held * states // 2 + TAIL_ROWS, half)
                outs += [VM(size, F32), VM(size, BF16)]
            else:
                outs += [VM((8, 128), F32), VM((sec, states, half), F32)]
            made = (HB(out_shape, F32) if direct else HB(full, BF16),)
        else:
            outs = [VM((held, half, width), BF16 if direct else F32)]
            made = (HB(full, BF16), VM(full, F32), VM((8, 128), F32))
        n_hbm = (step - 1) + len(envs)
        results = pl.pallas_call(
            functools.partial(_step_kernel, dict(cfg, n_out=len(outs)), step, places, env_places, last),
            out_shape=(*made, *outs),
            in_specs=_specs(SM, *[VM] * (len(shards) + 3 + len(vecs)), *[HB] * n_hbm),
            out_specs=tuple(_specs(HB, *[VM] * (len(made) - 1 + len(outs)))),
            scratch_shapes=[pltpu.VMEM(full, F32), pltpu.VMEM((held, states, half), F32)] * last
            + [pltpu.VMEM(full, BF16)] * (step - 1)
            + [
                pltpu.VMEM((n_terms, held, half, states), BF16),
                pltpu.VMEM((n_terms, held, states, width), BF16),
                pltpu.VMEM(full, BF16),
                pltpu.VMEM(full, BF16),
                pltpu.VMEM((held, half, width), F32),
                dma((step + len(envs) * n_moves,)),
            ]
            + [pltpu.VMEM((step, sec, 2 * chunk, states), F32), pltpu.VMEM((step, sec, chunk, states), F32)] * (last and direct),
            compiler_params=params,
            name=f"vector_and_sigma_{step}",
        )(
            meta,
            *_vmem(*shards, start, scale0, *vecs, pret),
            *_hbm(*olds, *envs),
        )
        olds.append(results[0])
        if last:
            known, *pieces = results[1:]
        else:
            vecs.append(results[1])
            first, partial = results[2:]

    if direct:
        kept, given = pieces
        got = far_term(given)
        size = (held * chunk + TAIL_ROWS, half)
        own, keep, give = pl.pallas_call(
            functools.partial(_merge_kernel, cfg),
            out_shape=(VM((held, chunk, half), F32), VM(size, BF16), VM(size, BF16)),
            in_specs=_specs(SM, VM, VM),
            out_specs=tuple(_specs(VM, VM, VM)),
            compiler_params=params,
            name="last_sums",
        )(meta, *_vmem(kept, got))
        parts = [other_env(keep), next_term(give), corners(give)]
        dots = pl.pallas_call(
            functools.partial(_dots_kernel, held * chunk),
            out_shape=VM((8, 128), F32),
            in_specs=_specs(*[VM] * 4),
            out_specs=_specs(VM)[0],
            compiler_params=params,
            name="last_dots",
        )(*_vmem(keep, *parts))
        other_dots = other_blk(dots)
        sigmas = pl.pallas_call(
            functools.partial(_final_kernel, cfg),
            out_shape=HB(out_shape, F32),
            in_specs=_specs(SM, *[VM] * 4, HB),
            out_specs=_specs(HB)[0],
            scratch_shapes=[pltpu.VMEM((1, sec, chunk, states), F32), dma],
            input_output_aliases={5: 0},
            compiler_params=params,
            name="last_rows",
        )(meta, *_vmem(own, *parts), *_hbm(olds[-1]))
        subspace = pl.pallas_call(
            _subspace_kernel,
            out_shape=jax.ShapeDtypeStruct((ITERS, ITERS), F32),
            in_specs=_specs(*[VM] * 4),
            out_specs=_specs(VM)[0],
            compiler_params=params,
            name="subspace",
        )(*_vmem(first, known, dots, other_dots))
        return sigmas, subspace
    dots = pieces.pop(0)
    own = lax.psum_scatter(pieces[0], "term", scatter_dimension=1, tiled=True)
    both = lax.all_gather(own, "env", axis=2, tiled=True)
    row = term_pos * chunk + lax.broadcasted_iota(jnp.int32, both.shape, 1)
    col = lax.broadcasted_iota(jnp.int32, both.shape, 2)
    live = live_own[:, None, None]
    both = jnp.where((row < live) & (col < live), both, 0.0)
    rows_out = []
    for sig in olds:
        part = lax.dynamic_slice(sig, (blk_pos * sec, 0, term_pos * chunk), (sec, states, chunk))
        rows_out.append(jnp.swapaxes(part, 1, 2).astype(F32))
    rows_out.append(both)
    scal = lax.psum(dots, ("term", "env", "blk"))[:ITERS, 0]
    first, second = first[:, 0], known[:, 0]
    subspace = jnp.stack([
        jnp.stack([first[0], first[1], second[2]]),
        jnp.stack([second[0], second[1], second[3]]),
        scal,
    ])
    return jnp.stack(rows_out), subspace
```
